512 devices in a mesh: gx: 16 (over y, core), gy: 4 (over x), gz: 8 (over z).
Axes of the slice: x: 4, y: 8, z: 8, core: 2. Of those that a mesh axis runs over, the one named last changes fastest.
Arguments:
- start_block: float32 [3, 32, 32, 32, 256], P(None, 'gx', 'gy', 'gz'), may hold values from -6 to 6
- node_mass: float32 [3, 32, 32, 32], P(None, 'gx', 'gy', 'gz'), may hold values from 0.5 to 2
- ground_spring: float32 [3, 32, 32, 32], P(None, 'gx', 'gy', 'gz'), may hold values from 0.05 to 0.5
- stiffness: float32 [3, 3, 32, 32, 32], P(None, None, 'gx', 'gy', 'gz'), may hold values from 0.5 to 2
- yield_flags: int32 [3, 16, 32, 32, 32], P(None, None, 'gx', 'gy', 'gz'), may hold values 0 or 1
- stress_old: float32 [3, 16, 32, 32, 32], P(None, None, 'gx', 'gy', 'gz'), may hold values from -6 to 6
Outputs:
- subspace: float32 [3, 32, 32, 32, 256], P(None, 'gx', 'gy', 'gz')
- projected: float32 [256, 256], replicated
- force: float32 [3, 32, 32, 32], P(None, 'gx', 'gy', 'gz')
- stress_new: float32 [3, 16, 32, 32, 32], P(None, None, 'gx', 'gy', 'gz')
The draws below stay inside these ranges and needn't reach their ends.
All inputs are finite; a program needn't handle non-finite values. No bound on the sum of `yield_flags` on one device may be relied on, other than what follows from the above.
Results may differ from the reference program's by a relative error of at most 0.00015.
Values sent between devices are 32-bit elements; how exact they have to be, the bound alone decides.
No kernel may reach another device: no remote copies, remote signals or barrier semaphores. Data moves between devices by JAX's collectives and lax.ppermute only.
A program may use at most 64 MiB of HBM per device.

```python
import math
import jax
import jax.numpy as jnp
from jax import lax

V = 256
FIB = 16
DEGREE = 4
ITERS = 2
NX = 32
NY = 32
NZ = 32
DOFS = 98304


def place_ends(values, stream_key, least, high):
    longest = values.shape.index(max(values.shape))
    spots = []
    for shift in (0, 1):
        where = [jax.random.randint(jax.random.fold_in(stream_key, axis), (), 0, length) for axis, length in enumerate(values.shape)]
        where[longest] = (where[longest] + shift) % values.shape[longest]
        spots.append(tuple(where))
    return values.at[spots[0]].set(least).at[spots[1]].set(high)


def block_levels(own_key, dims, split, least, high):
    level = 1.0
    for dim, shards_of in split:
        draws = jax.random.uniform(jax.random.fold_in(jax.random.fold_in(own_key, 6), dim), (shards_of,), jnp.float32, least / len(split), high / len(split))
        level = level * jnp.repeat(jnp.exp(draws), dims[dim] // shards_of).reshape((-1,) + (1,) * (len(dims) - 1 - dim))
    return level


def scatter_about(key, shape, scale, bound, shards=(), kind=jnp.bfloat16):
    values = jax.random.normal(key, shape, jnp.float32) * scale
    if len(shards) > 0:
        values = block_levels(key, shape, shards, -0.22, 0.18) * values
    return jnp.clip(values, min=-bound, max=bound).astype(kind)


def setup_inputs(seed: int = 0) -> dict:
    keys = jax.random.split(jax.random.key(seed), 7)
    return {
        "start_block": scatter_about(keys[0], (3, NX, NY, NZ, V), 1.0, 6.0, ((1, 16), (2, 4), (3, 8)), jnp.float32),
        "node_mass": jnp.clip(jnp.exp(math.log(2.0) - 1.3862944 * jax.random.uniform(keys[1], (3, NX, NY, NZ), jnp.float32) ** block_levels(keys[1], (3, NX, NY, NZ), ((1, 16), (2, 4), (3, 8)), -0.2, 0.2)), 0.5, 2.0),
        "ground_spring": jnp.clip(jnp.exp(math.log(0.5) - 2.3025851 * jax.random.uniform(keys[2], (3, NX, NY, NZ), jnp.float32) ** block_levels(keys[2], (3, NX, NY, NZ), ((1, 16), (2, 4), (3, 8)), -0.2, 0.2)), 0.05, 0.5),
        "stiffness": jnp.clip(jnp.exp(math.log(2.0) - 1.3862944 * jax.random.uniform(keys[3], (3, 3, NX, NY, NZ), jnp.float32) ** block_levels(keys[3], (3, 3, NX, NY, NZ), ((2, 16), (3, 4), (4, 8)), -0.2, 0.2)), 0.5, 2.0),
        "yield_flags": place_ends((jax.random.randint(keys[4], (3, FIB, NX, NY, NZ), 0, 3) < 1).astype(jnp.int32), jax.random.fold_in(keys[4], 1), 0, 1),
        "stress_old": scatter_about(keys[5], (3, FIB, NX, NY, NZ), 1.0, 6.0, ((2, 16), (3, 4), (4, 8)), jnp.float32),
    }


PRECISE = lax.Precision.HIGHEST

def neighbour(padded, leading, direction, sense):
    slicer = [slice(None)] * padded.ndim
    for position in range(3):
        slicer[leading + position] = slice(1, -1)
    if sense > 0:
        slicer[leading + direction] = slice(2, None)
    else:
        slicer[leading + direction] = slice(0, -2)
    return padded[tuple(slicer)]

def tangent_of(stiffness, yield_flags):
    share = lax.optimization_barrier(jnp.mean(yield_flags.astype(jnp.float32), axis=1))
    return stiffness * (1.0 - 0.9 * share)[:, None]

def edge_weights(tangent, padded_t):
    upward = []
    downward = []
    for direction in range(3):
        upward.append(0.5 * (tangent[direction] + neighbour(padded_t, 2, direction, 1)[direction]))
        downward.append(0.5 * (tangent[direction] + neighbour(padded_t, 2, direction, -1)[direction]))
    return (upward, downward)

def stiffness_times(vectors, padded_v, diagonal_sum, upward, downward):
    result = diagonal_sum[..., None] * vectors
    for direction in range(3):
        result = result - upward[direction][..., None] * neighbour(padded_v, 1, direction, 1)
        result = result - downward[direction][..., None] * neighbour(padded_v, 1, direction, -1)
    return result

def filtered(vectors, apply_k, node_mass, middle, spread):

    def operator_a(field):
        return apply_k(field) / node_mass[..., None]
    earlier = vectors
    current = (operator_a(vectors) - middle * vectors) / spread
    for repeat in range(DEGREE - 1):
        following = 2.0 * (operator_a(current) - middle * current) / spread - earlier
        earlier, current = (current, following)
    return current

def stress_update(displace, padded_u, stiffness, yield_flags, stress_old):
    fibers = stress_old.shape[1]
    heights = (jnp.arange(fibers).astype(jnp.float32) + 0.5) / fibers - 0.5
    results = []
    for direction in range(3):
        above = neighbour(padded_u, 1, direction, 1)
        below = neighbour(padded_u, 1, direction, -1)
        other = (direction + 1) % 3
        axial = 0.5 * (above[direction] - below[direction])
        bending = above[other] - 2.0 * displace[other] + below[other]
        strain = axial[None] + heights[:, None, None, None] * bending[None]
        modulus = stiffness[direction, direction][None] * jnp.where(yield_flags[direction] == 1, 0.05, 1.0)
        results.append(stress_old[direction] + modulus * strain)
    return jnp.stack(results)

def reference(start_block, node_mass, ground_spring, stiffness, yield_flags, stress_old):
    tangent = tangent_of(stiffness, yield_flags)
    padded_t = jnp.pad(tangent, ((0, 0), (0, 0), (1, 1), (1, 1), (1, 1)))
    upward, downward = edge_weights(tangent, padded_t)
    edge_total = sum(upward) + sum(downward)
    diagonal_sum = ground_spring + edge_total
    spectral_top = jnp.max((diagonal_sum + edge_total) / node_mass)
    middle = spectral_top * 9.0 / 16.0
    spread = spectral_top * 7.0 / 16.0

    def apply_k(field):
        padded_v = jnp.pad(field, ((0, 0), (1, 1), (1, 1), (1, 1), (0, 0)))
        return stiffness_times(field, padded_v, diagonal_sum, upward, downward)
    width = start_block.shape[-1]
    mass_rows = node_mass.reshape(-1)
    vectors = start_block
    for turn in range(ITERS):
        current = filtered(vectors, apply_k, node_mass, middle, spread)
        flat_rows = current.reshape(-1, width)
        gram = jnp.dot(flat_rows.T, mass_rows[:, None] * flat_rows, precision=PRECISE)
        factor = jnp.linalg.cholesky(gram)
        basis_t = lax.linalg.triangular_solve(factor, flat_rows.T, left_side=True, lower=True)
        vectors = basis_t.T.reshape(current.shape)
        image = apply_k(vectors).reshape(-1, width)
        projected = jnp.dot(basis_t, image, precision=PRECISE)
    count = mass_rows.shape[0] // 3
    lateral = jnp.dot(basis_t[:, :count], mass_rows[:count], precision=PRECISE)
    hfactor = jnp.linalg.cholesky(projected)
    halfway = lax.linalg.triangular_solve(hfactor, lateral[:, None], left_side=True, lower=True)
    weights = lax.linalg.triangular_solve(hfactor, halfway, left_side=True, lower=True, transpose_a=True)[:, 0]
    displace = jnp.dot(weights, basis_t, precision=PRECISE).reshape(node_mass.shape)
    force = node_mass * displace
    padded_u = jnp.pad(displace, ((0, 0), (1, 1), (1, 1), (1, 1)))
    stress_new = stress_update(displace, padded_u, stiffness, yield_flags, stress_old)
    subspace = vectors * jnp.sqrt(jnp.float32(DOFS))
    return (subspace, projected, force, stress_new)
```

```python
import functools

import jax
import jax.numpy as jnp
from jax import lax
from jax.experimental import pallas as pl
from jax.experimental.pallas import tpu as pltpu
from jax.sharding import PartitionSpec as P

DEGREE = 4
ITERS = 2
PRECISE = lax.Precision.HIGHEST
AXES = ("gx", "gy", "gz")

NODES = 64
DEVICES = 512
BLOCK = 32


def dot(a, b, contract=((1,), (0,))):
    return lax.dot_general(
        a, b, (contract, ((), ())), precision=PRECISE, preferred_element_type=jnp.float32
    )


def pack_kernel(start_ref, coef_ref, out_ref):
    for comp in range(4):
        if comp < 3:
            block = start_ref[comp * NODES : (comp + 1) * NODES, :]
            pairs = jnp.concatenate([block[:, :128], block[:, 128:]], axis=0).T
        else:
            pairs = jnp.zeros((128, 128), jnp.float32)
        source = comp % 3
        rows = [
            jnp.broadcast_to(coef_ref[source * 3 + r : source * 3 + r + 1, :], (8, 128))
            for r in range(3)
        ]
        for gx in range(16):
            first = (gx * 4 + comp) * 32
            out_ref[pl.ds(first, 8, stride=4), :] = pairs[gx * 8 : gx * 8 + 8]
            for r in range(3):
                out_ref[pl.ds(first + r + 1, 8, stride=4), :] = rows[r]


def iota(axis):
    return lax.broadcasted_iota(jnp.int32, (4, 8, 128), axis)


def grid_row(ref, kind, gx):
    return ref[pl.ds(gx * 128 + kind, 32, stride=4), :].reshape(4, 8, 128)


def roll(value, shift, axis=2):
    return pltpu.roll(value, shift, axis)


def both_halves(value):
    lane = iota(2)
    turned = roll(value, 64)
    return jnp.where(lane < 64, value, turned), jnp.where(lane < 64, turned, value)


def x_up(here, above):
    return jnp.where((iota(2) & 32) == 0, roll(here, 96), roll(above, 32))


def x_down(here, below):
    return jnp.where((iota(2) & 32) != 0, roll(here, 32), roll(below, 96))


def y_up(here):
    moved = jnp.concatenate([here[1:], jnp.zeros((1, 8, 128), jnp.float32)], axis=0)
    return jnp.where((iota(2) & 28) != 28, roll(here, 124), roll(moved, 28))


def y_down(here):
    moved = jnp.concatenate([jnp.zeros((1, 8, 128), jnp.float32), here[:-1]], axis=0)
    return jnp.where((iota(2) & 28) != 0, roll(here, 4), roll(moved, 100))


def z_up(here):
    other = jnp.where(iota(1) < 7, roll(roll(here, 3), 7, 1), 0.0)
    return jnp.where((iota(2) & 3) != 3, roll(here, 127), other)


def z_down(here):
    other = jnp.where(iota(1) > 0, roll(roll(here, 125), 1, 1), 0.0)
    return jnp.where((iota(2) & 3) != 0, roll(here, 1), other)


def around(ref, gx):
    here = ref[gx + 1]
    return here, (
        (x_up(here, ref[gx + 2]), x_down(here, ref[gx])),
        (y_up(here), y_down(here)),
        (z_up(here), z_down(here)),
    )


def load_tangents(rows_ref, tangent_ref):
    tangent_ref[0] = jnp.zeros((4, 8, 128), jnp.float32)
    tangent_ref[17] = jnp.zeros((4, 8, 128), jnp.float32)

    def step(gx, carry):
        tangent_ref[gx + 1] = both_halves(grid_row(rows_ref, 1, gx))[0]
        return carry

    lax.fori_loop(0, 16, step, 0, unroll=4)


def edges_at(rows_ref, tangent_ref, gx):
    first = tangent_ref[gx + 1]
    second = both_halves(grid_row(rows_ref, 1, gx))[1]
    third, mass = both_halves(grid_row(rows_ref, 2, gx))
    spring = grid_row(rows_ref, 3, gx)
    ups = [
        0.5 * (first + x_up(first, tangent_ref[gx + 2])),
        0.5 * (second + y_up(second)),
        0.5 * (third + z_up(third)),
    ]
    downs = [
        0.5 * (first + x_down(first, tangent_ref[gx])),
        0.5 * (second + y_down(second)),
        0.5 * (third + z_down(third)),
    ]
    total = (ups[0] + ups[1] + ups[2]) + (downs[0] + downs[1] + downs[2])
    return ups, downs, total, spring + total, mass


def spectrum_kernel(rows_ref, out_ref, tangent_ref):
    load_tangents(rows_ref, tangent_ref)

    def step(gx, best):
        _, _, total, diagonal, mass = edges_at(rows_ref, tangent_ref, gx)
        return jnp.maximum(best, (diagonal + total) / mass)

    best = lax.fori_loop(0, 16, step, jnp.zeros((4, 8, 128), jnp.float32), unroll=4)
    best = jnp.max(jnp.max(best, axis=0), axis=(0, 1), keepdims=True)
    out_ref[...] = jnp.broadcast_to(best, (8, 128))


def filter_kernel(
    comp_ref, rows_ref, top_ref, out_ref, tangent_ref, even_ref, odd_ref, up_ref, down_ref,
    diagonal_ref, inverse_ref
):
    load_tangents(rows_ref, tangent_ref)
    top = jnp.max(jnp.max(top_ref[...], axis=0, keepdims=True), axis=1, keepdims=True)
    middle = top * 9.0 / 16.0
    spread = top * 7.0 / 16.0
    inverse_spread = 1.0 / spread
    ratio = middle * inverse_spread
    for ref in (even_ref, odd_ref):
        ref[0] = jnp.zeros((4, 8, 128), jnp.float32)
        ref[17] = jnp.zeros((4, 8, 128), jnp.float32)

    def prepare(gx, carry):
        ups, downs, _, diagonal, mass = edges_at(rows_ref, tangent_ref, gx)
        for direction in range(3):
            up_ref[direction, gx] = ups[direction]
            down_ref[direction, gx] = downs[direction]
        diagonal_ref[gx] = diagonal
        inverse_ref[gx] = inverse_spread / mass
        even_ref[gx + 1] = grid_row(rows_ref, 0, gx)
        return carry

    lax.fori_loop(0, 16, prepare, 0, unroll=4)

    def stiffness_times(here, sides, gx):
        result = diagonal_ref[gx] * here
        for direction in range(3):
            result = result - up_ref[direction, gx] * sides[direction][0]
            result = result - down_ref[direction, gx] * sides[direction][1]
        return result

    def advance(current_ref, other_ref, first):
        def step(gx, carry):
            here, sides = around(current_ref, gx)
            image = stiffness_times(here, sides, gx) * inverse_ref[gx] - ratio * here
            if first:
                other_ref[gx + 1] = image
            else:
                other_ref[gx + 1] = 2.0 * image - other_ref[gx + 1]
            return carry

        lax.fori_loop(0, 16, step, 0, unroll=4)

    for turn in range(ITERS):
        for repeat in range(DEGREE):
            if repeat % 2 == 0:
                advance(even_ref, odd_ref, repeat == 0)
            else:
                advance(odd_ref, even_ref, False)

    comp = comp_ref[0]

    def finish(gx, carry):
        here, sides = around(even_ref, gx)
        axial = [0.5 * (up - down) for up, down in sides]
        bending = [(up - 2.0 * here) + down for up, down in sides]
        values = [
            here,
            stiffness_times(here, sides, gx),
            jnp.where(comp == 0, axial[0], jnp.where(comp == 1, axial[1], axial[2])),
            jnp.where(comp == 0, bending[2], jnp.where(comp == 1, bending[0], bending[1])),
        ]
        for kind in range(4):
            out_ref[pl.ds(gx * 128 + kind, 32, stride=4), :] = values[kind].reshape(32, 128)
        return carry

    lax.fori_loop(0, 16, finish, 0, unroll=4)


def local_rows(rows_ref, kind):
    lane = lax.broadcasted_iota(jnp.int32, (128, 128), 1)
    parts = []
    for comp in range(3):
        parts.append(
            jnp.concatenate(
                [rows_ref[pl.ds((gx * 4 + comp) * 32 + kind, 8, stride=4), :] for gx in range(16)],
                axis=0,
            )
        )
    turned = [pltpu.roll(part, 64, 1) for part in parts]
    low = lane < 64
    upper = [jnp.where(low, parts[0], turned[1]), jnp.where(low, parts[2], 0.0)]
    lower = [jnp.where(low, turned[0], parts[1]), jnp.where(low, turned[2], 0.0)]
    return jnp.concatenate(
        [jnp.concatenate(upper, axis=1), jnp.concatenate(lower, axis=1)], axis=0
    )


def product_kernel(rows_ref, mass_ref, out_ref):
    vectors = local_rows(rows_ref, 0)
    image = local_rows(rows_ref, 1)
    weighted = vectors * mass_ref[...]
    gram = dot(weighted, vectors, ((1,), (1,)))
    stiff = dot(vectors, image, ((1,), (1,)))
    row = lax.broadcasted_iota(jnp.int32, (256, 256), 0)
    column = lax.broadcasted_iota(jnp.int32, (256, 256), 1)
    both = jnp.where(row >= column, gram, stiff)
    diagonal = jnp.sum(vectors * image, axis=1, keepdims=True)
    lane = lax.broadcasted_iota(jnp.int32, (256, 256), 1)
    lateral = jnp.sum(jnp.where(lane < NODES, weighted, 0.0), axis=1, keepdims=True)
    out_ref[pl.ds(0, 256, stride=2), :] = both[:, :128]
    out_ref[pl.ds(512, 256, stride=2), :] = both[:, 128:]
    out_ref[pl.ds(1, 256, stride=2), :] = jnp.broadcast_to(diagonal, (256, 128))
    out_ref[pl.ds(513, 256, stride=2), :] = jnp.broadcast_to(lateral, (256, 128))


def total_kernel(rows_ref, out_ref):
    total = jnp.sum(rows_ref[...].reshape(128, 8, 128), axis=0)
    total = total + pltpu.roll(total, 2, 0)
    total = total + pltpu.roll(total, 4, 0)
    out_ref[...] = jnp.broadcast_to(total[None], (128, 8, 128)).reshape(1024, 128)


def factor_block(gram, stiff):
    lane = lax.broadcasted_iota(jnp.int32, (BLOCK, 128), 1)
    row = lax.broadcasted_iota(jnp.int32, (BLOCK, 128), 0)
    low = lane < 64
    columns = [
        jnp.where(
            low,
            jnp.broadcast_to(gram[:, j : j + 1], (BLOCK, 128)),
            jnp.broadcast_to(stiff[:, j : j + 1], (BLOCK, 128)),
        )
        for j in range(BLOCK)
    ]
    inverse = jnp.where((lane & 63) == row, 1.0, 0.0)
    pivots = jnp.ones((BLOCK, 128), jnp.float32)
    for k in range(BLOCK):
        column = columns[k]
        pivot = column[k : k + 1, :]
        pivots = jnp.where(row == k, pivot, pivots)
        if k + 1 == BLOCK:
            break
        part = (k + 1) // 8 * 8
        multiple = jnp.where(row[part:] > k, column[part:] * (1.0 / pivot), 0.0)

        def reduced(value):
            tail = value[part:] - multiple * value[k : k + 1, :]
            return tail if part == 0 else jnp.concatenate([value[:part], tail], axis=0)

        for j in range(k + 1, BLOCK):
            columns[j] = reduced(columns[j])
        inverse = reduced(inverse)
    return inverse * lax.rsqrt(pivots)


def final_kernel(sums_ref, rows_ref, subspace_ref, projected_ref, fields_ref, a_ref, e_ref):
    both = jnp.concatenate(
        [sums_ref[pl.ds(0, 256, stride=2), :], sums_ref[pl.ds(512, 256, stride=2), :]], axis=1
    )
    diagonal = sums_ref[pl.ds(1, 256, stride=2), :]
    diagonal = jnp.concatenate([diagonal, diagonal], axis=1)
    lateral = sums_ref[pl.ds(513, 256, stride=2), :]
    turned = both.T
    row = lax.broadcasted_iota(jnp.int32, (256, 256), 0)
    column = lax.broadcasted_iota(jnp.int32, (256, 256), 1)
    gram = jnp.where(row >= column, both, turned)
    stiff = jnp.where(row < column, both, jnp.where(row == column, diagonal, turned))
    a_ref[0] = gram
    a_ref[1] = stiff
    unit = jnp.where(row == column, 1.0, 0.0)
    e_ref[0] = unit
    e_ref[1] = unit
    lane = lax.broadcasted_iota(jnp.int32, (BLOCK, 128), 1)
    for first in range(0, 256, BLOCK):
        tile = first // 128 * 128
        inside = first - tile
        after = first + BLOCK
        small = [a_ref[m, first:after, tile : tile + 128][:, inside : inside + BLOCK] for m in (0, 1)]
        inverse = factor_block(small[0], small[1])
        for m in (0, 1):
            kept = jnp.where((lane >= 64 * m) & (lane < 64 * m + BLOCK), inverse, 0.0)
            shift = (inside - 64 * m) % 128
            spread = pltpu.roll(kept, shift, 1) if shift else kept
            own = kept[:, 64 * m : 64 * m + BLOCK]
            known = slice(0, 128) if after <= 128 else slice(0, 256)
            e_rows = dot(own, e_ref[m, first:after, known])
            e_ref[m, first:after, known] = e_rows
            if after < 256:
                open_ = slice(0, 256) if after < 128 else slice(128, 256)
                a_rows = dot(own, a_ref[m, first:after, open_])
                factor = dot(a_ref[m, after:, tile : tile + 128], spread, ((1,), (1,)))
                a_ref[m, after:, open_] = a_ref[m, after:, open_] - dot(factor, a_rows)
                e_ref[m, after:, known] = e_ref[m, after:, known] - dot(factor, e_rows)
    lower = e_ref[0]
    stiff_lower = e_ref[1]
    vectors = local_rows(rows_ref, 0)
    subspace = dot(vectors.T, lower, ((1,), (1,)))
    subspace_ref[...] = subspace[: 3 * NODES] * jnp.sqrt(jnp.float32(DEVICES * 3 * NODES))
    projected_ref[...] = dot(lower, dot(stiff, lower, ((1,), (1,))))
    weights = dot(stiff_lower.T, dot(stiff_lower, lateral))
    weights = jnp.concatenate([weights, weights], axis=1)
    for place, kind in enumerate((0, 2, 3)):
        value = vectors if kind == 0 else local_rows(rows_ref, kind)
        fields_ref[place : place + 1, :] = jnp.sum(value * weights, axis=0, keepdims=True)
    fields_ref[3:, :] = jnp.zeros((5, 256), jnp.float32)


def call(kernel, shape, scratch=(), smem=(), operands=()):
    return pl.pallas_call(
        kernel,
        out_shape=shape,
        in_specs=[
            pl.BlockSpec(memory_space=pltpu.SMEM if place in smem else pltpu.VMEM)
            for place in range(len(operands))
        ],
        out_specs=jax.tree.map(lambda _: pl.BlockSpec(memory_space=pltpu.VMEM), shape),
        scratch_shapes=list(scratch),
        compiler_params=pltpu.CompilerParams(vmem_limit_bytes=40 * 1024 * 1024),
    )(*operands)


def rows_of(count):
    return jax.ShapeDtypeStruct((count, 128), jnp.float32)


def exchange(rows, per_device):
    blocks = rows.reshape(DEVICES, per_device, 128)
    return lax.all_to_all(blocks, AXES, 0, 0, tiled=True).reshape(rows.shape)


def on_device(start_block, node_mass, ground_spring, stiffness, yield_flags, stress_old):
    width = start_block.shape[-1]
    share = jnp.mean(yield_flags.astype(jnp.float32), axis=1)
    tangent = (stiffness * (1.0 - 0.9 * share)[:, None]).reshape(3, 3, NODES)
    mass = node_mass.reshape(3, NODES)
    spring = ground_spring.reshape(3, NODES)
    coefficients = jnp.stack(
        [
            jnp.concatenate([tangent[0], tangent[1]], axis=1),
            jnp.concatenate([tangent[2], mass], axis=1),
            jnp.concatenate([spring, spring], axis=1),
        ],
        axis=1,
    ).reshape(9, 128)
    padded = pltpu.VMEM((18, 4, 8, 128), jnp.float32)
    plain = pltpu.VMEM((16, 4, 8, 128), jnp.float32)
    sent = call(
        pack_kernel, rows_of(2048), operands=(start_block.reshape(3 * NODES, width), coefficients)
    )
    gathered = exchange(sent, 4)
    own_top = call(spectrum_kernel, rows_of(8), (padded,), operands=(gathered,))
    tops = lax.all_to_all(
        jnp.broadcast_to(own_top[None], (4, 8, 128)), "gy", 0, 0, tiled=True
    ).reshape(32, 128)
    component = lax.axis_index("gy").astype(jnp.int32).reshape(1)
    filtered = call(
        filter_kernel,
        rows_of(2048),
        (
            padded,
            padded,
            padded,
            pltpu.VMEM((3, 16, 4, 8, 128), jnp.float32),
            pltpu.VMEM((3, 16, 4, 8, 128), jnp.float32),
            plain,
            plain,
        ),
        smem=(0,),
        operands=(component, gathered, tops),
    )
    returned = exchange(filtered, 4)
    mass_row = jnp.pad(mass.reshape(1, 3 * NODES), ((0, 0), (0, NODES)))
    products = call(product_kernel, rows_of(1024), operands=(returned, mass_row))
    totals = call(total_kernel, rows_of(1024), operands=(exchange(products, 2),))
    subspace, projected, fields = call(
        final_kernel,
        (
            jax.ShapeDtypeStruct((3 * NODES, width), jnp.float32),
            jax.ShapeDtypeStruct((width, width), jnp.float32),
            jax.ShapeDtypeStruct((8, 256), jnp.float32),
        ),
        (
            pltpu.VMEM((2, 256, 256), jnp.float32),
            pltpu.VMEM((2, 256, 256), jnp.float32),
        ),
        operands=(exchange(totals, 2), returned),
    )
    place = node_mass.shape[1:]
    fields = fields[:3, : 3 * NODES].reshape((3, 3) + place)
    force = node_mass * fields[0]
    axial = fields[1]
    bending = jnp.roll(fields[2], -1, axis=0)
    fibers = stress_old.shape[1]
    heights = ((jnp.arange(fibers).astype(jnp.float32) + 0.5) / fibers - 0.5)[:, None, None, None]
    strain = axial[:, None] + heights * bending[:, None]
    own = jnp.stack([stiffness[d, d] for d in range(3)])[:, None]
    stress_new = stress_old + own * jnp.where(yield_flags == 1, 0.05, 1.0) * strain
    return (subspace.reshape(start_block.shape), projected, force, stress_new)


def solution(mesh):
    return jax.shard_map(
        on_device,
        mesh=mesh,
        in_specs=(
            P(None, "gx", "gy", "gz", None),
            P(None, "gx", "gy", "gz"),
            P(None, "gx", "gy", "gz"),
            P(None, None, "gx", "gy", "gz"),
            P(None, None, "gx", "gy", "gz"),
            P(None, None, "gx", "gy", "gz"),
        ),
        out_specs=(
            P(None, "gx", "gy", "gz", None),
            P(),
            P(None, "gx", "gy", "gz"),
            P(None, None, "gx", "gy", "gz"),
        ),
        check_vma=False,
    )
```

```python
import functools

import jax
import jax.numpy as jnp
from jax import lax
from jax.experimental import pallas as pl
from jax.experimental.pallas import tpu as pltpu
from jax.sharding import PartitionSpec as P

DEGREE = 4
ITERS = 2
PRECISE = lax.Precision.HIGHEST
AXES = ("gx", "gy", "gz")

NODES = 64
DEVICES = 512
BLOCK = 32
STIFF_LANE = 5
MASS_LANE = 6


def dot(a, b, contract=((1,), (0,))):
    return lax.dot_general(
        a, b, (contract, ((), ())), precision=PRECISE, preferred_element_type=jnp.float32
    )


def pack_kernel(start_ref, coef_ref, out_ref):
    for comp in range(4):
        if comp < 3:
            block = start_ref[comp * NODES : (comp + 1) * NODES, :]
            pairs = jnp.concatenate([block[:, :128], block[:, 128:]], axis=0).T
        else:
            pairs = jnp.zeros((128, 128), jnp.float32)
        source = comp % 3
        rows = [
            jnp.broadcast_to(coef_ref[source * 3 + r : source * 3 + r + 1, :], (8, 128))
            for r in range(3)
        ]
        for gx in range(16):
            first = (gx * 4 + comp) * 32
            out_ref[pl.ds(first, 8, stride=4), :] = pairs[gx * 8 : gx * 8 + 8]
            for r in range(3):
                out_ref[pl.ds(first + r + 1, 8, stride=4), :] = rows[r]


def iota(axis):
    return lax.broadcasted_iota(jnp.int32, (4, 8, 128), axis)


def grid_row(ref, kind, gx):
    return ref[pl.ds(gx * 128 + kind, 32, stride=4), :].reshape(4, 8, 128)


def roll(value, shift, axis=2):
    return pltpu.roll(value, shift, axis)


def both_halves(value):
    lane = iota(2)
    turned = roll(value, 64)
    return jnp.where(lane < 64, value, turned), jnp.where(lane < 64, turned, value)


class Turned:
    def __init__(self, ref):
        self.ref = ref
        self.planes = {}

    def at(self, place):
        if place not in self.planes:
            if place in (0, 17):
                zero = jnp.zeros((4, 8, 128), jnp.float32)
                self.planes[place] = (zero, zero)
            else:
                here = self.ref[place]
                self.planes[place] = (roll(here, 96), roll(here, 32))
        return self.planes[place]

    def sides(self, gx):
        first = (iota(2) & 32) == 0
        up = jnp.where(first, self.at(gx + 1)[0], self.at(gx + 2)[1])
        down = jnp.where(first, self.at(gx)[0], self.at(gx + 1)[1])
        return up, down


def y_up(here):
    moved = jnp.concatenate([here[1:], jnp.zeros((1, 8, 128), jnp.float32)], axis=0)
    return jnp.where((iota(2) & 28) != 28, roll(here, 124), roll(moved, 28))


def y_down(here):
    moved = jnp.concatenate([jnp.zeros((1, 8, 128), jnp.float32), here[:-1]], axis=0)
    return jnp.where((iota(2) & 28) != 0, roll(here, 4), roll(moved, 100))


def z_up(here):
    other = jnp.where(iota(1) < 7, roll(roll(here, 3), 7, 1), 0.0)
    return jnp.where((iota(2) & 3) != 3, roll(here, 127), other)


def z_down(here):
    other = jnp.where(iota(1) > 0, roll(roll(here, 125), 1, 1), 0.0)
    return jnp.where((iota(2) & 3) != 0, roll(here, 1), other)


def around(ref, turned, gx):
    here = ref[gx + 1]
    return here, (turned.sides(gx), (y_up(here), y_down(here)), (z_up(here), z_down(here)))


def load_tangents(rows_ref, tangent_ref):
    for gx in range(16):
        tangent_ref[gx + 1] = both_halves(grid_row(rows_ref, 1, gx))[0]
    return Turned(tangent_ref)


def edges_at(rows_ref, turned, gx):
    first = turned.ref[gx + 1]
    above, below = turned.sides(gx)
    second = both_halves(grid_row(rows_ref, 1, gx))[1]
    third, mass = both_halves(grid_row(rows_ref, 2, gx))
    spring = grid_row(rows_ref, 3, gx)
    ups = [0.5 * (first + above), 0.5 * (second + y_up(second)), 0.5 * (third + z_up(third))]
    downs = [0.5 * (first + below), 0.5 * (second + y_down(second)), 0.5 * (third + z_down(third))]
    total = (ups[0] + ups[1] + ups[2]) + (downs[0] + downs[1] + downs[2])
    return ups, downs, total, spring + total, mass


def spectrum_kernel(rows_ref, out_ref, tangent_ref):
    turned = load_tangents(rows_ref, tangent_ref)
    best = jnp.zeros((4, 8, 128), jnp.float32)
    for gx in range(16):
        _, _, total, diagonal, mass = edges_at(rows_ref, turned, gx)
        best = jnp.maximum(best, (diagonal + total) / mass)
    best = jnp.max(jnp.max(best, axis=0), axis=(0, 1), keepdims=True)
    out_ref[...] = jnp.broadcast_to(best, (32, 128))


def filter_kernel(
    comp_ref, rows_ref, top_ref, out_ref, tangent_ref, even_ref, odd_ref, up_ref, down_ref,
    diagonal_ref, inverse_ref
):
    turned = load_tangents(rows_ref, tangent_ref)
    top = jnp.max(jnp.max(top_ref[...], axis=0, keepdims=True), axis=1, keepdims=True)
    middle = top * 9.0 / 16.0
    spread = top * 7.0 / 16.0
    inverse_spread = 1.0 / spread
    ratio = middle * inverse_spread

    for gx in range(16):
        ups, downs, _, diagonal, mass = edges_at(rows_ref, turned, gx)
        for direction in range(3):
            up_ref[direction, gx] = ups[direction]
            down_ref[direction, gx] = downs[direction]
        diagonal_ref[gx] = diagonal
        inverse_ref[gx] = inverse_spread / mass
        even_ref[gx + 1] = grid_row(rows_ref, 0, gx)

    def stiffness_times(here, sides, gx):
        result = diagonal_ref[gx] * here
        for direction in range(3):
            result = result - up_ref[direction, gx] * sides[direction][0]
            result = result - down_ref[direction, gx] * sides[direction][1]
        return result

    for turn in range(ITERS):
        for repeat in range(DEGREE):
            current_ref, other_ref = (even_ref, odd_ref) if repeat % 2 == 0 else (odd_ref, even_ref)
            turned = Turned(current_ref)
            for gx in range(16):
                here, sides = around(current_ref, turned, gx)
                image = stiffness_times(here, sides, gx) * inverse_ref[gx] - ratio * here
                if repeat > 0:
                    image = 2.0 * image - other_ref[gx + 1]
                other_ref[gx + 1] = image

    comp = comp_ref[0]
    turned = Turned(even_ref)
    stiff_sum = jnp.zeros((4, 8, 128), jnp.float32)
    mass_sum = jnp.zeros((4, 8, 128), jnp.float32)
    for gx in range(16):
        here, sides = around(even_ref, turned, gx)
        axial = [0.5 * (up - down) for up, down in sides]
        bending = [(up - 2.0 * here) + down for up, down in sides]
        image = stiffness_times(here, sides, gx)
        values = [
            here,
            image,
            jnp.where(comp == 0, bending[2], jnp.where(comp == 1, axial[1], axial[2])),
            jnp.where(comp == 0, axial[0], jnp.where(comp == 1, bending[0], bending[1])),
        ]
        for kind in range(4):
            out_ref[pl.ds(gx * 128 + kind, 32, stride=4), :] = values[kind].reshape(32, 128)
        stiff_sum = stiff_sum + here * image
        mass_sum = mass_sum + here * both_halves(grid_row(rows_ref, 2, gx))[1]
    lane = lax.broadcasted_iota(jnp.int32, (1, 128), 1)
    sums = []
    for value in (stiff_sum, mass_sum):
        value = jnp.sum(jnp.sum(value, axis=0), axis=0, keepdims=True)
        low = jnp.sum(jnp.where(lane < 64, value, 0.0), axis=1, keepdims=True)
        high = jnp.sum(jnp.where(lane < 64, 0.0, value), axis=1, keepdims=True)
        sums.append(jnp.where(lane < 64, low, high))
    for gx in range(16):
        rows = pl.ds(gx * 128 + 2, 32, stride=4)
        value = jnp.where((lane & 63) == STIFF_LANE, sums[0], out_ref[rows, :])
        out_ref[rows, :] = jnp.where((lane & 63) == MASS_LANE, sums[1], value)


def parts_of(rows_ref, kind):
    return [
        jnp.concatenate(
            [rows_ref[pl.ds((gx * 4 + comp) * 32 + kind, 8, stride=4), :] for gx in range(16)],
            axis=0,
        )
        for comp in range(3)
    ]


def by_vector(parts):
    low = lax.broadcasted_iota(jnp.int32, (128, 128), 1) < 64
    turned = [pltpu.roll(part, 64, 1) for part in parts]
    upper = [jnp.where(low, parts[0], turned[1]), jnp.where(low, parts[2], 0.0)]
    lower = [jnp.where(low, turned[0], parts[1]), jnp.where(low, turned[2], 0.0)]
    return jnp.concatenate(
        [jnp.concatenate(upper, axis=1), jnp.concatenate(lower, axis=1)], axis=0
    )


def one_lane(part, place):
    return jnp.concatenate(
        [jnp.broadcast_to(part[:, at : at + 1], (128, 128)) for at in (place, 64 + place)], axis=0
    )


def untucked(vectors, mixed):
    lane = lax.broadcasted_iota(jnp.int32, (128, 128), 1) & 63
    fixed = []
    for comp in range(3):
        here = vectors[comp]
        step = 4 if comp == 1 else 1
        above = pltpu.roll(here, 128 - step, 1)
        below = pltpu.roll(here, step, 1)
        value = (above - 2.0 * here) + below if comp == 0 else 0.5 * (above - below)
        held = (lane == STIFF_LANE) | (lane == MASS_LANE)
        fixed.append(jnp.where(held, value, mixed[comp]))
    return fixed


def product_kernel(rows_ref, mass_ref, out_ref):
    vectors = by_vector(parts_of(rows_ref, 0))
    image = by_vector(parts_of(rows_ref, 1))
    gram = dot(vectors * mass_ref[...], vectors, ((1,), (1,)))
    stiff = dot(vectors, image, ((1,), (1,)))
    row = lax.broadcasted_iota(jnp.int32, (256, 256), 0)
    column = lax.broadcasted_iota(jnp.int32, (256, 256), 1)
    both = jnp.where(row >= column, gram, stiff)
    out_ref[:256, :] = both[:, :128]
    out_ref[256:, :] = both[:, 128:]


def total_kernel(rows_ref, out_ref):
    total = jnp.sum(jnp.sum(rows_ref[...].reshape(64, 8, 128), axis=0), axis=0, keepdims=True)
    out_ref[...] = jnp.broadcast_to(total, (512, 128))


def factor_block(gram, stiff):
    lane = lax.broadcasted_iota(jnp.int32, (BLOCK, 128), 1)
    row = lax.broadcasted_iota(jnp.int32, (BLOCK, 128), 0)
    low = lane < 64
    columns = [
        jnp.where(
            low,
            jnp.broadcast_to(gram[:, j : j + 1], (BLOCK, 128)),
            jnp.broadcast_to(stiff[:, j : j + 1], (BLOCK, 128)),
        )
        for j in range(BLOCK)
    ]
    inverse = jnp.where((lane & 63) == row, 1.0, 0.0)
    pivots = jnp.ones((BLOCK, 128), jnp.float32)
    for k in range(BLOCK):
        column = columns[k]
        pivot = column[k : k + 1, :]
        pivots = jnp.where(row == k, pivot, pivots)
        if k + 1 == BLOCK:
            break
        part = (k + 1) // 8 * 8
        multiple = jnp.where(row[part:] > k, column[part:] * (1.0 / pivot), 0.0)

        def reduced(value):
            tail = value[part:] - multiple * value[k : k + 1, :]
            return tail if part == 0 else jnp.concatenate([value[:part], tail], axis=0)

        for j in range(k + 1, BLOCK):
            columns[j] = reduced(columns[j])
        inverse = reduced(inverse)
    return inverse * lax.rsqrt(pivots)


def final_kernel(sums_ref, rows_ref, subspace_ref, projected_ref, fields_ref, a_ref, e_ref):
    both = jnp.concatenate([sums_ref[:256, :], sums_ref[256:, :]], axis=1)
    mixed = parts_of(rows_ref, 2)
    diagonal = one_lane(mixed[0] + mixed[1] + mixed[2], STIFF_LANE)
    diagonal = jnp.concatenate([diagonal, diagonal], axis=1)
    lateral = one_lane(mixed[0], MASS_LANE)
    turned = both.T
    row = lax.broadcasted_iota(jnp.int32, (256, 256), 0)
    column = lax.broadcasted_iota(jnp.int32, (256, 256), 1)
    gram = jnp.where(row >= column, both, turned)
    stiff = jnp.where(row < column, both, jnp.where(row == column, diagonal, turned))
    a_ref[0] = gram
    a_ref[1] = stiff
    unit = jnp.where(row == column, 1.0, 0.0)
    e_ref[0] = unit
    e_ref[1] = unit
    lane = lax.broadcasted_iota(jnp.int32, (BLOCK, 128), 1)
    for first in range(0, 256, BLOCK):
        tile = first // 128 * 128
        inside = first - tile
        after = first + BLOCK
        small = [a_ref[m, first:after, tile : tile + 128][:, inside : inside + BLOCK] for m in (0, 1)]
        inverse = factor_block(small[0], small[1])
        for m in (0, 1):
            kept = jnp.where((lane >= 64 * m) & (lane < 64 * m + BLOCK), inverse, 0.0)
            shift = (inside - 64 * m) % 128
            spread = pltpu.roll(kept, shift, 1) if shift else kept
            own = kept[:, 64 * m : 64 * m + BLOCK]
            known = slice(0, 128) if after <= 128 else slice(0, 256)
            e_rows = dot(own, e_ref[m, first:after, known])
            e_ref[m, first:after, known] = e_rows
            if after < 256:
                open_ = slice(0, 256) if after < 128 else slice(128, 256)
                a_rows = dot(own, a_ref[m, first:after, open_])
                factor = dot(a_ref[m, after:, tile : tile + 128], spread, ((1,), (1,)))
                a_ref[m, after:, open_] = a_ref[m, after:, open_] - dot(factor, a_rows)
                e_ref[m, after:, known] = e_ref[m, after:, known] - dot(factor, e_rows)
    lower = e_ref[0]
    stiff_lower = e_ref[1]
    parts = parts_of(rows_ref, 0)
    vectors = by_vector(parts)
    mixed = untucked(parts, mixed)
    other = parts_of(rows_ref, 3)
    subspace = dot(vectors.T, lower, ((1,), (1,)))
    subspace_ref[...] = subspace[: 3 * NODES] * jnp.sqrt(jnp.float32(DEVICES * 3 * NODES))
    projected_ref[...] = dot(lower, dot(stiff, lower, ((1,), (1,))))
    weights = dot(stiff_lower.T, dot(stiff_lower, lateral))
    weights = jnp.concatenate([weights, weights], axis=1)
    axial = by_vector([other[0], mixed[1], mixed[2]])
    bending = by_vector([mixed[0], other[1], other[2]])
    for place, value in enumerate((vectors, axial, bending)):
        fields_ref[place : place + 1, :] = jnp.sum(value * weights, axis=0, keepdims=True)
    fields_ref[3:, :] = jnp.zeros((5, 256), jnp.float32)


def call(kernel, shape, scratch=(), smem=(), operands=()):
    return pl.pallas_call(
        kernel,
        out_shape=shape,
        in_specs=[
            pl.BlockSpec(memory_space=pltpu.SMEM if place in smem else pltpu.VMEM)
            for place in range(len(operands))
        ],
        out_specs=jax.tree.map(lambda _: pl.BlockSpec(memory_space=pltpu.VMEM), shape),
        scratch_shapes=list(scratch),
        compiler_params=pltpu.CompilerParams(vmem_limit_bytes=40 * 1024 * 1024),
    )(*operands)


def rows_of(count):
    return jax.ShapeDtypeStruct((count, 128), jnp.float32)


def exchange(rows, per_device):
    blocks = rows.reshape(DEVICES, per_device, 128)
    return lax.all_to_all(blocks, AXES, 0, 0, tiled=True).reshape(rows.shape)


def on_device(start_block, node_mass, ground_spring, stiffness, yield_flags, stress_old):
    width = start_block.shape[-1]
    share = jnp.mean(yield_flags.astype(jnp.float32), axis=1)
    tangent = (stiffness * (1.0 - 0.9 * share)[:, None]).reshape(3, 3, NODES)
    mass = node_mass.reshape(3, NODES)
    spring = ground_spring.reshape(3, NODES)
    coefficients = jnp.stack(
        [
            jnp.concatenate([tangent[0], tangent[1]], axis=1),
            jnp.concatenate([tangent[2], mass], axis=1),
            jnp.concatenate([spring, spring], axis=1),
        ],
        axis=1,
    ).reshape(9, 128)
    padded = pltpu.VMEM((18, 4, 8, 128), jnp.float32)
    plain = pltpu.VMEM((16, 4, 8, 128), jnp.float32)
    sent = call(
        pack_kernel, rows_of(2048), operands=(start_block.reshape(3 * NODES, width), coefficients)
    )
    gathered = exchange(sent, 4)
    own_top = call(spectrum_kernel, rows_of(32), (padded,), operands=(gathered,))
    tops = lax.all_to_all(
        own_top.reshape(4, 8, 128), "gy", 0, 0, tiled=True
    ).reshape(32, 128)
    component = lax.axis_index("gy").astype(jnp.int32).reshape(1)
    filtered = call(
        filter_kernel,
        rows_of(2048),
        (
            padded,
            padded,
            padded,
            pltpu.VMEM((3, 16, 4, 8, 128), jnp.float32),
            pltpu.VMEM((3, 16, 4, 8, 128), jnp.float32),
            plain,
            plain,
        ),
        smem=(0,),
        operands=(component, gathered, tops),
    )
    returned = exchange(filtered, 4)
    mass_row = jnp.pad(mass.reshape(1, 3 * NODES), ((0, 0), (0, NODES)))
    products = call(product_kernel, rows_of(512), operands=(returned, mass_row))
    totals = call(total_kernel, rows_of(512), operands=(exchange(products, 1),))
    subspace, projected, fields = call(
        final_kernel,
        (
            jax.ShapeDtypeStruct((3 * NODES, width), jnp.float32),
            jax.ShapeDtypeStruct((width, width), jnp.float32),
            jax.ShapeDtypeStruct((8, 256), jnp.float32),
        ),
        (
            pltpu.VMEM((2, 256, 256), jnp.float32),
            pltpu.VMEM((2, 256, 256), jnp.float32),
        ),
        operands=(exchange(totals, 1), returned),
    )
    place = node_mass.shape[1:]
    fields = fields[:3, : 3 * NODES].reshape((3, 3) + place)
    force = node_mass * fields[0]
    axial = fields[1]
    bending = jnp.roll(fields[2], -1, axis=0)
    fibers = stress_old.shape[1]
    heights = ((jnp.arange(fibers).astype(jnp.float32) + 0.5) / fibers - 0.5)[:, None, None, None]
    strain = axial[:, None] + heights * bending[:, None]
    own = jnp.stack([stiffness[d, d] for d in range(3)])[:, None]
    stress_new = stress_old + own * jnp.where(yield_flags == 1, 0.05, 1.0) * strain
    return (subspace.reshape(start_block.shape), projected, force, stress_new)


def solution(mesh):
    return jax.shard_map(
        on_device,
        mesh=mesh,
        in_specs=(
            P(None, "gx", "gy", "gz", None),
            P(None, "gx", "gy", "gz"),
            P(None, "gx", "gy", "gz"),
            P(None, None, "gx", "gy", "gz"),
            P(None, None, "gx", "gy", "gz"),
            P(None, None, "gx", "gy", "gz"),
        ),
        out_specs=(
            P(None, "gx", "gy", "gz", None),
            P(),
            P(None, "gx", "gy", "gz"),
            P(None, None, "gx", "gy", "gz"),
        ),
        check_vma=False,
    )
```

```python
import functools

import jax
import jax.numpy as jnp
from jax import lax
from jax.experimental import pallas as pl
from jax.experimental.pallas import tpu as pltpu
from jax.sharding import Mesh, PartitionSpec as P

DEGREE = 4
ITERS = 2
PRECISE = lax.Precision.HIGHEST
GX = ("cy", "core")
AXES = ("cy", "core", "gy", "gz")
CHIPS = ("cy", "gy", "gz")

NODES = 64
DEVICES = 512
OUT_ROWS = 5
BLOCK = 32
STIFF_LANE = 5
MASS_LANE = 6


def dot(a, b, contract=((1,), (0,))):
    return lax.dot_general(
        a, b, (contract, ((), ())), precision=PRECISE, preferred_element_type=jnp.float32
    )


def pack_kernel(start_ref, coef_ref, out_ref):
    for comp in range(4):
        if comp < 3:
            block = start_ref[comp * NODES : (comp + 1) * NODES, :]
            pairs = jnp.concatenate([block[:, :128], block[:, 128:]], axis=0).T
        else:
            pairs = jnp.zeros((128, 128), jnp.float32)
        source = comp % 3
        rows = [
            jnp.broadcast_to(coef_ref[source * 3 + r : source * 3 + r + 1, :], (8, 128))
            for r in range(3)
        ]
        for cy in range(8):
            first = (cy * 4 + comp) * 8 * OUT_ROWS
            for core in range(2):
                at = (cy * 2 + core) * 8
                out_ref[pl.ds(first + core, 8, stride=OUT_ROWS), :] = pairs[at : at + 8]
            for r in range(3):
                out_ref[pl.ds(first + 2 + r, 8, stride=OUT_ROWS), :] = rows[r]


def iota(axis):
    return lax.broadcasted_iota(jnp.int32, (4, 8, 128), axis)


def grid_row(refs, kind, gx, core):
    rows = [ref[pl.ds(gx // 2 * 32 * OUT_ROWS + kind, 32, stride=OUT_ROWS), :] for ref in refs]
    return jnp.where(core == gx % 2, rows[0], rows[1]).reshape(4, 8, 128)


def roll(value, shift, axis=2):
    return pltpu.roll(value, shift, axis)


def both_halves(value):
    lane = iota(2)
    turned = roll(value, 64)
    return jnp.where(lane < 64, value, turned), jnp.where(lane < 64, turned, value)


class Turned:
    def __init__(self, ref):
        self.ref = ref
        self.planes = {}

    def at(self, gx):
        if gx not in self.planes:
            if gx in (-1, 16):
                zero = jnp.zeros((4, 8, 128), jnp.float32)
                self.planes[gx] = (zero, zero)
            else:
                here = self.ref[gx]
                self.planes[gx] = (roll(here, 96), roll(here, 32))
        return self.planes[gx]

    def sides(self, gx):
        first = (iota(2) & 32) == 0
        up = jnp.where(first, self.at(gx)[0], self.at(gx + 1)[1])
        down = jnp.where(first, self.at(gx - 1)[0], self.at(gx)[1])
        return up, down


def y_up(here):
    moved = jnp.concatenate([here[1:], jnp.zeros((1, 8, 128), jnp.float32)], axis=0)
    return jnp.where((iota(2) & 28) != 28, roll(here, 124), roll(moved, 28))


def y_down(here):
    moved = jnp.concatenate([jnp.zeros((1, 8, 128), jnp.float32), here[:-1]], axis=0)
    return jnp.where((iota(2) & 28) != 0, roll(here, 4), roll(moved, 100))


def z_up(here):
    other = jnp.where(iota(1) < 7, roll(roll(here, 3), 7, 1), 0.0)
    return jnp.where((iota(2) & 3) != 3, roll(here, 127), other)


def z_down(here):
    other = jnp.where(iota(1) > 0, roll(roll(here, 125), 1, 1), 0.0)
    return jnp.where((iota(2) & 3) != 0, roll(here, 1), other)


def around(ref, turned, gx):
    here = ref[gx]
    return here, (turned.sides(gx), (y_up(here), y_down(here)), (z_up(here), z_down(here)))


def weights_kernel(
    core_ref, own_ref, other_ref, vectors_ref, up_ref, down_ref, diagonal_ref, mass_ref, top_ref,
    tangent_ref
):
    core = core_ref[0]
    refs = (own_ref, other_ref)
    second = []
    for gx in range(16):
        vectors_ref[gx] = grid_row(refs, core, gx, core)
        first, along_y = both_halves(grid_row(refs, 2, gx, core))
        tangent_ref[gx] = first
        second.append(along_y)
    turned = Turned(tangent_ref)
    best = jnp.zeros((4, 8, 128), jnp.float32)
    for gx in range(16):
        first = tangent_ref[gx]
        above, below = turned.sides(gx)
        third, mass = both_halves(grid_row(refs, 3, gx, core))
        spring = grid_row(refs, 4, gx, core)
        ups = [
            0.5 * (first + above),
            0.5 * (second[gx] + y_up(second[gx])),
            0.5 * (third + z_up(third)),
        ]
        downs = [
            0.5 * (first + below),
            0.5 * (second[gx] + y_down(second[gx])),
            0.5 * (third + z_down(third)),
        ]
        total = (ups[0] + ups[1] + ups[2]) + (downs[0] + downs[1] + downs[2])
        for direction in range(3):
            up_ref[direction, gx] = ups[direction]
            down_ref[direction, gx] = downs[direction]
        diagonal = spring + total
        diagonal_ref[gx] = diagonal
        mass_ref[gx] = mass
        best = jnp.maximum(best, (diagonal + total) / mass)
    best = jnp.max(jnp.max(best, axis=0), axis=(0, 1), keepdims=True)
    top_ref[...] = jnp.broadcast_to(best, (32, 128))


def filter_kernel(
    comp_ref, vectors_ref, up_ref, down_ref, diagonal_ref, mass_ref, top_ref, out_ref, even_ref,
    odd_ref, inverse_ref
):
    top = jnp.max(jnp.max(top_ref[...], axis=0, keepdims=True), axis=1, keepdims=True)
    middle = top * 9.0 / 16.0
    spread = top * 7.0 / 16.0
    inverse_spread = 1.0 / spread
    ratio = middle * inverse_spread
    for gx in range(16):
        inverse_ref[gx] = inverse_spread / mass_ref[gx]

    def stiffness_times(here, sides, gx):
        result = diagonal_ref[gx] * here
        for direction in range(3):
            result = result - up_ref[direction, gx] * sides[direction][0]
            result = result - down_ref[direction, gx] * sides[direction][1]
        return result

    for turn in range(ITERS):
        for repeat in range(DEGREE):
            current_ref, other_ref = (even_ref, odd_ref) if repeat % 2 == 0 else (odd_ref, even_ref)
            earlier_ref = other_ref
            if turn == 0:
                current_ref = vectors_ref if repeat == 0 else current_ref
                earlier_ref = vectors_ref if repeat == 1 else earlier_ref
            turned = Turned(current_ref)
            for gx in range(16):
                here, sides = around(current_ref, turned, gx)
                image = stiffness_times(here, sides, gx) * inverse_ref[gx] - ratio * here
                if repeat > 0:
                    image = 2.0 * image - earlier_ref[gx]
                other_ref[gx] = image

    comp = comp_ref[0]
    turned = Turned(even_ref)
    stiff_sum = jnp.zeros((4, 8, 128), jnp.float32)
    mass_sum = jnp.zeros((4, 8, 128), jnp.float32)
    for gx in range(16):
        here, sides = around(even_ref, turned, gx)
        axial = [0.5 * (up - down) for up, down in sides]
        bending = [(up - 2.0 * here) + down for up, down in sides]
        image = stiffness_times(here, sides, gx)
        values = [
            here,
            image,
            jnp.where(comp == 0, bending[2], jnp.where(comp == 1, axial[1], axial[2])),
            jnp.where(comp == 0, axial[0], jnp.where(comp == 1, bending[0], bending[1])),
        ]
        for kind in range(4):
            out_ref[pl.ds(gx * 128 + kind, 32, stride=4), :] = values[kind].reshape(32, 128)
        stiff_sum = stiff_sum + here * image
        mass_sum = mass_sum + here * mass_ref[gx]
    lane = lax.broadcasted_iota(jnp.int32, (1, 128), 1)
    sums = []
    for value in (stiff_sum, mass_sum):
        value = jnp.sum(jnp.sum(value, axis=0), axis=0, keepdims=True)
        low = jnp.sum(jnp.where(lane < 64, value, 0.0), axis=1, keepdims=True)
        high = jnp.sum(jnp.where(lane < 64, 0.0, value), axis=1, keepdims=True)
        sums.append(jnp.where(lane < 64, low, high))
    for gx in range(16):
        rows = pl.ds(gx * 128 + 2, 32, stride=4)
        value = jnp.where((lane & 63) == STIFF_LANE, sums[0], out_ref[rows, :])
        out_ref[rows, :] = jnp.where((lane & 63) == MASS_LANE, sums[1], value)


def parts_of(rows_ref, kind):
    return [
        jnp.concatenate(
            [rows_ref[pl.ds((gx * 4 + comp) * 32 + kind, 8, stride=4), :] for gx in range(16)],
            axis=0,
        )
        for comp in range(3)
    ]


def by_vector(parts):
    low = lax.broadcasted_iota(jnp.int32, (128, 128), 1) < 64
    turned = [pltpu.roll(part, 64, 1) for part in parts]
    upper = [jnp.where(low, parts[0], turned[1]), jnp.where(low, parts[2], 0.0)]
    lower = [jnp.where(low, turned[0], parts[1]), jnp.where(low, turned[2], 0.0)]
    return jnp.concatenate(
        [jnp.concatenate(upper, axis=1), jnp.concatenate(lower, axis=1)], axis=0
    )


def one_lane(part, place):
    return jnp.concatenate(
        [jnp.broadcast_to(part[:, at : at + 1], (128, 128)) for at in (place, 64 + place)], axis=0
    )


def untucked(vectors, mixed):
    lane = lax.broadcasted_iota(jnp.int32, (128, 128), 1) & 63
    fixed = []
    for comp in range(3):
        here = vectors[comp]
        step = 4 if comp == 1 else 1
        above = pltpu.roll(here, 128 - step, 1)
        below = pltpu.roll(here, step, 1)
        value = (above - 2.0 * here) + below if comp == 0 else 0.5 * (above - below)
        held = (lane == STIFF_LANE) | (lane == MASS_LANE)
        fixed.append(jnp.where(held, value, mixed[comp]))
    return fixed


def product_kernel(rows_ref, mass_ref, out_ref):
    vectors = by_vector(parts_of(rows_ref, 0))
    image = by_vector(parts_of(rows_ref, 1))
    gram = dot(vectors * mass_ref[...], vectors, ((1,), (1,)))
    stiff = dot(vectors, image, ((1,), (1,)))
    row = lax.broadcasted_iota(jnp.int32, (256, 256), 0)
    column = lax.broadcasted_iota(jnp.int32, (256, 256), 1)
    both = jnp.where(row >= column, gram, stiff)
    out_ref[:256, :] = both[:, :128]
    out_ref[256:, :] = both[:, 128:]


def total_kernel(count, copies, rows_ref, out_ref):
    total = jnp.sum(rows_ref[...].reshape(count, 16, 128), axis=0)
    out_ref[...] = jnp.broadcast_to(total[None], (copies, 16, 128)).reshape(copies * 16, 128)


def factor_block(gram, stiff):
    lane = lax.broadcasted_iota(jnp.int32, (BLOCK, 128), 1)
    row = lax.broadcasted_iota(jnp.int32, (BLOCK, 128), 0)
    low = lane < 64
    columns = [
        jnp.where(
            low,
            jnp.broadcast_to(gram[:, j : j + 1], (BLOCK, 128)),
            jnp.broadcast_to(stiff[:, j : j + 1], (BLOCK, 128)),
        )
        for j in range(BLOCK)
    ]
    inverse = jnp.where((lane & 63) == row, 1.0, 0.0)
    pivots = jnp.ones((BLOCK, 128), jnp.float32)
    for k in range(BLOCK):
        column = columns[k]
        pivot = column[k : k + 1, :]
        pivots = jnp.where(row == k, pivot, pivots)
        if k + 1 == BLOCK:
            break
        part = (k + 1) // 8 * 8
        multiple = jnp.where(row[part:] > k, column[part:] * (1.0 / pivot), 0.0)

        def reduced(value):
            tail = value[part:] - multiple * value[k : k + 1, :]
            return tail if part == 0 else jnp.concatenate([value[:part], tail], axis=0)

        for j in range(k + 1, BLOCK):
            columns[j] = reduced(columns[j])
        inverse = reduced(inverse)
    return inverse * lax.rsqrt(pivots)


def final_kernel(sums_ref, rows_ref, subspace_ref, projected_ref, fields_ref, a_ref, e_ref):
    both = jnp.concatenate([sums_ref[:256, :], sums_ref[256:, :]], axis=1)
    mixed = parts_of(rows_ref, 2)
    diagonal = one_lane(mixed[0] + mixed[1] + mixed[2], STIFF_LANE)
    diagonal = jnp.concatenate([diagonal, diagonal], axis=1)
    lateral = one_lane(mixed[0], MASS_LANE)
    turned = both.T
    row = lax.broadcasted_iota(jnp.int32, (256, 256), 0)
    column = lax.broadcasted_iota(jnp.int32, (256, 256), 1)
    gram = jnp.where(row >= column, both, turned)
    stiff = jnp.where(row < column, both, jnp.where(row == column, diagonal, turned))
    a_ref[0] = gram
    a_ref[1] = stiff
    unit = jnp.where(row == column, 1.0, 0.0)
    e_ref[0] = unit
    e_ref[1] = unit
    lane = lax.broadcasted_iota(jnp.int32, (BLOCK, 128), 1)
    for first in range(0, 256, BLOCK):
        tile = first // 128 * 128
        inside = first - tile
        after = first + BLOCK
        small = [a_ref[m, first:after, tile : tile + 128][:, inside : inside + BLOCK] for m in (0, 1)]
        inverse = factor_block(small[0], small[1])
        for m in (0, 1):
            kept = jnp.where((lane >= 64 * m) & (lane < 64 * m + BLOCK), inverse, 0.0)
            shift = (inside - 64 * m) % 128
            spread = pltpu.roll(kept, shift, 1) if shift else kept
            own = kept[:, 64 * m : 64 * m + BLOCK]
            known = slice(0, 128) if after <= 128 else slice(0, 256)
            e_rows = dot(own, e_ref[m, first:after, known])
            e_ref[m, first:after, known] = e_rows
            if after < 256:
                open_ = slice(0, 256) if after < 128 else slice(128, 256)
                a_rows = dot(own, a_ref[m, first:after, open_])
                factor = dot(a_ref[m, after:, tile : tile + 128], spread, ((1,), (1,)))
                a_ref[m, after:, open_] = a_ref[m, after:, open_] - dot(factor, a_rows)
                e_ref[m, after:, known] = e_ref[m, after:, known] - dot(factor, e_rows)
    lower = e_ref[0]
    stiff_lower = e_ref[1]
    parts = parts_of(rows_ref, 0)
    vectors = by_vector(parts)
    mixed = untucked(parts, mixed)
    other = parts_of(rows_ref, 3)
    subspace = dot(vectors.T, lower, ((1,), (1,)))
    subspace_ref[...] = subspace[: 3 * NODES] * jnp.sqrt(jnp.float32(DEVICES * 3 * NODES))
    projected_ref[...] = dot(lower, dot(stiff, lower, ((1,), (1,))))
    weights = dot(stiff_lower.T, dot(stiff_lower, lateral))
    weights = jnp.concatenate([weights, weights], axis=1)
    axial = by_vector([other[0], mixed[1], mixed[2]])
    bending = by_vector([mixed[0], other[1], other[2]])
    for place, value in enumerate((vectors, axial, bending)):
        fields_ref[place : place + 1, :] = jnp.sum(value * weights, axis=0, keepdims=True)
    fields_ref[3:, :] = jnp.zeros((5, 256), jnp.float32)


def call(kernel, shape, scratch=(), smem=(), operands=()):
    return pl.pallas_call(
        kernel,
        out_shape=shape,
        in_specs=[
            pl.BlockSpec(memory_space=pltpu.SMEM if place in smem else pltpu.VMEM)
            for place in range(len(operands))
        ],
        out_specs=jax.tree.map(lambda _: pl.BlockSpec(memory_space=pltpu.VMEM), shape),
        scratch_shapes=list(scratch),
        compiler_params=pltpu.CompilerParams(vmem_limit_bytes=40 * 1024 * 1024),
    )(*operands)


def rows_of(count):
    return jax.ShapeDtypeStruct((count, 128), jnp.float32)


def exchange(rows, axes, devices):
    per_device = rows.shape[0] // devices
    if per_device % 8 == 0:
        blocks = rows.reshape(devices, per_device, 128)
    else:
        blocks = rows.reshape(devices, per_device, 1, 128)
    return lax.all_to_all(blocks, axes, 0, 0, tiled=True).reshape(rows.shape)


def on_device(start_block, node_mass, ground_spring, stiffness, yield_flags, stress_old):
    width = start_block.shape[-1]
    share = jnp.mean(yield_flags.astype(jnp.float32), axis=1)
    tangent = (stiffness * (1.0 - 0.9 * share)[:, None]).reshape(3, 3, NODES)
    mass = node_mass.reshape(3, NODES)
    spring = ground_spring.reshape(3, NODES)
    coefficients = jnp.stack(
        [
            jnp.concatenate([tangent[0], tangent[1]], axis=1),
            jnp.concatenate([tangent[2], mass], axis=1),
            jnp.concatenate([spring, spring], axis=1),
        ],
        axis=1,
    ).reshape(9, 128)
    grid_shape = (16, 4, 8, 128)
    plain = pltpu.VMEM(grid_shape, jnp.float32)
    grid = jax.ShapeDtypeStruct(grid_shape, jnp.float32)
    grids = jax.ShapeDtypeStruct((3,) + grid_shape, jnp.float32)
    sent = call(
        pack_kernel,
        rows_of(256 * OUT_ROWS),
        operands=(start_block.reshape(3 * NODES, width), coefficients),
    )
    own = exchange(sent, CHIPS, 256)
    other = lax.ppermute(own, "core", [(0, 1), (1, 0)])
    core = lax.axis_index("core").astype(jnp.int32).reshape(1)
    component = lax.axis_index("gy").astype(jnp.int32).reshape(1)
    *weights, own_top = call(
        weights_kernel,
        (grid, grids, grids, grid, grid, rows_of(32)),
        (plain,),
        smem=(0,),
        operands=(core, own, other),
    )
    tops = exchange(own_top, "gy", 4)
    filtered = call(
        filter_kernel,
        rows_of(2048),
        (plain, plain, plain),
        smem=(0,),
        operands=(component, *weights, tops),
    )
    returned = exchange(filtered, AXES, DEVICES)
    mass_row = jnp.pad(mass.reshape(1, 3 * NODES), ((0, 0), (0, NODES)))
    products = call(product_kernel, rows_of(512), operands=(returned, mass_row))
    partial = call(
        functools.partial(total_kernel, 32, 16),
        rows_of(256),
        operands=(exchange(products, ("cy", "gy"), 32),),
    )
    totals = call(
        functools.partial(total_kernel, 16, 32),
        rows_of(512),
        operands=(exchange(partial, ("core", "gz"), 16),),
    )
    subspace, projected, fields = call(
        final_kernel,
        (
            jax.ShapeDtypeStruct((3 * NODES, width), jnp.float32),
            jax.ShapeDtypeStruct((width, width), jnp.float32),
            jax.ShapeDtypeStruct((8, 256), jnp.float32),
        ),
        (
            pltpu.VMEM((2, 256, 256), jnp.float32),
            pltpu.VMEM((2, 256, 256), jnp.float32),
        ),
        operands=(exchange(totals, ("cy", "gy"), 32), returned),
    )
    place = node_mass.shape[1:]
    fields = fields[:3, : 3 * NODES].reshape((3, 3) + place)
    force = node_mass * fields[0]
    axial = fields[1]
    bending = jnp.roll(fields[2], -1, axis=0)
    fibers = stress_old.shape[1]
    heights = ((jnp.arange(fibers).astype(jnp.float32) + 0.5) / fibers - 0.5)[:, None, None, None]
    strain = axial[:, None] + heights * bending[:, None]
    own = jnp.stack([stiffness[d, d] for d in range(3)])[:, None]
    stress_new = stress_old + own * jnp.where(yield_flags == 1, 0.05, 1.0) * strain
    return (subspace.reshape(start_block.shape), projected, force, stress_new)


def solution(mesh):
    chips = Mesh(mesh.devices.reshape(8, 2, 4, 8), AXES)
    return jax.shard_map(
        on_device,
        mesh=chips,
        in_specs=(
            P(None, GX, "gy", "gz", None),
            P(None, GX, "gy", "gz"),
            P(None, GX, "gy", "gz"),
            P(None, None, GX, "gy", "gz"),
            P(None, None, GX, "gy", "gz"),
            P(None, None, GX, "gy", "gz"),
        ),
        out_specs=(
            P(None, GX, "gy", "gz", None),
            P(),
            P(None, GX, "gy", "gz"),
            P(None, None, GX, "gy", "gz"),
        ),
        check_vma=False,
    )
```

```python
import functools

import jax
import jax.numpy as jnp
from jax import lax
from jax.experimental import pallas as pl
from jax.experimental.pallas import tpu as pltpu
from jax.sharding import Mesh, PartitionSpec as P

DEGREE = 4
ITERS = 2
PRECISE = lax.Precision.HIGHEST
GX = ("cy", "core")
AXES = ("cy", "core", "gy", "gz")
CHIPS = ("cy", "gy", "gz")

NODES = 64
DEVICES = 512
OUT_ROWS = 5
LEAST_PIVOT = 0.1
BLOCK = 32
STIFF_LANE = 5
MASS_LANE = 6


def dot(a, b, contract=((1,), (0,))):
    return lax.dot_general(
        a, b, (contract, ((), ())), precision=PRECISE, preferred_element_type=jnp.float32
    )


def pack_kernel(start_ref, coef_ref, out_ref):
    for comp in range(4):
        if comp < 3:
            block = start_ref[comp * NODES : (comp + 1) * NODES, :]
            pairs = jnp.concatenate([block[:, :128], block[:, 128:]], axis=0).T
        else:
            pairs = jnp.zeros((128, 128), jnp.float32)
        source = comp % 3
        rows = [
            jnp.broadcast_to(coef_ref[source * 3 + r : source * 3 + r + 1, :], (8, 128))
            for r in range(3)
        ]
        for cy in range(8):
            first = (cy * 4 + comp) * 8 * OUT_ROWS
            for core in range(2):
                at = (cy * 2 + core) * 8
                out_ref[pl.ds(first + core, 8, stride=OUT_ROWS), :] = pairs[at : at + 8]
            for r in range(3):
                out_ref[pl.ds(first + 2 + r, 8, stride=OUT_ROWS), :] = rows[r]


def iota(axis):
    return lax.broadcasted_iota(jnp.int32, (4, 8, 128), axis)


def grid_row(refs, kind, gx, core):
    rows = [ref[pl.ds(gx // 2 * 32 * OUT_ROWS + kind, 32, stride=OUT_ROWS), :] for ref in refs]
    return jnp.where(core == gx % 2, rows[0], rows[1]).reshape(4, 8, 128)


def roll(value, shift, axis=2):
    return pltpu.roll(value, shift, axis)


def both_halves(value):
    lane = iota(2)
    turned = roll(value, 64)
    return jnp.where(lane < 64, value, turned), jnp.where(lane < 64, turned, value)


class Turned:
    def __init__(self, ref):
        self.ref = ref
        self.planes = {}

    def at(self, gx):
        if gx not in self.planes:
            if gx in (-1, 16):
                zero = jnp.zeros((4, 8, 128), jnp.float32)
                self.planes[gx] = (zero, zero)
            else:
                here = self.ref[gx]
                self.planes[gx] = (roll(here, 96), roll(here, 32))
        return self.planes[gx]

    def sides(self, gx):
        first = (iota(2) & 32) == 0
        up = jnp.where(first, self.at(gx)[0], self.at(gx + 1)[1])
        down = jnp.where(first, self.at(gx - 1)[0], self.at(gx)[1])
        return up, down


def y_up(here):
    moved = jnp.concatenate([here[1:], jnp.zeros((1, 8, 128), jnp.float32)], axis=0)
    return jnp.where((iota(2) & 28) != 28, roll(here, 124), roll(moved, 28))


def y_down(here):
    moved = jnp.concatenate([jnp.zeros((1, 8, 128), jnp.float32), here[:-1]], axis=0)
    return jnp.where((iota(2) & 28) != 0, roll(here, 4), roll(moved, 100))


def z_up(here):
    other = jnp.where(iota(1) < 7, roll(roll(here, 3), 7, 1), 0.0)
    return jnp.where((iota(2) & 3) != 3, roll(here, 127), other)


def z_down(here):
    other = jnp.where(iota(1) > 0, roll(roll(here, 125), 1, 1), 0.0)
    return jnp.where((iota(2) & 3) != 0, roll(here, 1), other)


def around(ref, turned, gx):
    here = ref[gx]
    return here, (turned.sides(gx), (y_up(here), y_down(here)), (z_up(here), z_down(here)))


def weights_kernel(
    core_ref, own_ref, other_ref, vectors_ref, up_ref, down_ref, diagonal_ref, mass_ref, top_ref,
    tangent_ref
):
    core = core_ref[0]
    refs = (own_ref, other_ref)
    second = []
    for gx in range(16):
        vectors_ref[gx] = grid_row(refs, core, gx, core)
        first, along_y = both_halves(grid_row(refs, 2, gx, core))
        tangent_ref[gx] = first
        second.append(along_y)
    turned = Turned(tangent_ref)
    best = jnp.zeros((4, 8, 128), jnp.float32)
    for gx in range(16):
        first = tangent_ref[gx]
        above, below = turned.sides(gx)
        third, mass = both_halves(grid_row(refs, 3, gx, core))
        spring = grid_row(refs, 4, gx, core)
        ups = [
            0.5 * (first + above),
            0.5 * (second[gx] + y_up(second[gx])),
            0.5 * (third + z_up(third)),
        ]
        downs = [
            0.5 * (first + below),
            0.5 * (second[gx] + y_down(second[gx])),
            0.5 * (third + z_down(third)),
        ]
        total = (ups[0] + ups[1] + ups[2]) + (downs[0] + downs[1] + downs[2])
        for direction in range(3):
            up_ref[direction, gx] = ups[direction]
            down_ref[direction, gx] = downs[direction]
        diagonal = spring + total
        diagonal_ref[gx] = diagonal
        mass_ref[gx] = mass
        best = jnp.maximum(best, (diagonal + total) / mass)
    best = jnp.max(jnp.max(best, axis=0), axis=(0, 1), keepdims=True)
    top_ref[...] = jnp.broadcast_to(best, (32, 128))


def filter_kernel(
    comp_ref, vectors_ref, up_ref, down_ref, diagonal_ref, mass_ref, top_ref, out_ref, even_ref,
    odd_ref, inverse_ref
):
    top = jnp.max(jnp.max(top_ref[...], axis=0, keepdims=True), axis=1, keepdims=True)
    middle = top * 9.0 / 16.0
    spread = top * 7.0 / 16.0
    inverse_spread = 1.0 / spread
    ratio = middle * inverse_spread
    for gx in range(16):
        inverse_ref[gx] = inverse_spread / mass_ref[gx]

    def stiffness_times(here, sides, gx):
        result = diagonal_ref[gx] * here
        for direction in range(3):
            result = result - up_ref[direction, gx] * sides[direction][0]
            result = result - down_ref[direction, gx] * sides[direction][1]
        return result

    for turn in range(ITERS):
        for repeat in range(DEGREE):
            current_ref, other_ref = (even_ref, odd_ref) if repeat % 2 == 0 else (odd_ref, even_ref)
            earlier_ref = other_ref
            if turn == 0:
                current_ref = vectors_ref if repeat == 0 else current_ref
                earlier_ref = vectors_ref if repeat == 1 else earlier_ref
            turned = Turned(current_ref)
            for gx in range(16):
                here, sides = around(current_ref, turned, gx)
                image = stiffness_times(here, sides, gx) * inverse_ref[gx] - ratio * here
                if repeat > 0:
                    image = 2.0 * image - earlier_ref[gx]
                other_ref[gx] = image

    comp = comp_ref[0]
    turned = Turned(even_ref)
    stiff_sum = jnp.zeros((4, 8, 128), jnp.float32)
    mass_sum = jnp.zeros((4, 8, 128), jnp.float32)
    for gx in range(16):
        here, sides = around(even_ref, turned, gx)
        axial = [0.5 * (up - down) for up, down in sides]
        bending = [(up - 2.0 * here) + down for up, down in sides]
        image = stiffness_times(here, sides, gx)
        values = [
            here,
            image,
            jnp.where(comp == 0, bending[2], jnp.where(comp == 1, axial[1], axial[2])),
            jnp.where(comp == 0, axial[0], jnp.where(comp == 1, bending[0], bending[1])),
        ]
        for kind in range(4):
            out_ref[pl.ds(gx * 128 + kind, 32, stride=4), :] = values[kind].reshape(32, 128)
        stiff_sum = stiff_sum + here * image
        mass_sum = mass_sum + here * mass_ref[gx]
    lane = lax.broadcasted_iota(jnp.int32, (1, 128), 1)
    sums = []
    for value in (stiff_sum, mass_sum):
        value = jnp.sum(jnp.sum(value, axis=0), axis=0, keepdims=True)
        low = jnp.sum(jnp.where(lane < 64, value, 0.0), axis=1, keepdims=True)
        high = jnp.sum(jnp.where(lane < 64, 0.0, value), axis=1, keepdims=True)
        sums.append(jnp.where(lane < 64, low, high))
    for gx in range(16):
        rows = pl.ds(gx * 128 + 2, 32, stride=4)
        value = jnp.where((lane & 63) == STIFF_LANE, sums[0], out_ref[rows, :])
        out_ref[rows, :] = jnp.where((lane & 63) == MASS_LANE, sums[1], value)


def parts_of(rows_ref, kind):
    return [
        jnp.concatenate(
            [rows_ref[pl.ds((gx * 4 + comp) * 32 + kind, 8, stride=4), :] for gx in range(16)],
            axis=0,
        )
        for comp in range(3)
    ]


def by_vector(parts):
    low = lax.broadcasted_iota(jnp.int32, (128, 128), 1) < 64
    turned = [pltpu.roll(part, 64, 1) for part in parts]
    upper = [jnp.where(low, parts[0], turned[1]), jnp.where(low, parts[2], 0.0)]
    lower = [jnp.where(low, turned[0], parts[1]), jnp.where(low, turned[2], 0.0)]
    return jnp.concatenate(
        [jnp.concatenate(upper, axis=1), jnp.concatenate(lower, axis=1)], axis=0
    )


def one_lane(part, place):
    return jnp.concatenate(
        [jnp.broadcast_to(part[:, at : at + 1], (128, 128)) for at in (place, 64 + place)], axis=0
    )


def untucked(vectors, mixed):
    lane = lax.broadcasted_iota(jnp.int32, (128, 128), 1) & 63
    fixed = []
    for comp in range(3):
        here = vectors[comp]
        step = 4 if comp == 1 else 1
        above = pltpu.roll(here, 128 - step, 1)
        below = pltpu.roll(here, step, 1)
        value = (above - 2.0 * here) + below if comp == 0 else 0.5 * (above - below)
        held = (lane == STIFF_LANE) | (lane == MASS_LANE)
        fixed.append(jnp.where(held, value, mixed[comp]))
    return fixed


def product_kernel(rows_ref, mass_ref, out_ref):
    vectors = by_vector(parts_of(rows_ref, 0))
    image = by_vector(parts_of(rows_ref, 1))
    gram = dot(vectors * mass_ref[...], vectors, ((1,), (1,)))
    stiff = dot(vectors, image, ((1,), (1,)))
    row = lax.broadcasted_iota(jnp.int32, (256, 256), 0)
    column = lax.broadcasted_iota(jnp.int32, (256, 256), 1)
    both = jnp.where(row >= column, gram, stiff)
    out_ref[:256, :] = both[:, :128]
    out_ref[256:, :] = both[:, 128:]


def total_kernel(count, copies, rows_ref, out_ref):
    total = jnp.sum(rows_ref[...].reshape(count, 16, 128), axis=0)
    out_ref[...] = jnp.broadcast_to(total[None], (copies, 16, 128)).reshape(copies * 16, 128)


def factor_block(gram, stiff):
    lane = lax.broadcasted_iota(jnp.int32, (BLOCK, 128), 1)
    row = lax.broadcasted_iota(jnp.int32, (BLOCK, 128), 0)
    low = lane < 64
    columns = [
        jnp.where(
            low,
            jnp.broadcast_to(gram[:, j : j + 1], (BLOCK, 128)),
            jnp.broadcast_to(stiff[:, j : j + 1], (BLOCK, 128)),
        )
        for j in range(BLOCK)
    ]
    inverse = jnp.where((lane & 63) == row, 1.0, 0.0)
    scale = jnp.ones((BLOCK, 128), jnp.float32)
    link = jnp.zeros((BLOCK, 128), jnp.float32)
    for k in range(0, BLOCK, 2):
        one, two = columns[k], columns[k + 1]
        top = one[k : k + 1, :]
        side = one[k + 1 : k + 2, :]
        corner = two[k + 1 : k + 2, :]
        rest = top * corner - side * side
        scale = jnp.where(row == k, top, jnp.where(row == k + 1, rest / top, scale))
        link = jnp.where(row == k + 1, side / top, link)
        if k + 2 == BLOCK:
            break
        part = (k + 2) // 8 * 8
        factor = 1.0 / rest
        below = row[part:] > k + 1
        first = jnp.where(below, (one[part:] * corner - two[part:] * side) * factor, 0.0)
        second = jnp.where(below, (two[part:] * top - one[part:] * side) * factor, 0.0)

        def reduced(value):
            tail = value[part:] - (first * value[k : k + 1, :] + second * value[k + 1 : k + 2, :])
            return tail if part == 0 else jnp.concatenate([value[:part], tail], axis=0)

        for j in range(k + 2, BLOCK):
            columns[j] = reduced(columns[j])
        inverse = reduced(inverse)
    inverse = inverse - link * pltpu.roll(inverse, 1, 0)
    return inverse * lax.rsqrt(scale), scale


def rounded(value):
    return value.astype(jnp.bfloat16).astype(jnp.float32)


def three_parts(value):
    high = rounded(value)
    rest = value - high
    middle = rounded(rest)
    return high, middle, rest - middle


def four_copies(value):
    value = value + pltpu.roll(value, 32, 1)
    return value + pltpu.roll(value, 64, 1)


def left_groups(first, second):
    group = lax.broadcasted_iota(jnp.int32, first.shape, 1) // BLOCK
    high, middle, _ = three_parts(first)
    parts = three_parts(second)
    one = jnp.where(group < 2, high, middle)
    two = jnp.where(group == 0, parts[0], jnp.where(group == 1, parts[2], 0.0))
    return jnp.concatenate([one, two], axis=1).astype(jnp.bfloat16)


def right_lanes(copies):
    group = lax.broadcasted_iota(jnp.int32, copies.shape, 1) // BLOCK
    high, middle, low = three_parts(copies)
    one = jnp.where(group % 2 == 0, high, middle)
    two = jnp.where(group == 0, low, high)
    return jnp.concatenate([one, two], axis=1).astype(jnp.bfloat16)


def right_rows(value):
    high, middle, low = [part.astype(jnp.bfloat16) for part in three_parts(value)]
    return jnp.concatenate([high, middle, high, middle, low, high, high, high], axis=0)


def product(left, right, contract):
    return lax.dot_general(
        left, right, (contract, ((), ())), preferred_element_type=jnp.float32
    )


def invert_factors(m_ref, diagonal):
    lane = lax.broadcasted_iota(jnp.int32, (BLOCK, 128), 1)
    least = jnp.ones((BLOCK, 128), jnp.float32)
    for first in range(0, 256, BLOCK):
        tile = first // 128 * 128
        inside = first - tile
        after = first + BLOCK
        small = [m_ref[m, first:after, tile : tile + 128][:, inside : inside + BLOCK] for m in (0, 1)]
        inverse, pivots = factor_block(small[0], small[1])
        least = jnp.minimum(least, pivots / diagonal[first:after, :])
        for m in (0, 1):
            own = four_copies(
                jnp.where((lane >= 64 * m) & (lane < 64 * m + BLOCK), inverse, 0.0)
            )
            row = lax.broadcasted_iota(jnp.int32, (BLOCK, 256), 0)
            column = lax.broadcasted_iota(jnp.int32, (BLOCK, 256), 1) - first
            rows = m_ref[m, first:after, :]
            unit = jnp.where(column == row, 1.0, 0.0)
            rows = jnp.where((column >= 0) & (column < BLOCK), unit, rows)
            result = product(left_groups(own, own), right_rows(rows), ((1,), (0,)))
            m_ref[m, first:after, :] = result
            if after < 256:
                count = 256 - after
                lanes = lax.broadcasted_iota(jnp.int32, (count, 128), 1)
                held = (lanes >= inside) & (lanes < inside + BLOCK)
                left = four_copies(jnp.where(held, m_ref[m, after:, tile : tile + 128], 0.0))
                right = jnp.concatenate([right_lanes(own)] * 8, axis=0)
                factor = product(left_groups(left, left), right, ((1,), (1,)))
                column = lax.broadcasted_iota(jnp.int32, (count, 256), 1)
                rows = m_ref[m, after:, :]
                rows = jnp.where((column >= first) & (column < after), 0.0, rows)
                m_ref[m, after:, :] = rows - product(
                    left_groups(factor[:, :128], factor[:, 128:]), right_rows(result), ((1,), (0,))
                )
    return jnp.min(least, axis=(0, 1), keepdims=True)


def final_kernel(sums_ref, rows_ref, subspace_ref, projected_ref, fields_ref, least_ref, m_ref):
    both = jnp.concatenate([sums_ref[:256, :], sums_ref[256:, :]], axis=1)
    mixed = parts_of(rows_ref, 2)
    diagonal = one_lane(mixed[0] + mixed[1] + mixed[2], STIFF_LANE)
    diagonal = jnp.concatenate([diagonal, diagonal], axis=1)
    lateral = one_lane(mixed[0], MASS_LANE)
    turned = both.T
    row = lax.broadcasted_iota(jnp.int32, (256, 256), 0)
    column = lax.broadcasted_iota(jnp.int32, (256, 256), 1)
    gram = jnp.where(row >= column, both, turned)
    stiff = jnp.where(row < column, both, jnp.where(row == column, diagonal, turned))
    m_ref[0] = gram
    m_ref[1] = stiff
    half = lax.broadcasted_iota(jnp.int32, (256, 128), 1) < 64
    gram_diagonal = jnp.sum(jnp.where(row == column, gram, 0.0), axis=1, keepdims=True)
    least = invert_factors(m_ref, jnp.where(half, gram_diagonal, diagonal[:, :128]))
    least_ref[...] = jnp.broadcast_to(least, (8, 128))
    lower = jnp.where(row >= column, m_ref[0], 0.0)
    stiff_lower = jnp.where(row >= column, m_ref[1], 0.0)
    parts = parts_of(rows_ref, 0)
    vectors = by_vector(parts)
    mixed = untucked(parts, mixed)
    other = parts_of(rows_ref, 3)
    subspace = dot(vectors.T, lower, ((1,), (1,)))
    subspace_ref[...] = subspace[: 3 * NODES] * jnp.sqrt(jnp.float32(DEVICES * 3 * NODES))
    projected_ref[...] = dot(lower, dot(stiff, lower, ((1,), (1,))))
    weights = dot(stiff_lower.T, dot(stiff_lower, lateral))
    weights = jnp.concatenate([weights, weights], axis=1)
    axial = by_vector([other[0], mixed[1], mixed[2]])
    bending = by_vector([mixed[0], other[1], other[2]])
    for place, value in enumerate((vectors, axial, bending)):
        fields_ref[place : place + 1, :] = jnp.sum(value * weights, axis=0, keepdims=True)
    fields_ref[3:, :] = jnp.zeros((5, 256), jnp.float32)


def extended(block, first_dim):
    for place, axis in enumerate((GX, "gy", "gz")):
        dim = first_dim + place
        count = lax.axis_size(axis)
        forward = [(i, i + 1) for i in range(count - 1)]
        backward = [(target, source) for source, target in forward]
        last = block.shape[dim]
        low = lax.ppermute(lax.slice_in_dim(block, last - 1, last, axis=dim), axis, forward)
        high = lax.ppermute(lax.slice_in_dim(block, 0, 1, axis=dim), axis, backward)
        block = jnp.concatenate([low, block, high], axis=dim)
    return block


def neighbour(padded, leading, direction, sense):
    slicer = [slice(None)] * padded.ndim
    for position in range(3):
        slicer[leading + position] = slice(1, -1)
    slicer[leading + direction] = slice(2, None) if sense > 0 else slice(0, -2)
    return padded[tuple(slicer)]


def step_by_step(start_block, node_mass, ground_spring, stiffness, yield_flags):
    share = jnp.mean(yield_flags.astype(jnp.float32), axis=1)
    tangent = stiffness * (1.0 - 0.9 * share)[:, None]
    padded = extended(tangent, 2)
    edges = [
        [0.5 * (tangent[d] + neighbour(padded, 2, d, sense)[d]) for d in range(3)]
        for sense in (1, -1)
    ]
    edge_total = sum(edges[0]) + sum(edges[1])
    diagonal = ground_spring + edge_total
    top = lax.pmax(jnp.max((diagonal + edge_total) / node_mass), AXES)
    middle = top * 9.0 / 16.0
    spread = top * 7.0 / 16.0

    def apply_k(field):
        around_field = extended(field, 1)
        result = diagonal[..., None] * field
        for d in range(3):
            for sense, weights in ((1, edges[0]), (-1, edges[1])):
                result = result - weights[d][..., None] * neighbour(around_field, 1, d, sense)
        return result

    def shifted(field):
        return (apply_k(field) / node_mass[..., None] - middle * field) / spread

    width = start_block.shape[-1]
    mass_rows = node_mass.reshape(-1)
    vectors = start_block
    for turn in range(ITERS):
        earlier, current = vectors, shifted(vectors)
        for repeat in range(DEGREE - 1):
            earlier, current = current, 2.0 * shifted(current) - earlier
        flat_rows = current.reshape(-1, width)
        gram = lax.psum(dot(flat_rows.T, mass_rows[:, None] * flat_rows), AXES)
        factor = jnp.linalg.cholesky(gram)
        basis = lax.linalg.triangular_solve(factor, flat_rows.T, left_side=True, lower=True)
        vectors = basis.T.reshape(current.shape)
    image = apply_k(vectors).reshape(-1, width)
    projected = lax.psum(dot(basis, image), AXES)
    lateral = lax.psum(dot(basis[:, :NODES], mass_rows[:NODES, None]), AXES)
    factor = jnp.linalg.cholesky(projected)
    halfway = lax.linalg.triangular_solve(factor, lateral, left_side=True, lower=True)
    weights = lax.linalg.triangular_solve(
        factor, halfway, left_side=True, lower=True, transpose_a=True
    )
    displace = dot(weights.T, basis).reshape(node_mass.shape)
    padded = extended(displace, 1)
    axial = []
    bending = []
    for d in range(3):
        above = neighbour(padded, 1, d, 1)
        below = neighbour(padded, 1, d, -1)
        other = (d + 1) % 3
        axial.append(0.5 * (above[d] - below[d]))
        bending.append(above[other] - 2.0 * displace[other] + below[other])
    fields = jnp.stack([displace, jnp.stack(axial), jnp.roll(jnp.stack(bending), 1, axis=0)])
    return vectors * jnp.sqrt(jnp.float32(DEVICES * 3 * NODES)), projected, fields


def call(kernel, shape, scratch=(), smem=(), operands=()):
    return pl.pallas_call(
        kernel,
        out_shape=shape,
        in_specs=[
            pl.BlockSpec(memory_space=pltpu.SMEM if place in smem else pltpu.VMEM)
            for place in range(len(operands))
        ],
        out_specs=jax.tree.map(lambda _: pl.BlockSpec(memory_space=pltpu.VMEM), shape),
        scratch_shapes=list(scratch),
        compiler_params=pltpu.CompilerParams(vmem_limit_bytes=40 * 1024 * 1024),
    )(*operands)


def rows_of(count):
    return jax.ShapeDtypeStruct((count, 128), jnp.float32)


def exchange(rows, axes, devices):
    per_device = rows.shape[0] // devices
    if per_device % 8 == 0:
        blocks = rows.reshape(devices, per_device, 128)
    else:
        blocks = rows.reshape(devices, per_device, 1, 128)
    return lax.all_to_all(blocks, axes, 0, 0, tiled=True).reshape(rows.shape)


def on_device(start_block, node_mass, ground_spring, stiffness, yield_flags, stress_old):
    width = start_block.shape[-1]
    share = jnp.mean(yield_flags.astype(jnp.float32), axis=1)
    tangent = (stiffness * (1.0 - 0.9 * share)[:, None]).reshape(3, 3, NODES)
    mass = node_mass.reshape(3, NODES)
    spring = ground_spring.reshape(3, NODES)
    coefficients = jnp.stack(
        [
            jnp.concatenate([tangent[0], tangent[1]], axis=1),
            jnp.concatenate([tangent[2], mass], axis=1),
            jnp.concatenate([spring, spring], axis=1),
        ],
        axis=1,
    ).reshape(9, 128)
    grid_shape = (16, 4, 8, 128)
    plain = pltpu.VMEM(grid_shape, jnp.float32)
    grid = jax.ShapeDtypeStruct(grid_shape, jnp.float32)
    grids = jax.ShapeDtypeStruct((3,) + grid_shape, jnp.float32)
    sent = call(
        pack_kernel,
        rows_of(256 * OUT_ROWS),
        operands=(start_block.reshape(3 * NODES, width), coefficients),
    )
    own = exchange(sent, CHIPS, 256)
    other = lax.ppermute(own, "core", [(0, 1), (1, 0)])
    core = lax.axis_index("core").astype(jnp.int32).reshape(1)
    component = lax.axis_index("gy").astype(jnp.int32).reshape(1)
    *weights, own_top = call(
        weights_kernel,
        (grid, grids, grids, grid, grid, rows_of(32)),
        (plain,),
        smem=(0,),
        operands=(core, own, other),
    )
    tops = exchange(own_top, "gy", 4)
    filtered = call(
        filter_kernel,
        rows_of(2048),
        (plain, plain, plain),
        smem=(0,),
        operands=(component, *weights, tops),
    )
    returned = exchange(filtered, AXES, DEVICES)
    mass_row = jnp.pad(mass.reshape(1, 3 * NODES), ((0, 0), (0, NODES)))
    products = call(product_kernel, rows_of(512), operands=(returned, mass_row))
    partial = call(
        functools.partial(total_kernel, 32, 16),
        rows_of(256),
        operands=(exchange(products, ("cy", "gy"), 32),),
    )
    totals = call(
        functools.partial(total_kernel, 16, 32),
        rows_of(512),
        operands=(exchange(partial, ("core", "gz"), 16),),
    )
    subspace, projected, fields, least = call(
        final_kernel,
        (
            jax.ShapeDtypeStruct((3 * NODES, width), jnp.float32),
            jax.ShapeDtypeStruct((width, width), jnp.float32),
            jax.ShapeDtypeStruct((8, 256), jnp.float32),
            rows_of(8),
        ),
        (pltpu.VMEM((2, 256, 256), jnp.float32),),
        operands=(exchange(totals, ("cy", "gy"), 32), returned),
    )
    place = node_mass.shape[1:]
    fields = fields[:3, : 3 * NODES].reshape((3, 3) + place)
    subspace, projected, fields = lax.cond(
        least[0, 0] > LEAST_PIVOT,
        lambda *operands: operands[:3],
        lambda *operands: step_by_step(*operands[3:]),
        subspace.reshape(start_block.shape),
        projected,
        fields,
        start_block,
        node_mass,
        ground_spring,
        stiffness,
        yield_flags,
    )
    force = node_mass * fields[0]
    axial = fields[1]
    bending = jnp.roll(fields[2], -1, axis=0)
    fibers = stress_old.shape[1]
    heights = ((jnp.arange(fibers).astype(jnp.float32) + 0.5) / fibers - 0.5)[:, None, None, None]
    strain = axial[:, None] + heights * bending[:, None]
    own_stiffness = jnp.stack([stiffness[d, d] for d in range(3)])[:, None]
    stress_new = stress_old + own_stiffness * jnp.where(yield_flags == 1, 0.05, 1.0) * strain
    return (subspace, projected, force, stress_new)


def solution(mesh):
    chips = Mesh(mesh.devices.reshape(8, 2, 4, 8), AXES)
    return jax.shard_map(
        on_device,
        mesh=chips,
        in_specs=(
            P(None, GX, "gy", "gz", None),
            P(None, GX, "gy", "gz"),
            P(None, GX, "gy", "gz"),
            P(None, None, GX, "gy", "gz"),
            P(None, None, GX, "gy", "gz"),
            P(None, None, GX, "gy", "gz"),
        ),
        out_specs=(
            P(None, GX, "gy", "gz", None),
            P(),
            P(None, GX, "gy", "gz"),
            P(None, None, GX, "gy", "gz"),
        ),
        check_vma=False,
    )
```

```python
import functools

import jax
import jax.numpy as jnp
import numpy as np
from jax import lax
from jax.experimental import pallas as pl
from jax.experimental.pallas import tpu as pltpu
from jax.sharding import Mesh, PartitionSpec as P

DEGREE = 4
ITERS = 2
TOTAL = DEGREE * ITERS
PRECISE = lax.Precision.HIGHEST
GX = ("cy", "core")
AXES = ("cy", "core", "gy", "gz")
CHIPS = ("cy", "gy", "gz")

NODES = 64
DEVICES = 512
OUT_ROWS = 5
LEAST_PIVOT = 0.1
BLOCK = 32
STIFF_LANE = 9
MASS_LANE = 10


def dot(a, b, contract=((1,), (0,))):
    return lax.dot_general(
        a, b, (contract, ((), ())), precision=PRECISE, preferred_element_type=jnp.float32
    )


def spread_nodes(values, keep):
    groups = jnp.where(keep, values.reshape((-1,) + keep.shape), 0.0)
    return jnp.sum(groups, axis=1)


def pack_kernel(start_ref, stiffness_ref, node_ref, flags_ref, out_ref):
    lane = lax.broadcasted_iota(jnp.int32, (8, 128), 1)
    place = lax.broadcasted_iota(jnp.int32, (8, 128), 0)
    repeated = jnp.where((lane & 7) == place, 1.0, 0.0)
    keep = ((lane >> 3) & 7) == place
    stiffness = spread_nodes(dot(stiffness_ref[...], repeated), keep)
    nodes = spread_nodes(dot(node_ref[...], repeated), keep)
    counts = jnp.dot(
        flags_ref[...].astype(jnp.bfloat16),
        jnp.ones((16, 128), jnp.bfloat16),
        preferred_element_type=jnp.float32,
    )
    lane = lax.broadcasted_iota(jnp.int32, (NODES, 128), 1)
    place = lax.broadcasted_iota(jnp.int32, (NODES, 128), 0)
    own = ((place >> 5) * 32 + (place & 3) * 8 + ((place >> 2) & 7)) == (lane & 63)
    softening = 1.0 - 0.9 * (spread_nodes(counts, own) / 16.0)
    low = lax.broadcasted_iota(jnp.int32, (1, 128), 1) < 64
    for comp in range(4):
        source = comp % 3
        if comp < 3:
            block = jnp.concatenate(
                [
                    start_ref[comp * 16 + x * 8 : comp * 16 + x * 8 + 8, z, :]
                    for x in range(2)
                    for z in range(4)
                ],
                axis=0,
            )
            pairs = jnp.concatenate([block[:, :128], block[:, 128:]], axis=0).T
        else:
            pairs = jnp.zeros((128, 128), jnp.float32)
        tangent = [
            stiffness[3 * d + source : 3 * d + source + 1, :] * softening[d : d + 1, :]
            for d in range(3)
        ]
        mass = nodes[source : source + 1, :]
        spring = nodes[3 + source : 4 + source, :]
        rows = [
            jnp.broadcast_to(row, (8, 128))
            for row in (
                jnp.where(low, tangent[0], tangent[1]),
                jnp.where(low, tangent[2], mass),
                spring,
            )
        ]
        for cy in range(8):
            first = (cy * 4 + comp) * 8 * OUT_ROWS
            for core in range(2):
                at = (cy * 2 + core) * 8
                out_ref[pl.ds(first + core, 8, stride=OUT_ROWS), :] = pairs[at : at + 8]
            for r in range(3):
                out_ref[pl.ds(first + 2 + r, 8, stride=OUT_ROWS), :] = rows[r]


def iota(axis):
    return lax.broadcasted_iota(jnp.int32, (4, 8, 128), axis)


def grid_row(refs, kind, gx, core):
    rows = [ref[pl.ds(gx // 2 * 32 * OUT_ROWS + kind, 32, stride=OUT_ROWS), :] for ref in refs]
    return jnp.where(core == gx % 2, rows[0], rows[1]).reshape(4, 8, 128)


def roll(value, shift, axis=2):
    return pltpu.roll(value, shift, axis)


def both_halves(value):
    lane = iota(2)
    turned = roll(value, 64)
    return jnp.where(lane < 64, value, turned), jnp.where(lane < 64, turned, value)


class Turned:
    def __init__(self, ref):
        self.ref = ref
        self.planes = {}

    def at(self, gx):
        if gx not in self.planes:
            if gx in (-1, 16):
                zero = jnp.zeros((4, 8, 128), jnp.float32)
                self.planes[gx] = (zero, zero)
            else:
                here = self.ref[gx]
                self.planes[gx] = (roll(here, 96), roll(here, 32))
        return self.planes[gx]

    def sides(self, gx):
        first = (iota(2) & 32) == 0
        up = jnp.where(first, self.at(gx)[0], self.at(gx + 1)[1])
        down = jnp.where(first, self.at(gx - 1)[0], self.at(gx)[1])
        return up, down


def y_up(here):
    moved = jnp.concatenate([here[1:], jnp.zeros((1, 8, 128), jnp.float32)], axis=0)
    return jnp.where((iota(2) & 7) != 7, roll(here, 127), roll(moved, 7))


def y_down(here):
    moved = jnp.concatenate([jnp.zeros((1, 8, 128), jnp.float32), here[:-1]], axis=0)
    return jnp.where((iota(2) & 7) != 0, roll(here, 1), roll(moved, 121))


def z_up(here):
    other = jnp.where(iota(1) < 7, roll(roll(here, 24), 7, 1), 0.0)
    return jnp.where((iota(2) & 24) != 24, roll(here, 120), other)


def z_down(here):
    other = jnp.where(iota(1) > 0, roll(roll(here, 104), 1, 1), 0.0)
    return jnp.where((iota(2) & 24) != 0, roll(here, 8), other)


def around(ref, turned, gx):
    here = ref[gx]
    return here, (turned.sides(gx), (y_up(here), y_down(here)), (z_up(here), z_down(here)))


def weights_kernel(
    core_ref, own_ref, other_ref, vectors_ref, up_ref, down_ref, diagonal_ref, mass_ref, top_ref,
    tangent_ref
):
    core = core_ref[0]
    refs = (own_ref, other_ref)
    second = []
    for gx in range(16):
        vectors_ref[gx] = grid_row(refs, core, gx, core)
        first, along_y = both_halves(grid_row(refs, 2, gx, core))
        tangent_ref[gx] = first
        second.append(along_y)
    turned = Turned(tangent_ref)
    best = jnp.zeros((4, 8, 128), jnp.float32)
    for gx in range(16):
        first = tangent_ref[gx]
        above, below = turned.sides(gx)
        third, mass = both_halves(grid_row(refs, 3, gx, core))
        spring = grid_row(refs, 4, gx, core)
        ups = [
            0.5 * (first + above),
            0.5 * (second[gx] + y_up(second[gx])),
            0.5 * (third + z_up(third)),
        ]
        downs = [
            0.5 * (first + below),
            0.5 * (second[gx] + y_down(second[gx])),
            0.5 * (third + z_down(third)),
        ]
        total = (ups[0] + ups[1] + ups[2]) + (downs[0] + downs[1] + downs[2])
        for direction in range(3):
            up_ref[direction, gx] = ups[direction]
            down_ref[direction, gx] = downs[direction]
        diagonal = spring + total
        diagonal_ref[gx] = diagonal
        mass_ref[gx] = mass
        best = jnp.maximum(best, (diagonal + total) / mass)
    best = jnp.max(jnp.max(best, axis=0), axis=(0, 1), keepdims=True)
    top_ref[...] = jnp.broadcast_to(best, (32, 128))


def filter_kernel(
    vectors_ref, up_ref, down_ref, diagonal_ref, mass_ref, top_ref, terms_ref, inverse_ref
):
    top = top_ref[0:1, :]
    inverse_spread = 1.0 / (top * 7.0 / 16.0)
    ratio = (top * 9.0 / 16.0) * inverse_spread
    for gx in range(16):
        inverse_ref[gx] = inverse_spread / mass_ref[gx]
        terms_ref[0, gx] = vectors_ref[gx]
        terms_ref[TOTAL + 2, gx] = mass_ref[gx]
    for degree in range(1, TOTAL + 2):
        current_ref = vectors_ref if degree == 1 else terms_ref.at[degree - 1]
        turned = Turned(current_ref)
        for gx in range(16):
            here, sides = around(current_ref, turned, gx)
            image = diagonal_ref[gx] * here
            for direction in range(3):
                image = image - up_ref[direction, gx] * sides[direction][0]
                image = image - down_ref[direction, gx] * sides[direction][1]
            image = image * inverse_ref[gx] - ratio * here
            if degree > 1:
                image = 2.0 * image - terms_ref[degree - 2, gx]
            terms_ref[degree, gx] = image


def combine_kernel(
    comp_ref, terms_ref, own_top_ref, top_ref, nodes_ref, out_ref, even_ref, image_ref
):
    top = jnp.max(jnp.max(top_ref[...], axis=0, keepdims=True), axis=1, keepdims=True)
    own_top = own_top_ref[0:1, :]
    part = own_top / top
    place = part * nodes_ref[0:1, :] + (part - 1.0) * (9.0 / 7.0)
    square = place * place
    once = 8.0 * square * square - 8.0 * square + 1.0
    coefficients = jnp.sum(nodes_ref[8:40, :] * (once * once), axis=1, keepdims=True)
    middle = own_top * 9.0 / 16.0
    spread = own_top * 7.0 / 16.0
    for gx in range(16):
        total = coefficients[0:1, :] * terms_ref[0, gx]
        scaled = coefficients[16:17, :] * terms_ref[0, gx]
        for degree in range(1, TOTAL + 2):
            term = terms_ref[degree, gx]
            if degree <= TOTAL:
                total = total + coefficients[degree : degree + 1, :] * term
            scaled = scaled + coefficients[16 + degree : 17 + degree, :] * term
        even_ref[gx] = total
        image_ref[gx] = terms_ref[TOTAL + 2, gx] * (middle * total + spread * scaled)

    comp = comp_ref[0]
    turned = Turned(even_ref)
    stiff_sum = jnp.zeros((4, 8, 128), jnp.float32)
    mass_sum = jnp.zeros((4, 8, 128), jnp.float32)
    for gx in range(16):
        here, sides = around(even_ref, turned, gx)
        axial = [0.5 * (up - down) for up, down in sides]
        bending = [(up - 2.0 * here) + down for up, down in sides]
        image = image_ref[gx]
        values = [
            here,
            image,
            jnp.where(comp == 0, bending[2], jnp.where(comp == 1, axial[1], axial[2])),
            jnp.where(comp == 0, axial[0], jnp.where(comp == 1, bending[0], bending[1])),
        ]
        for kind in range(4):
            out_ref[pl.ds(gx * 128 + kind, 32, stride=4), :] = values[kind].reshape(32, 128)
        stiff_sum = stiff_sum + here * image
        mass_sum = mass_sum + here * terms_ref[TOTAL + 2, gx]
    lane = lax.broadcasted_iota(jnp.int32, (1, 128), 1)
    sums = []
    for value in (stiff_sum, mass_sum):
        value = jnp.sum(jnp.sum(value, axis=0), axis=0, keepdims=True)
        low = jnp.sum(jnp.where(lane < 64, value, 0.0), axis=1, keepdims=True)
        high = jnp.sum(jnp.where(lane < 64, 0.0, value), axis=1, keepdims=True)
        sums.append(jnp.where(lane < 64, low, high))
    for gx in range(16):
        rows = pl.ds(gx * 128 + 2, 32, stride=4)
        value = jnp.where((lane & 63) == STIFF_LANE, sums[0], out_ref[rows, :])
        out_ref[rows, :] = jnp.where((lane & 63) == MASS_LANE, sums[1], value)


def parts_of(rows_ref, kind):
    return [
        jnp.concatenate(
            [rows_ref[pl.ds((gx * 4 + comp) * 32 + kind, 8, stride=4), :] for gx in range(16)],
            axis=0,
        )
        for comp in range(3)
    ]


def by_vector(parts):
    low = lax.broadcasted_iota(jnp.int32, (128, 128), 1) < 64
    turned = [pltpu.roll(part, 64, 1) for part in parts]
    upper = [jnp.where(low, parts[0], turned[1]), jnp.where(low, parts[2], 0.0)]
    lower = [jnp.where(low, turned[0], parts[1]), jnp.where(low, turned[2], 0.0)]
    return jnp.concatenate(
        [jnp.concatenate(upper, axis=1), jnp.concatenate(lower, axis=1)], axis=0
    )


def one_lane(part, place):
    return jnp.concatenate(
        [jnp.broadcast_to(part[:, at : at + 1], (128, 128)) for at in (place, 64 + place)], axis=0
    )


def untucked(vectors, mixed):
    lane = lax.broadcasted_iota(jnp.int32, (128, 128), 1) & 63
    fixed = []
    for comp in range(3):
        here = vectors[comp]
        step = 1 if comp == 1 else 8
        above = pltpu.roll(here, 128 - step, 1)
        below = pltpu.roll(here, step, 1)
        value = (above - 2.0 * here) + below if comp == 0 else 0.5 * (above - below)
        held = (lane == STIFF_LANE) | (lane == MASS_LANE)
        fixed.append(jnp.where(held, value, mixed[comp]))
    return fixed


def product_kernel(rows_ref, mass_ref, out_ref):
    vectors = by_vector(parts_of(rows_ref, 0))
    image = by_vector(parts_of(rows_ref, 1))
    gram = dot(vectors * mass_ref[...], vectors, ((1,), (1,)))
    stiff = dot(vectors, image, ((1,), (1,)))
    row = lax.broadcasted_iota(jnp.int32, (256, 256), 0)
    column = lax.broadcasted_iota(jnp.int32, (256, 256), 1)
    both = jnp.where(row >= column, gram, stiff)
    out_ref[:256, :] = both[:, :128]
    out_ref[256:, :] = both[:, 128:]


def total_kernel(count, copies, rows_ref, out_ref):
    total = jnp.sum(rows_ref[...].reshape(count, 16, 128), axis=0)
    out_ref[...] = jnp.broadcast_to(total[None], (copies, 16, 128)).reshape(copies * 16, 128)


def factor_block(gram, stiff):
    lane = lax.broadcasted_iota(jnp.int32, (BLOCK, 128), 1)
    row = lax.broadcasted_iota(jnp.int32, (BLOCK, 128), 0)
    low = lane < 64
    columns = [
        jnp.where(
            low,
            jnp.broadcast_to(gram[:, j : j + 1], (BLOCK, 128)),
            jnp.broadcast_to(stiff[:, j : j + 1], (BLOCK, 128)),
        )
        for j in range(BLOCK)
    ]
    inverse = jnp.where((lane & 63) == row, 1.0, 0.0)
    scale = jnp.ones((BLOCK, 128), jnp.float32)
    link = jnp.zeros((BLOCK, 128), jnp.float32)
    for k in range(0, BLOCK, 2):
        one, two = columns[k], columns[k + 1]
        top = one[k : k + 1, :]
        side = one[k + 1 : k + 2, :]
        corner = two[k + 1 : k + 2, :]
        rest = top * corner - side * side
        scale = jnp.where(row == k, top, jnp.where(row == k + 1, rest / top, scale))
        link = jnp.where(row == k + 1, side / top, link)
        if k + 2 == BLOCK:
            break
        part = (k + 2) // 8 * 8
        factor = 1.0 / rest
        below = row[part:] > k + 1
        first = jnp.where(below, (one[part:] * corner - two[part:] * side) * factor, 0.0)
        second = jnp.where(below, (two[part:] * top - one[part:] * side) * factor, 0.0)

        def reduced(value):
            tail = value[part:] - (first * value[k : k + 1, :] + second * value[k + 1 : k + 2, :])
            return tail if part == 0 else jnp.concatenate([value[:part], tail], axis=0)

        for j in range(k + 2, BLOCK):
            columns[j] = reduced(columns[j])
        inverse = reduced(inverse)
    inverse = inverse - link * pltpu.roll(inverse, 1, 0)
    return inverse * lax.rsqrt(scale), scale


def rounded(value):
    return value.astype(jnp.bfloat16).astype(jnp.float32)


def three_parts(value):
    high = rounded(value)
    rest = value - high
    middle = rounded(rest)
    return high, middle, rest - middle


def four_copies(value):
    value = value + pltpu.roll(value, 32, 1)
    return value + pltpu.roll(value, 64, 1)


def left_groups(first, second):
    group = lax.broadcasted_iota(jnp.int32, first.shape, 1) // BLOCK
    high, middle, _ = three_parts(first)
    parts = three_parts(second)
    one = jnp.where(group < 2, high, middle)
    two = jnp.where(group == 0, parts[0], jnp.where(group == 1, parts[2], 0.0))
    return jnp.concatenate([one, two], axis=1).astype(jnp.bfloat16)


def right_lanes(copies):
    group = lax.broadcasted_iota(jnp.int32, copies.shape, 1) // BLOCK
    high, middle, low = three_parts(copies)
    one = jnp.where(group % 2 == 0, high, middle)
    two = jnp.where(group == 0, low, high)
    return jnp.concatenate([one, two], axis=1).astype(jnp.bfloat16)


def right_rows(value):
    high, middle, low = [part.astype(jnp.bfloat16) for part in three_parts(value)]
    return jnp.concatenate([high, middle, high, middle, low, high, high, high], axis=0)


def product(left, right, contract):
    return lax.dot_general(
        left, right, (contract, ((), ())), preferred_element_type=jnp.float32
    )


def invert_factors(m_ref, diagonal):
    lane = lax.broadcasted_iota(jnp.int32, (BLOCK, 128), 1)
    least = jnp.ones((BLOCK, 128), jnp.float32)
    for first in range(0, 256, BLOCK):
        tile = first // 128 * 128
        inside = first - tile
        after = first + BLOCK
        small = [m_ref[m, first:after, tile : tile + 128][:, inside : inside + BLOCK] for m in (0, 1)]
        inverse, pivots = factor_block(small[0], small[1])
        least = jnp.minimum(least, pivots / diagonal[first:after, :])
        for m in (0, 1):
            own = four_copies(
                jnp.where((lane >= 64 * m) & (lane < 64 * m + BLOCK), inverse, 0.0)
            )
            row = lax.broadcasted_iota(jnp.int32, (BLOCK, 256), 0)
            column = lax.broadcasted_iota(jnp.int32, (BLOCK, 256), 1) - first
            rows = m_ref[m, first:after, :]
            unit = jnp.where(column == row, 1.0, 0.0)
            rows = jnp.where((column >= 0) & (column < BLOCK), unit, rows)
            result = product(left_groups(own, own), right_rows(rows), ((1,), (0,)))
            m_ref[m, first:after, :] = result
            if after < 256:
                count = 256 - after
                lanes = lax.broadcasted_iota(jnp.int32, (count, 128), 1)
                held = (lanes >= inside) & (lanes < inside + BLOCK)
                left = four_copies(jnp.where(held, m_ref[m, after:, tile : tile + 128], 0.0))
                right = jnp.concatenate([right_lanes(own)] * 8, axis=0)
                factor = product(left_groups(left, left), right, ((1,), (1,)))
                column = lax.broadcasted_iota(jnp.int32, (count, 256), 1)
                rows = m_ref[m, after:, :]
                rows = jnp.where((column >= first) & (column < after), 0.0, rows)
                m_ref[m, after:, :] = rows - product(
                    left_groups(factor[:, :128], factor[:, 128:]), right_rows(result), ((1,), (0,))
                )
    return jnp.min(least, axis=(0, 1), keepdims=True)


def final_kernel(
    sums_ref, rows_ref, mass_ref, modulus_ref, stress_ref, subspace_ref, projected_ref, force_ref,
    stress_new_ref, least_ref, m_ref
):
    both = jnp.concatenate([sums_ref[:256, :], sums_ref[256:, :]], axis=1)
    mixed = parts_of(rows_ref, 2)
    diagonal = one_lane(mixed[0] + mixed[1] + mixed[2], STIFF_LANE)
    diagonal = jnp.concatenate([diagonal, diagonal], axis=1)
    lateral = one_lane(mixed[0], MASS_LANE)
    turned = both.T
    row = lax.broadcasted_iota(jnp.int32, (256, 256), 0)
    column = lax.broadcasted_iota(jnp.int32, (256, 256), 1)
    gram = jnp.where(row >= column, both, turned)
    stiff = jnp.where(row < column, both, jnp.where(row == column, diagonal, turned))
    m_ref[0] = gram
    m_ref[1] = stiff
    half = lax.broadcasted_iota(jnp.int32, (256, 128), 1) < 64
    gram_diagonal = jnp.sum(jnp.where(row == column, gram, 0.0), axis=1, keepdims=True)
    least = invert_factors(m_ref, jnp.where(half, gram_diagonal, diagonal[:, :128]))
    least_ref[...] = jnp.broadcast_to(least, (8, 128))
    lower = jnp.where(row >= column, m_ref[0], 0.0)
    stiff_lower = jnp.where(row >= column, m_ref[1], 0.0)
    parts = parts_of(rows_ref, 0)
    vectors = by_vector(parts)
    mixed = untucked(parts, mixed)
    other = parts_of(rows_ref, 3)
    subspace = dot(vectors.T, lower, ((1,), (1,)))
    subspace = subspace * jnp.sqrt(jnp.float32(DEVICES * 3 * NODES))
    projected_ref[...] = dot(lower, dot(stiff, lower, ((1,), (1,))))
    weights = dot(stiff_lower.T, dot(stiff_lower, lateral))
    weights = jnp.concatenate([weights, weights], axis=1)
    axial = by_vector([other[0], mixed[1], mixed[2]])
    bending = by_vector([mixed[0], other[1], other[2]])
    fields = [
        jnp.sum(value * weights, axis=0, keepdims=True) for value in (vectors, axial, bending)
    ]
    lane = lax.broadcasted_iota(jnp.int32, (24, 256), 1)
    group = lax.broadcasted_iota(jnp.int32, (24, 256), 0)
    laid = jnp.where((lane >> 3) == group, fields[0] * mass_ref[...], 0.0)
    column = lax.broadcasted_iota(jnp.int32, (256, 128), 0)
    place = lax.broadcasted_iota(jnp.int32, (256, 128), 1)
    force_ref[...] = dot(laid, jnp.where((column & 7) == place, 1.0, 0.0))[:, :8]
    columns = jnp.concatenate(
        [fields[1], fields[2], jnp.zeros((126, 256), jnp.float32)], axis=0
    ).T
    axial = jnp.broadcast_to(columns[:, 0:1], (256, 16))
    bending = jnp.broadcast_to(columns[:, 1:2], (256, 16))
    fiber = lax.broadcasted_iota(jnp.int32, (8, 16), 1).astype(jnp.float32)
    heights = (fiber + 0.5) / 16.0 - 0.5
    for direction in range(3):
        other = (direction + 1) % 3
        for x in range(2):
            for z in range(4):
                rows = slice(direction * 16 + x * 8, direction * 16 + x * 8 + 8)
                inner = x * 32 + z * 8
                one = direction * NODES + inner
                two = other * NODES + inner
                subspace_ref[rows, z, :] = subspace[one : one + 8]
                strain = axial[one : one + 8] + heights * bending[two : two + 8]
                stress_new_ref[rows, z, :] = stress_ref[rows, z, :] + modulus_ref[rows, z, :] * strain


def fiber_modulus(stiffness, yield_flags):
    own = jnp.stack([stiffness[d, d] for d in range(3)])[:, None]
    return own * jnp.where(yield_flags == 1, 0.05, 1.0)


def extended(block, first_dim):
    for place, axis in enumerate((GX, "gy", "gz")):
        dim = first_dim + place
        count = lax.axis_size(axis)
        forward = [(i, i + 1) for i in range(count - 1)]
        backward = [(target, source) for source, target in forward]
        last = block.shape[dim]
        low = lax.ppermute(lax.slice_in_dim(block, last - 1, last, axis=dim), axis, forward)
        high = lax.ppermute(lax.slice_in_dim(block, 0, 1, axis=dim), axis, backward)
        block = jnp.concatenate([low, block, high], axis=dim)
    return block


def neighbour(padded, leading, direction, sense):
    slicer = [slice(None)] * padded.ndim
    for position in range(3):
        slicer[leading + position] = slice(1, -1)
    slicer[leading + direction] = slice(2, None) if sense > 0 else slice(0, -2)
    return padded[tuple(slicer)]


def summed(square):
    rows = jnp.concatenate([square[:, :128], square[:, 128:]], axis=0)
    for axes, count, copies in ((("cy", "gy"), 32, 16), (("core", "gz"), 16, 32)):
        rows = jnp.sum(exchange(rows, axes, count).reshape(count, 16, 128), axis=0)
        rows = jnp.tile(rows, (copies, 1))
    rows = exchange(rows, ("cy", "gy"), 32)
    return jnp.concatenate([rows[:256], rows[256:]], axis=1)


def step_by_step(start_block, node_mass, ground_spring, stiffness, yield_flags, stress_old):
    share = jnp.mean(yield_flags.astype(jnp.float32), axis=1)
    tangent = stiffness * (1.0 - 0.9 * share)[:, None]
    padded = extended(tangent, 2)
    edges = [
        [0.5 * (tangent[d] + neighbour(padded, 2, d, sense)[d]) for d in range(3)]
        for sense in (1, -1)
    ]
    edge_total = sum(edges[0]) + sum(edges[1])
    diagonal = ground_spring + edge_total
    top = jnp.broadcast_to(jnp.max((diagonal + edge_total) / node_mass), (128, 128))
    for axes, count in ((("cy", "core"), 16), ("gy", 4), ("gz", 8)):
        top = jnp.broadcast_to(jnp.max(exchange(top, axes, count)), (128, 128))
    top = top[0, 0]
    middle = top * 9.0 / 16.0
    spread = top * 7.0 / 16.0

    def apply_k(field):
        around_field = extended(field, 1)
        result = diagonal[..., None] * field
        for d in range(3):
            for sense, weights in ((1, edges[0]), (-1, edges[1])):
                result = result - weights[d][..., None] * neighbour(around_field, 1, d, sense)
        return result

    def shifted(field):
        return (apply_k(field) / node_mass[..., None] - middle * field) / spread

    width = start_block.shape[-1]
    mass_rows = node_mass.reshape(-1)
    vectors = start_block
    for turn in range(ITERS):
        earlier, current = vectors, shifted(vectors)
        for repeat in range(DEGREE - 1):
            earlier, current = current, 2.0 * shifted(current) - earlier
        flat_rows = current.reshape(-1, width)
        gram = summed(dot(flat_rows.T, mass_rows[:, None] * flat_rows))
        factor = jnp.linalg.cholesky(gram)
        basis = lax.linalg.triangular_solve(factor, flat_rows.T, left_side=True, lower=True)
        vectors = basis.T.reshape(current.shape)
    image = apply_k(vectors).reshape(-1, width)
    projected = summed(dot(basis, image))
    lateral = dot(basis[:, :NODES], mass_rows[:NODES, None])
    lateral = summed(jnp.broadcast_to(lateral, (width, width)))[:, :1]
    factor = jnp.linalg.cholesky(projected)
    halfway = lax.linalg.triangular_solve(factor, lateral, left_side=True, lower=True)
    weights = lax.linalg.triangular_solve(
        factor, halfway, left_side=True, lower=True, transpose_a=True
    )
    displace = dot(weights.T, basis).reshape(node_mass.shape)
    padded = extended(displace, 1)
    axial = []
    bending = []
    for d in range(3):
        above = neighbour(padded, 1, d, 1)
        below = neighbour(padded, 1, d, -1)
        other = (d + 1) % 3
        axial.append(0.5 * (above[d] - below[d]))
        bending.append(above[other] - 2.0 * displace[other] + below[other])
    fibers = stress_old.shape[1]
    heights = ((jnp.arange(fibers).astype(jnp.float32) + 0.5) / fibers - 0.5)[:, None, None, None]
    strain = jnp.stack(axial)[:, None] + heights * jnp.stack(bending)[:, None]
    stress_new = stress_old + fiber_modulus(stiffness, yield_flags) * strain
    subspace = vectors * jnp.sqrt(jnp.float32(DEVICES * 3 * NODES))
    return subspace, projected, node_mass * displace, stress_new


def call(kernel, shape, scratch=(), smem=(), operands=()):
    return pl.pallas_call(
        kernel,
        out_shape=shape,
        in_specs=[
            pl.BlockSpec(memory_space=pltpu.SMEM if place in smem else pltpu.VMEM)
            for place in range(len(operands))
        ],
        out_specs=jax.tree.map(lambda _: pl.BlockSpec(memory_space=pltpu.VMEM), shape),
        scratch_shapes=list(scratch),
        compiler_params=pltpu.CompilerParams(vmem_limit_bytes=40 * 1024 * 1024),
    )(*operands)


def rows_of(count):
    return jax.ShapeDtypeStruct((count, 128), jnp.float32)


def exchange(rows, axes, devices):
    per_device = rows.shape[0] // devices
    if per_device % 8 == 0:
        blocks = rows.reshape(devices, per_device, 128)
    else:
        blocks = rows.reshape(devices, per_device, 1, 128)
    return lax.all_to_all(blocks, axes, 0, 0, tiled=True).reshape(rows.shape)


def chebyshev_nodes():
    count = TOTAL + 1
    angles = np.pi * (np.arange(count) + 0.5) / count
    plain = np.zeros((count, count))
    timesx = np.zeros((count + 1, count))
    for degree in range(count):
        plain[degree] = (2.0 if degree else 1.0) / count * np.cos(degree * angles)
        timesx[degree + 1] += plain[degree] * (0.5 if degree else 1.0)
        if degree:
            timesx[degree - 1] += plain[degree] * 0.5
    table = np.zeros((40, 128), np.float32)
    table[0, :count] = np.cos(angles)
    table[8 : 8 + count, :count] = plain
    table[24 : 25 + count, :count] = timesx
    return jnp.asarray(table)


def on_device(start_block, node_mass, ground_spring, stiffness, yield_flags, stress_old):
    width = start_block.shape[-1]
    fibers = stress_old.shape[1]

    def node_rows(value):
        return jnp.swapaxes(value, -1, -2).reshape(-1, 8)

    def fibers_last(value):
        return jnp.moveaxis(value, 1, -1).reshape(48, 4, fibers)

    grid_shape = (16, 4, 8, 128)
    plain = pltpu.VMEM(grid_shape, jnp.float32)
    grid = jax.ShapeDtypeStruct(grid_shape, jnp.float32)
    grids = jax.ShapeDtypeStruct((3,) + grid_shape, jnp.float32)
    sent = call(
        pack_kernel,
        rows_of(256 * OUT_ROWS),
        operands=(
            start_block.reshape(48, 4, width),
            node_rows(stiffness),
            jnp.concatenate([node_rows(node_mass), node_rows(ground_spring)], axis=0),
            fibers_last(yield_flags).reshape(3 * NODES, fibers),
        ),
    )
    own = exchange(sent, CHIPS, 256)
    other = lax.ppermute(own, "core", [(0, 1), (1, 0)])
    core = lax.axis_index("core").astype(jnp.int32).reshape(1)
    component = lax.axis_index("gy").astype(jnp.int32).reshape(1)
    *weights, own_top = call(
        weights_kernel,
        (grid, grids, grids, grid, grid, rows_of(32)),
        (plain,),
        smem=(0,),
        operands=(core, own, other),
    )
    tops = exchange(own_top, "gy", 4)
    terms = call(
        filter_kernel,
        jax.ShapeDtypeStruct((TOTAL + 3,) + grid_shape, jnp.float32),
        (plain,),
        operands=(*weights, own_top),
    )
    filtered = call(
        combine_kernel,
        rows_of(2048),
        (plain, plain),
        smem=(0,),
        operands=(component, terms, own_top, tops, chebyshev_nodes()),
    )
    returned = exchange(filtered, AXES, DEVICES)
    mass_row = node_rows(node_mass).reshape(1, 3 * NODES)
    mass_row = jnp.pad(mass_row, ((0, 0), (0, NODES)))
    products = call(product_kernel, rows_of(512), operands=(returned, mass_row))
    partial = call(
        functools.partial(total_kernel, 32, 16),
        rows_of(256),
        operands=(exchange(products, ("cy", "gy"), 32),),
    )
    totals = call(
        functools.partial(total_kernel, 16, 32),
        rows_of(512),
        operands=(exchange(partial, ("core", "gz"), 16),),
    )
    subspace, projected, force, stress_new, least = call(
        final_kernel,
        (
            jax.ShapeDtypeStruct((48, 4, width), jnp.float32),
            jax.ShapeDtypeStruct((width, width), jnp.float32),
            jax.ShapeDtypeStruct((24, 8), jnp.float32),
            jax.ShapeDtypeStruct((48, 4, fibers), jnp.float32),
            rows_of(8),
        ),
        (pltpu.VMEM((2, 256, 256), jnp.float32),),
        operands=(
            exchange(totals, ("cy", "gy"), 32),
            returned,
            mass_row,
            fibers_last(fiber_modulus(stiffness, yield_flags)),
            fibers_last(stress_old),
        ),
    )
    place = node_mass.shape[1:]
    force = jnp.swapaxes(force.reshape(3, place[0], place[2], place[1]), -1, -2)
    stress_new = jnp.moveaxis(stress_new.reshape((3,) + place + (fibers,)), -1, 1)
    return lax.cond(
        least[0, 0] > LEAST_PIVOT,
        lambda *operands: operands[:4],
        lambda *operands: step_by_step(*operands[4:]),
        subspace.reshape(start_block.shape),
        projected,
        force,
        stress_new,
        start_block,
        node_mass,
        ground_spring,
        stiffness,
        yield_flags,
        stress_old,
    )


def solution(mesh):
    chips = Mesh(mesh.devices.reshape(8, 2, 4, 8), AXES)
    return jax.shard_map(
        on_device,
        mesh=chips,
        in_specs=(
            P(None, GX, "gy", "gz", None),
            P(None, GX, "gy", "gz"),
            P(None, GX, "gy", "gz"),
            P(None, None, GX, "gy", "gz"),
            P(None, None, GX, "gy", "gz"),
            P(None, None, GX, "gy", "gz"),
        ),
        out_specs=(
            P(None, GX, "gy", "gz", None),
            P(),
            P(None, GX, "gy", "gz"),
            P(None, None, GX, "gy", "gz"),
        ),
        check_vma=False,
    )
```

```python
import functools

import jax
import jax.numpy as jnp
import numpy as np
from jax import lax
from jax.experimental import pallas as pl
from jax.experimental.pallas import tpu as pltpu
from jax.sharding import Mesh, PartitionSpec as P

DEGREE = 4
ITERS = 2
TOTAL = DEGREE * ITERS
PRECISE = lax.Precision.HIGHEST
GX = ("cy", "core")
AXES = ("cy", "core", "gy", "gz")
CHIPS = ("cy", "gy", "gz")

NODES = 64
DEVICES = 512
OUT_ROWS = 5
LEAST_PIVOT = 0.1
BLOCK = 32
CHUNK = 17
LEAST_PIVOT = 0.1
BLOCK = 32
STIFF_LANE = 9
MASS_LANE = 10


def dot(a, b, contract=((1,), (0,))):
    return lax.dot_general(
        a, b, (contract, ((), ())), precision=PRECISE, preferred_element_type=jnp.float32
    )


def spread_nodes(values, keep):
    groups = jnp.where(keep, values.reshape((-1,) + keep.shape), 0.0)
    return jnp.sum(groups, axis=1)


def pack_kernel(start_ref, stiffness_ref, node_ref, flags_ref, out_ref):
    lane = lax.broadcasted_iota(jnp.int32, (8, 128), 1)
    place = lax.broadcasted_iota(jnp.int32, (8, 128), 0)
    repeated = jnp.where((lane & 7) == place, 1.0, 0.0)
    keep = ((lane >> 3) & 7) == place
    stiffness = spread_nodes(dot(stiffness_ref[...], repeated), keep)
    nodes = spread_nodes(dot(node_ref[...], repeated), keep)
    counts = jnp.dot(
        flags_ref[...].astype(jnp.bfloat16),
        jnp.ones((16, 128), jnp.bfloat16),
        preferred_element_type=jnp.float32,
    )
    lane = lax.broadcasted_iota(jnp.int32, (NODES, 128), 1)
    place = lax.broadcasted_iota(jnp.int32, (NODES, 128), 0)
    own = ((place >> 5) * 32 + (place & 3) * 8 + ((place >> 2) & 7)) == (lane & 63)
    softening = 1.0 - 0.9 * (spread_nodes(counts, own) / 16.0)
    low = lax.broadcasted_iota(jnp.int32, (1, 128), 1) < 64
    for comp in range(4):
        source = comp % 3
        if comp < 3:
            block = jnp.concatenate(
                [
                    start_ref[comp * 16 + x * 8 : comp * 16 + x * 8 + 8, z, :]
                    for x in range(2)
                    for z in range(4)
                ],
                axis=0,
            )
            pairs = jnp.concatenate([block[:, :128], block[:, 128:]], axis=0).T
        else:
            pairs = jnp.zeros((128, 128), jnp.float32)
        tangent = [
            stiffness[3 * d + source : 3 * d + source + 1, :] * softening[d : d + 1, :]
            for d in range(3)
        ]
        mass = nodes[source : source + 1, :]
        spring = nodes[3 + source : 4 + source, :]
        rows = [
            jnp.broadcast_to(row, (8, 128))
            for row in (
                jnp.where(low, tangent[0], tangent[1]),
                jnp.where(low, tangent[2], mass),
                spring,
            )
        ]
        for cy in range(8):
            first = (cy * 4 + comp) * 8 * OUT_ROWS
            for core in range(2):
                at = (cy * 2 + core) * 8
                out_ref[pl.ds(first + core, 8, stride=OUT_ROWS), :] = pairs[at : at + 8]
            for r in range(3):
                out_ref[pl.ds(first + 2 + r, 8, stride=OUT_ROWS), :] = rows[r]


def iota(axis):
    return lax.broadcasted_iota(jnp.int32, (4, 8, 128), axis)


def grid_row(refs, kind, gx, core):
    rows = [ref[pl.ds(gx // 2 * 32 * OUT_ROWS + kind, 32, stride=OUT_ROWS), :] for ref in refs]
    return jnp.where(core == gx % 2, rows[0], rows[1]).reshape(4, 8, 128)


def roll(value, shift, axis=2):
    return pltpu.roll(value, shift, axis)


def both_halves(value):
    lane = iota(2)
    turned = roll(value, 64)
    return jnp.where(lane < 64, value, turned), jnp.where(lane < 64, turned, value)


class Turned:
    def __init__(self, ref):
        self.ref = ref
        self.planes = {}

    def at(self, gx):
        if gx not in self.planes:
            if gx in (-1, 16):
                zero = jnp.zeros((4, 8, 128), jnp.float32)
                self.planes[gx] = (zero, zero)
            else:
                here = self.ref[gx]
                self.planes[gx] = (roll(here, 96), roll(here, 32))
        return self.planes[gx]

    def sides(self, gx):
        first = (iota(2) & 32) == 0
        up = jnp.where(first, self.at(gx)[0], self.at(gx + 1)[1])
        down = jnp.where(first, self.at(gx - 1)[0], self.at(gx)[1])
        return up, down


def y_up(here):
    moved = jnp.concatenate([here[1:], jnp.zeros((1, 8, 128), jnp.float32)], axis=0)
    return jnp.where((iota(2) & 7) != 7, roll(here, 127), roll(moved, 7))


def y_down(here):
    moved = jnp.concatenate([jnp.zeros((1, 8, 128), jnp.float32), here[:-1]], axis=0)
    return jnp.where((iota(2) & 7) != 0, roll(here, 1), roll(moved, 121))


def z_up(here):
    other = jnp.where(iota(1) < 7, roll(roll(here, 24), 7, 1), 0.0)
    return jnp.where((iota(2) & 24) != 24, roll(here, 120), other)


def z_down(here):
    other = jnp.where(iota(1) > 0, roll(roll(here, 104), 1, 1), 0.0)
    return jnp.where((iota(2) & 24) != 0, roll(here, 8), other)


def around(ref, turned, gx):
    here = ref[gx]
    return here, (turned.sides(gx), (y_up(here), y_down(here)), (z_up(here), z_down(here)))


UP, DOWN, DIAGONAL, MASS, KINDS = 1, 4, 7, 8, 9


def weights_kernel(
    core_ref, own_ref, other_ref, held_ref, top_ref, tangent_ref
):
    core = core_ref[0]
    refs = (own_ref, other_ref)
    second = []
    for gx in range(16):
        held_ref[gx, 0] = grid_row(refs, core, gx, core)
        first, along_y = both_halves(grid_row(refs, 2, gx, core))
        tangent_ref[gx] = first
        second.append(along_y)
    turned = Turned(tangent_ref)
    best = jnp.zeros((4, 8, 128), jnp.float32)
    for gx in range(16):
        first = tangent_ref[gx]
        above, below = turned.sides(gx)
        third, mass = both_halves(grid_row(refs, 3, gx, core))
        spring = grid_row(refs, 4, gx, core)
        ups = [
            0.5 * (first + above),
            0.5 * (second[gx] + y_up(second[gx])),
            0.5 * (third + z_up(third)),
        ]
        downs = [
            0.5 * (first + below),
            0.5 * (second[gx] + y_down(second[gx])),
            0.5 * (third + z_down(third)),
        ]
        total = (ups[0] + ups[1] + ups[2]) + (downs[0] + downs[1] + downs[2])
        for direction in range(3):
            held_ref[gx, UP + direction] = ups[direction]
            held_ref[gx, DOWN + direction] = downs[direction]
        diagonal = spring + total
        held_ref[gx, DIAGONAL] = diagonal
        held_ref[gx, MASS] = mass
        best = jnp.maximum(best, (diagonal + total) / mass)
    best = jnp.max(jnp.max(best, axis=0), axis=(0, 1), keepdims=True)
    top_ref[...] = jnp.broadcast_to(best, (32, 128))


def filter_kernel(held_ref, top_ref, terms_ref, inverse_ref):
    top = top_ref[0:1, :]
    inverse_spread = 1.0 / (top * 7.0 / 16.0)
    ratio = (top * 9.0 / 16.0) * inverse_spread
    for gx in range(16):
        mass = held_ref[gx, MASS]
        inverse_ref[gx] = inverse_spread / mass
        terms_ref[0, gx] = held_ref[gx, 0]
        terms_ref[TOTAL + 2, gx] = mass
    for degree in range(1, TOTAL + 2):
        current_ref = terms_ref.at[degree - 1]
        turned = Turned(current_ref)
        for gx in range(16):
            here, sides = around(current_ref, turned, gx)
            image = held_ref[gx, DIAGONAL] * here
            for direction in range(3):
                image = image - held_ref[gx, UP + direction] * sides[direction][0]
                image = image - held_ref[gx, DOWN + direction] * sides[direction][1]
            image = image * inverse_ref[gx] - ratio * here
            if degree > 1:
                image = 2.0 * image - terms_ref[degree - 2, gx]
            terms_ref[degree, gx] = image


def combine_kernel(terms_ref, own_top_ref, top_ref, nodes_ref, out_ref):
    top = jnp.max(jnp.max(top_ref[...], axis=0, keepdims=True), axis=1, keepdims=True)
    own_top = own_top_ref[0:1, :]
    part = own_top / top
    place = part * nodes_ref[0:1, :] + (part - 1.0) * (9.0 / 7.0)
    square = place * place
    once = 8.0 * square * square - 8.0 * square + 1.0
    coefficients = jnp.sum(nodes_ref[8:40, :] * (once * once), axis=1, keepdims=True)
    middle = own_top * 9.0 / 16.0
    spread = own_top * 7.0 / 16.0
    for gx in range(16):
        total = coefficients[0:1, :] * terms_ref[0, gx]
        scaled = coefficients[16:17, :] * terms_ref[0, gx]
        for degree in range(1, TOTAL + 2):
            term = terms_ref[degree, gx]
            if degree <= TOTAL:
                total = total + coefficients[degree : degree + 1, :] * term
            scaled = scaled + coefficients[16 + degree : 17 + degree, :] * term
        image = terms_ref[TOTAL + 2, gx] * (middle * total + spread * scaled)
        out_ref[pl.ds(gx * 64, 32, stride=2), :] = total.reshape(32, 128)
        out_ref[pl.ds(gx * 64 + 1, 32, stride=2), :] = image.reshape(32, 128)


def parts_of(rows_ref, kind):
    return [
        jnp.concatenate(
            [rows_ref[pl.ds((gx * 4 + comp) * 16 + kind, 8, stride=2), :] for gx in range(16)],
            axis=0,
        )
        for comp in range(3)
    ]


def pair_rows(one, two):
    low = lax.broadcasted_iota(jnp.int32, (128, 128), 1) < 64
    upper = jnp.where(low, one, 0.0 if two is None else pltpu.roll(two, 64, 1))
    lower = jnp.where(low, pltpu.roll(one, 64, 1), 0.0 if two is None else two)
    return jnp.concatenate([upper, lower], axis=0)


def by_vector(parts):
    return jnp.concatenate(
        [pair_rows(parts[0], parts[1]), pair_rows(parts[2], None)], axis=1
    )


def product_kernel(rows_ref, mass_ref, out_ref, along_x_ref, along_y_ref, along_z_ref):
    parts = parts_of(rows_ref, 0)
    vectors = by_vector(parts)
    along_x_ref[...] = vectors[:, :128]
    along_y_ref[...] = pair_rows(parts[1], parts[2])
    along_z_ref[...] = pair_rows(parts[2], parts[0])
    image = by_vector(parts_of(rows_ref, 1))
    weighted = vectors * mass_ref[...]
    gram = dot(weighted, vectors, ((1,), (1,)))
    stiff = dot(vectors, image, ((1,), (1,)))
    row = lax.broadcasted_iota(jnp.int32, (256, 256), 0)
    column = lax.broadcasted_iota(jnp.int32, (256, 256), 1)
    both = jnp.where(row >= column, gram, stiff)
    diagonal = jnp.sum(vectors * image, axis=1, keepdims=True)
    lane = lax.broadcasted_iota(jnp.int32, (256, 128), 1)
    lateral = jnp.sum(jnp.where(lane < NODES, weighted[:, :128], 0.0), axis=1, keepdims=True)
    further = jnp.where(lane == 0, diagonal, jnp.where(lane == 1, lateral, 0.0)).T
    for chunk in range(32):
        half = slice(0, 128) if chunk < 16 else slice(128, 256)
        first = chunk % 16 * 16
        out_ref[chunk * CHUNK : chunk * CHUNK + 16, :] = both[first : first + 16, half]
        last = further[chunk // 2 : chunk // 2 + 1, chunk % 2 * 128 : chunk % 2 * 128 + 128]
        out_ref[chunk * CHUNK + 16 : chunk * CHUNK + 17, :] = last


def total_kernel(count, copies, rows_ref, out_ref):
    total = rows_ref[0:CHUNK, :]
    for place in range(1, count):
        total = total + rows_ref[place * CHUNK : place * CHUNK + CHUNK, :]
    for place in range(copies):
        out_ref[place * CHUNK : place * CHUNK + CHUNK, :] = total


def factor_block(gram, stiff):
    lane = lax.broadcasted_iota(jnp.int32, (BLOCK, 128), 1)
    row = lax.broadcasted_iota(jnp.int32, (BLOCK, 128), 0)
    low = lane < 64
    columns = [
        jnp.where(
            low,
            jnp.broadcast_to(gram[:, j : j + 1], (BLOCK, 128)),
            jnp.broadcast_to(stiff[:, j : j + 1], (BLOCK, 128)),
        )
        for j in range(BLOCK)
    ]
    inverse = jnp.where((lane & 63) == row, 1.0, 0.0)
    scale = jnp.ones((BLOCK, 128), jnp.float32)
    link = jnp.zeros((BLOCK, 128), jnp.float32)
    for k in range(0, BLOCK, 2):
        one, two = columns[k], columns[k + 1]
        top = one[k : k + 1, :]
        side = one[k + 1 : k + 2, :]
        corner = two[k + 1 : k + 2, :]
        rest = top * corner - side * side
        scale = jnp.where(row == k, top, jnp.where(row == k + 1, rest / top, scale))
        link = jnp.where(row == k + 1, side / top, link)
        if k + 2 == BLOCK:
            break
        part = (k + 2) // 8 * 8
        factor = 1.0 / rest
        below = row[part:] > k + 1
        first = jnp.where(below, (one[part:] * corner - two[part:] * side) * factor, 0.0)
        second = jnp.where(below, (two[part:] * top - one[part:] * side) * factor, 0.0)

        def reduced(value):
            tail = value[part:] - (first * value[k : k + 1, :] + second * value[k + 1 : k + 2, :])
            return tail if part == 0 else jnp.concatenate([value[:part], tail], axis=0)

        for j in range(k + 2, BLOCK):
            columns[j] = reduced(columns[j])
        inverse = reduced(inverse)
    inverse = inverse - link * pltpu.roll(inverse, 1, 0)
    return inverse * lax.rsqrt(scale), scale


def rounded(value):
    return value.astype(jnp.bfloat16).astype(jnp.float32)


def three_parts(value):
    high = rounded(value)
    rest = value - high
    middle = rounded(rest)
    return high, middle, rest - middle


def four_copies(value):
    value = value + pltpu.roll(value, 32, 1)
    return value + pltpu.roll(value, 64, 1)


def left_groups(first, second):
    group = lax.broadcasted_iota(jnp.int32, first.shape, 1) // BLOCK
    high, middle, _ = three_parts(first)
    parts = three_parts(second)
    one = jnp.where(group < 2, high, middle)
    two = jnp.where(group == 0, parts[0], jnp.where(group == 1, parts[2], 0.0))
    return jnp.concatenate([one, two], axis=1).astype(jnp.bfloat16)


def right_lanes(copies):
    group = lax.broadcasted_iota(jnp.int32, copies.shape, 1) // BLOCK
    high, middle, low = three_parts(copies)
    one = jnp.where(group % 2 == 0, high, middle)
    two = jnp.where(group == 0, low, high)
    return jnp.concatenate([one, two], axis=1).astype(jnp.bfloat16)


def right_rows(value):
    high, middle, low = [part.astype(jnp.bfloat16) for part in three_parts(value)]
    return jnp.concatenate([high, middle, high, middle, low, high, high, high], axis=0)


def product(left, right, contract):
    return lax.dot_general(
        left, right, (contract, ((), ())), preferred_element_type=jnp.float32
    )


def invert_factors(m_ref, diagonal):
    lane = lax.broadcasted_iota(jnp.int32, (BLOCK, 128), 1)
    least = jnp.ones((BLOCK, 128), jnp.float32)
    for first in range(0, 256, BLOCK):
        tile = first // 128 * 128
        inside = first - tile
        after = first + BLOCK
        small = [m_ref[m, first:after, tile : tile + 128][:, inside : inside + BLOCK] for m in (0, 1)]
        inverse, pivots = factor_block(small[0], small[1])
        least = jnp.minimum(least, pivots / diagonal[first:after, :])
        for m in (0, 1):
            own = four_copies(
                jnp.where((lane >= 64 * m) & (lane < 64 * m + BLOCK), inverse, 0.0)
            )
            row = lax.broadcasted_iota(jnp.int32, (BLOCK, 256), 0)
            column = lax.broadcasted_iota(jnp.int32, (BLOCK, 256), 1) - first
            rows = m_ref[m, first:after, :]
            unit = jnp.where(column == row, 1.0, 0.0)
            rows = jnp.where((column >= 0) & (column < BLOCK), unit, rows)
            result = product(left_groups(own, own), right_rows(rows), ((1,), (0,)))
            m_ref[m, first:after, :] = result
            if after < 256:
                count = 256 - after
                lanes = lax.broadcasted_iota(jnp.int32, (count, 128), 1)
                held = (lanes >= inside) & (lanes < inside + BLOCK)
                left = four_copies(jnp.where(held, m_ref[m, after:, tile : tile + 128], 0.0))
                right = jnp.concatenate([right_lanes(own)] * 8, axis=0)
                factor = product(left_groups(left, left), right, ((1,), (1,)))
                column = lax.broadcasted_iota(jnp.int32, (count, 256), 1)
                rows = m_ref[m, after:, :]
                rows = jnp.where((column >= first) & (column < after), 0.0, rows)
                m_ref[m, after:, :] = rows - product(
                    left_groups(factor[:, :128], factor[:, 128:]), right_rows(result), ((1,), (0,))
                )
    return jnp.min(least, axis=(0, 1), keepdims=True)


def final_kernel(
    sums_ref, rows_ref, above_x_ref, below_x_ref, above_y_ref, below_y_ref, above_z_ref,
    below_z_ref, mass_ref, modulus_ref, stress_ref, subspace_ref, projected_ref, force_ref,
    stress_new_ref, least_ref, m_ref
):
    chunks = [sums_ref[chunk * CHUNK : chunk * CHUNK + 16, :] for chunk in range(32)]
    both = jnp.concatenate(
        [jnp.concatenate(chunks[:16], axis=0), jnp.concatenate(chunks[16:], axis=0)], axis=1
    )
    further = [
        jnp.broadcast_to(sums_ref[chunk * CHUNK + 16 : chunk * CHUNK + 17, :], (128, 128)).T
        for chunk in range(4)
    ]
    diagonal = jnp.concatenate(further[:2], axis=0)
    diagonal = jnp.concatenate([diagonal, diagonal], axis=1)
    lateral = jnp.concatenate(further[2:], axis=0)
    turned = both.T
    row = lax.broadcasted_iota(jnp.int32, (256, 256), 0)
    column = lax.broadcasted_iota(jnp.int32, (256, 256), 1)
    gram = jnp.where(row >= column, both, turned)
    stiff = jnp.where(row < column, both, jnp.where(row == column, diagonal, turned))
    m_ref[0] = gram
    m_ref[1] = stiff
    half = lax.broadcasted_iota(jnp.int32, (256, 128), 1) < 64
    gram_diagonal = jnp.sum(jnp.where(row == column, gram, 0.0), axis=1, keepdims=True)
    least = invert_factors(m_ref, jnp.where(half, gram_diagonal, diagonal[:, :128]))
    least_ref[...] = jnp.broadcast_to(least, (8, 128))
    lower = jnp.where(row >= column, m_ref[0], 0.0)
    stiff_lower = jnp.where(row >= column, m_ref[1], 0.0)
    vectors = by_vector(parts_of(rows_ref, 0))
    subspace = dot(vectors.T, lower, ((1,), (1,)))
    subspace = subspace * jnp.sqrt(jnp.float32(DEVICES * 3 * NODES))
    projected_ref[...] = dot(lower, dot(stiff, lower, ((1,), (1,))))
    weights = dot(stiff_lower.T, dot(stiff_lower, lateral))
    weights = jnp.concatenate([weights, weights], axis=1)
    displace = jnp.sum(vectors * weights, axis=0, keepdims=True)
    own = [displace[:, :128], pltpu.roll(displace[:, :128], 64, 1), displace[:, 128:]]
    outside = [
        jnp.sum(ref[...] * weights[:, :128], axis=0, keepdims=True)
        for ref in (above_x_ref, below_x_ref, above_y_ref, below_y_ref, above_z_ref, below_z_ref)
    ]
    lane = lax.broadcasted_iota(jnp.int32, (1, 128), 1)
    axial = []
    bending = []
    for direction, (step, mask) in enumerate(((32, 32), (1, 7), (8, 24))):
        wide = jnp.where(lane < 64, own[direction], pltpu.roll(own[(direction + 1) % 3], 64, 1))
        above = jnp.where(
            (lane & mask) == mask,
            pltpu.roll(outside[2 * direction], mask, 1),
            pltpu.roll(wide, 128 - step, 1),
        )
        below = jnp.where(
            (lane & mask) == 0,
            pltpu.roll(outside[2 * direction + 1], 128 - mask, 1),
            pltpu.roll(wide, step, 1),
        )
        axial.append(0.5 * (above - below))
        bending.append(pltpu.roll((above - 2.0 * wide) + below, 64, 1))
    lane = lax.broadcasted_iota(jnp.int32, (24, 256), 1)
    group = lax.broadcasted_iota(jnp.int32, (24, 256), 0)
    laid = jnp.where((lane >> 3) == group, displace * mass_ref[...], 0.0)
    column = lax.broadcasted_iota(jnp.int32, (256, 128), 0)
    place = lax.broadcasted_iota(jnp.int32, (256, 128), 1)
    force_ref[...] = dot(laid, jnp.where((column & 7) == place, 1.0, 0.0))[:, :8]
    columns = jnp.concatenate(
        axial + bending + [jnp.zeros((122, 128), jnp.float32)], axis=0
    ).T
    axial = [jnp.broadcast_to(columns[:, d : d + 1], (128, 16)) for d in range(3)]
    bending = [jnp.broadcast_to(columns[:, 3 + d : 4 + d], (128, 16)) for d in range(3)]
    fiber = lax.broadcasted_iota(jnp.int32, (8, 16), 1).astype(jnp.float32)
    heights = (fiber + 0.5) / 16.0 - 0.5
    for direction in range(3):
        for x in range(2):
            for z in range(4):
                rows = slice(direction * 16 + x * 8, direction * 16 + x * 8 + 8)
                inner = x * 32 + z * 8
                one = direction * NODES + inner
                subspace_ref[rows, z, :] = subspace[one : one + 8]
                strain = axial[direction][inner : inner + 8]
                strain = strain + heights * bending[direction][inner : inner + 8]
                stress_new_ref[rows, z, :] = stress_ref[rows, z, :] + modulus_ref[rows, z, :] * strain


def fiber_modulus(stiffness, yield_flags):
    own = jnp.stack([stiffness[d, d] for d in range(3)])[:, None]
    return own * jnp.where(yield_flags == 1, 0.05, 1.0)


def extended(block, first_dim):
    for place, axis in enumerate((GX, "gy", "gz")):
        dim = first_dim + place
        count = lax.axis_size(axis)
        forward = [(i, i + 1) for i in range(count - 1)]
        backward = [(target, source) for source, target in forward]
        last = block.shape[dim]
        low = lax.ppermute(lax.slice_in_dim(block, last - 1, last, axis=dim), axis, forward)
        high = lax.ppermute(lax.slice_in_dim(block, 0, 1, axis=dim), axis, backward)
        block = jnp.concatenate([low, block, high], axis=dim)
    return block


def neighbour(padded, leading, direction, sense):
    slicer = [slice(None)] * padded.ndim
    for position in range(3):
        slicer[leading + position] = slice(1, -1)
    slicer[leading + direction] = slice(2, None) if sense > 0 else slice(0, -2)
    return padded[tuple(slicer)]


def summed(square):
    rows = jnp.concatenate([square[:, :128], square[:, 128:]], axis=0)
    for axes, count, copies in ((("cy", "gy"), 32, 16), (("core", "gz"), 16, 32)):
        rows = jnp.sum(exchange(rows, axes, count).reshape(count, 16, 128), axis=0)
        rows = jnp.tile(rows, (copies, 1))
    rows = exchange(rows, ("cy", "gy"), 32)
    return jnp.concatenate([rows[:256], rows[256:]], axis=1)


def step_by_step(start_block, node_mass, ground_spring, stiffness, yield_flags, stress_old):
    share = jnp.mean(yield_flags.astype(jnp.float32), axis=1)
    tangent = stiffness * (1.0 - 0.9 * share)[:, None]
    padded = extended(tangent, 2)
    edges = [
        [0.5 * (tangent[d] + neighbour(padded, 2, d, sense)[d]) for d in range(3)]
        for sense in (1, -1)
    ]
    edge_total = sum(edges[0]) + sum(edges[1])
    diagonal = ground_spring + edge_total
    top = jnp.broadcast_to(jnp.max((diagonal + edge_total) / node_mass), (128, 128))
    for axes, count in ((("cy", "core"), 16), ("gy", 4), ("gz", 8)):
        top = jnp.broadcast_to(jnp.max(exchange(top, axes, count)), (128, 128))
    top = top[0, 0]
    middle = top * 9.0 / 16.0
    spread = top * 7.0 / 16.0

    def apply_k(field):
        around_field = extended(field, 1)
        result = diagonal[..., None] * field
        for d in range(3):
            for sense, weights in ((1, edges[0]), (-1, edges[1])):
                result = result - weights[d][..., None] * neighbour(around_field, 1, d, sense)
        return result

    def shifted(field):
        return (apply_k(field) / node_mass[..., None] - middle * field) / spread

    width = start_block.shape[-1]
    mass_rows = node_mass.reshape(-1)
    vectors = start_block
    for turn in range(ITERS):
        earlier, current = vectors, shifted(vectors)
        for repeat in range(DEGREE - 1):
            earlier, current = current, 2.0 * shifted(current) - earlier
        flat_rows = current.reshape(-1, width)
        gram = summed(dot(flat_rows.T, mass_rows[:, None] * flat_rows))
        factor = jnp.linalg.cholesky(gram)
        basis = lax.linalg.triangular_solve(factor, flat_rows.T, left_side=True, lower=True)
        vectors = basis.T.reshape(current.shape)
    image = apply_k(vectors).reshape(-1, width)
    projected = summed(dot(basis, image))
    lateral = dot(basis[:, :NODES], mass_rows[:NODES, None])
    lateral = summed(jnp.broadcast_to(lateral, (width, width)))[:, :1]
    factor = jnp.linalg.cholesky(projected)
    halfway = lax.linalg.triangular_solve(factor, lateral, left_side=True, lower=True)
    weights = lax.linalg.triangular_solve(
        factor, halfway, left_side=True, lower=True, transpose_a=True
    )
    displace = dot(weights.T, basis).reshape(node_mass.shape)
    padded = extended(displace, 1)
    axial = []
    bending = []
    for d in range(3):
        above = neighbour(padded, 1, d, 1)
        below = neighbour(padded, 1, d, -1)
        other = (d + 1) % 3
        axial.append(0.5 * (above[d] - below[d]))
        bending.append(above[other] - 2.0 * displace[other] + below[other])
    fibers = stress_old.shape[1]
    heights = ((jnp.arange(fibers).astype(jnp.float32) + 0.5) / fibers - 0.5)[:, None, None, None]
    strain = jnp.stack(axial)[:, None] + heights * jnp.stack(bending)[:, None]
    stress_new = stress_old + fiber_modulus(stiffness, yield_flags) * strain
    subspace = vectors * jnp.sqrt(jnp.float32(DEVICES * 3 * NODES))
    return subspace, projected, node_mass * displace, stress_new


def call(kernel, shape, scratch=(), smem=(), operands=()):
    return pl.pallas_call(
        kernel,
        out_shape=shape,
        in_specs=[
            pl.BlockSpec(memory_space=pltpu.SMEM if place in smem else pltpu.VMEM)
            for place in range(len(operands))
        ],
        out_specs=jax.tree.map(lambda _: pl.BlockSpec(memory_space=pltpu.VMEM), shape),
        scratch_shapes=list(scratch),
        compiler_params=pltpu.CompilerParams(vmem_limit_bytes=40 * 1024 * 1024),
    )(*operands)


def rows_of(count):
    return jax.ShapeDtypeStruct((count, 128), jnp.float32)


def exchange(rows, axes, devices):
    per_device = rows.shape[0] // devices
    if per_device % 8 == 0:
        blocks = rows.reshape(devices, per_device, 128)
    else:
        blocks = rows.reshape(devices, per_device, 1, 128)
    return lax.all_to_all(blocks, axes, 0, 0, tiled=True).reshape(rows.shape)


def chebyshev_nodes():
    count = TOTAL + 1
    angles = np.pi * (np.arange(count) + 0.5) / count
    plain = np.zeros((count, count))
    timesx = np.zeros((count + 1, count))
    for degree in range(count):
        plain[degree] = (2.0 if degree else 1.0) / count * np.cos(degree * angles)
        timesx[degree + 1] += plain[degree] * (0.5 if degree else 1.0)
        if degree:
            timesx[degree - 1] += plain[degree] * 0.5
    table = np.zeros((40, 128), np.float32)
    table[0, :count] = np.cos(angles)
    table[8 : 8 + count, :count] = plain
    table[24 : 25 + count, :count] = timesx
    return jnp.asarray(table)


def on_device(start_block, node_mass, ground_spring, stiffness, yield_flags, stress_old):
    width = start_block.shape[-1]
    fibers = stress_old.shape[1]

    def node_rows(value):
        return jnp.swapaxes(value, -1, -2).reshape(-1, 8)

    def fibers_last(value):
        return jnp.moveaxis(value, 1, -1).reshape(48, 4, fibers)

    grid_shape = (16, 4, 8, 128)
    plain = pltpu.VMEM(grid_shape, jnp.float32)
    planes_shape = (16, KINDS, 4, 8, 128)
    sent = call(
        pack_kernel,
        rows_of(256 * OUT_ROWS),
        operands=(
            start_block.reshape(48, 4, width),
            node_rows(stiffness),
            jnp.concatenate([node_rows(node_mass), node_rows(ground_spring)], axis=0),
            fibers_last(yield_flags).reshape(3 * NODES, fibers),
        ),
    )
    own = exchange(sent, CHIPS, 256)
    other = lax.ppermute(own, "core", [(0, 1), (1, 0)])
    core = lax.axis_index("core").astype(jnp.int32).reshape(1)
    planes, own_top = call(
        weights_kernel,
        (jax.ShapeDtypeStruct(planes_shape, jnp.float32), rows_of(32)),
        (plain,),
        smem=(0,),
        operands=(core, own, other),
    )
    tops = exchange(own_top, "gy", 4)
    terms = call(
        filter_kernel,
        jax.ShapeDtypeStruct((TOTAL + 3,) + grid_shape, jnp.float32),
        (plain,),
        operands=(planes, own_top),
    )
    filtered = call(
        combine_kernel,
        rows_of(1024),
        operands=(terms, own_top, tops, chebyshev_nodes()),
    )
    returned = exchange(filtered, AXES, DEVICES)
    mass_row = node_rows(node_mass).reshape(1, 3 * NODES)
    mass_row = jnp.pad(mass_row, ((0, 0), (0, NODES)))
    along = jax.ShapeDtypeStruct((width, 128), jnp.float32)
    products, *along = call(
        product_kernel,
        (rows_of(32 * CHUNK), along, along, along),
        operands=(returned, mass_row),
    )
    neighbours = []
    for axis, mine in zip((GX, "gy", "gz"), along):
        count = lax.axis_size(axis)
        forward = [(i, i + 1) for i in range(count - 1)]
        backward = [(target, source) for source, target in forward]
        neighbours.append(lax.ppermute(mine, axis, backward))
        neighbours.append(lax.ppermute(mine, axis, forward))
    part = exchange(products, ("cy", "gy"), 32)
    part, *neighbours[:4] = lax.optimization_barrier((part, *neighbours[:4]))
    part = call(functools.partial(total_kernel, 32, 16), rows_of(16 * CHUNK), operands=(part,))
    part = exchange(part, ("core", "gz"), 16)
    part, *neighbours[4:] = lax.optimization_barrier((part, *neighbours[4:]))
    totals = call(functools.partial(total_kernel, 16, 32), rows_of(32 * CHUNK), operands=(part,))
    subspace, projected, force, stress_new, least = call(
        final_kernel,
        (
            jax.ShapeDtypeStruct((48, 4, width), jnp.float32),
            jax.ShapeDtypeStruct((width, width), jnp.float32),
            jax.ShapeDtypeStruct((24, 8), jnp.float32),
            jax.ShapeDtypeStruct((48, 4, fibers), jnp.float32),
            rows_of(8),
        ),
        (pltpu.VMEM((2, 256, 256), jnp.float32),),
        operands=(
            exchange(totals, ("cy", "gy"), 32),
            returned,
            *neighbours,
            mass_row,
            fibers_last(fiber_modulus(stiffness, yield_flags)),
            fibers_last(stress_old),
        ),
    )
    place = node_mass.shape[1:]
    force = jnp.swapaxes(force.reshape(3, place[0], place[2], place[1]), -1, -2)
    stress_new = jnp.moveaxis(stress_new.reshape((3,) + place + (fibers,)), -1, 1)
    return lax.cond(
        least[0, 0] > LEAST_PIVOT,
        lambda *operands: operands[:4],
        lambda *operands: step_by_step(*operands[4:]),
        subspace.reshape(start_block.shape),
        projected,
        force,
        stress_new,
        start_block,
        node_mass,
        ground_spring,
        stiffness,
        yield_flags,
        stress_old,
    )


def solution(mesh):
    chips = Mesh(mesh.devices.reshape(8, 2, 4, 8), AXES)
    return jax.shard_map(
        on_device,
        mesh=chips,
        in_specs=(
            P(None, GX, "gy", "gz", None),
            P(None, GX, "gy", "gz"),
            P(None, GX, "gy", "gz"),
            P(None, None, GX, "gy", "gz"),
            P(None, None, GX, "gy", "gz"),
            P(None, None, GX, "gy", "gz"),
        ),
        out_specs=(
            P(None, GX, "gy", "gz", None),
            P(),
            P(None, GX, "gy", "gz"),
            P(None, None, GX, "gy", "gz"),
        ),
        check_vma=False,
    )
```

```python
import functools

import jax
import jax.numpy as jnp
import numpy as np
from jax import lax
from jax.experimental import pallas as pl
from jax.experimental.pallas import tpu as pltpu
from jax.sharding import Mesh, PartitionSpec as P

DEGREE = 4
ITERS = 2
TOTAL = DEGREE * ITERS
PRECISE = lax.Precision.HIGHEST
GX = ("cy", "core")
AXES = ("cy", "core", "gy", "gz")
CHIPS = ("cy", "gy", "gz")

NODES = 64
DEVICES = 512
OUT_ROWS = 5
LEAST_PIVOT = 0.1
BLOCK = 32
CHUNK = 17
LEAST_PIVOT = 0.1
BLOCK = 32
STIFF_LANE = 9
MASS_LANE = 10


def dot(a, b, contract=((1,), (0,))):
    return lax.dot_general(
        a, b, (contract, ((), ())), precision=PRECISE, preferred_element_type=jnp.float32
    )


def spread_nodes(values, keep):
    groups = jnp.where(keep, values.reshape((-1,) + keep.shape), 0.0)
    return jnp.sum(groups, axis=1)


def pack_kernel(start_ref, stiffness_ref, node_ref, flags_ref, out_ref):
    lane = lax.broadcasted_iota(jnp.int32, (8, 128), 1)
    place = lax.broadcasted_iota(jnp.int32, (8, 128), 0)
    repeated = jnp.where((lane & 7) == place, 1.0, 0.0)
    keep = ((lane >> 3) & 7) == place
    stiffness = spread_nodes(dot(stiffness_ref[...], repeated), keep)
    nodes = spread_nodes(dot(node_ref[...], repeated), keep)
    counts = jnp.dot(
        flags_ref[...].astype(jnp.bfloat16),
        jnp.ones((16, 128), jnp.bfloat16),
        preferred_element_type=jnp.float32,
    )
    lane = lax.broadcasted_iota(jnp.int32, (NODES, 128), 1)
    place = lax.broadcasted_iota(jnp.int32, (NODES, 128), 0)
    own = ((place >> 5) * 32 + (place & 3) * 8 + ((place >> 2) & 7)) == (lane & 63)
    softening = 1.0 - 0.9 * (spread_nodes(counts, own) / 16.0)
    low = lax.broadcasted_iota(jnp.int32, (1, 128), 1) < 64
    for comp in range(4):
        source = comp % 3
        if comp < 3:
            block = jnp.concatenate(
                [
                    start_ref[comp * 16 + x * 8 : comp * 16 + x * 8 + 8, z, :]
                    for x in range(2)
                    for z in range(4)
                ],
                axis=0,
            )
            pairs = jnp.concatenate([block[:, :128], block[:, 128:]], axis=0).T
        else:
            pairs = jnp.zeros((128, 128), jnp.float32)
        tangent = [
            stiffness[3 * d + source : 3 * d + source + 1, :] * softening[d : d + 1, :]
            for d in range(3)
        ]
        mass = nodes[source : source + 1, :]
        spring = nodes[3 + source : 4 + source, :]
        rows = [
            jnp.broadcast_to(row, (8, 128))
            for row in (
                jnp.where(low, tangent[0], tangent[1]),
                jnp.where(low, tangent[2], mass),
                spring,
            )
        ]
        for cy in range(8):
            first = (cy * 4 + comp) * 8 * OUT_ROWS
            for core in range(2):
                at = (cy * 2 + core) * 8
                out_ref[pl.ds(first + core, 8, stride=OUT_ROWS), :] = pairs[at : at + 8]
            for r in range(3):
                out_ref[pl.ds(first + 2 + r, 8, stride=OUT_ROWS), :] = rows[r]


def iota(axis):
    return lax.broadcasted_iota(jnp.int32, (4, 8, 128), axis)


def grid_row(refs, kind, gx, core):
    rows = [ref[pl.ds(gx // 2 * 32 * OUT_ROWS + kind, 32, stride=OUT_ROWS), :] for ref in refs]
    return jnp.where(core == gx % 2, rows[0], rows[1]).reshape(4, 8, 128)


def roll(value, shift, axis=2):
    return pltpu.roll(value, shift, axis)


def both_halves(value):
    lane = iota(2)
    turned = roll(value, 64)
    return jnp.where(lane < 64, value, turned), jnp.where(lane < 64, turned, value)


class Turned:
    def __init__(self, ref):
        self.ref = ref
        self.planes = {}

    def at(self, gx):
        if gx not in self.planes:
            if gx in (-1, 16):
                zero = jnp.zeros((4, 8, 128), jnp.float32)
                self.planes[gx] = (zero, zero)
            else:
                here = self.ref[gx]
                self.planes[gx] = (roll(here, 96), roll(here, 32))
        return self.planes[gx]

    def sides(self, gx):
        first = (iota(2) & 32) == 0
        up = jnp.where(first, self.at(gx)[0], self.at(gx + 1)[1])
        down = jnp.where(first, self.at(gx - 1)[0], self.at(gx)[1])
        return up, down


def y_up(here):
    moved = jnp.concatenate([here[1:], jnp.zeros((1, 8, 128), jnp.float32)], axis=0)
    return jnp.where((iota(2) & 7) != 7, roll(here, 127), roll(moved, 7))


def y_down(here):
    moved = jnp.concatenate([jnp.zeros((1, 8, 128), jnp.float32), here[:-1]], axis=0)
    return jnp.where((iota(2) & 7) != 0, roll(here, 1), roll(moved, 121))


def z_up(here):
    other = jnp.where(iota(1) < 7, roll(roll(here, 24), 7, 1), 0.0)
    return jnp.where((iota(2) & 24) != 24, roll(here, 120), other)


def z_down(here):
    other = jnp.where(iota(1) > 0, roll(roll(here, 104), 1, 1), 0.0)
    return jnp.where((iota(2) & 24) != 0, roll(here, 8), other)


def around(ref, turned, gx):
    here = ref[gx]
    return here, (turned.sides(gx), (y_up(here), y_down(here)), (z_up(here), z_down(here)))


UP, DOWN, DIAGONAL, MASS, KINDS = 1, 4, 7, 8, 9


def weights_kernel(
    core_ref, own_ref, other_ref, held_ref, top_ref, tangent_ref
):
    core = core_ref[0]
    refs = (own_ref, other_ref)
    second = []
    for gx in range(16):
        held_ref[gx, 0] = grid_row(refs, core, gx, core)
        first, along_y = both_halves(grid_row(refs, 2, gx, core))
        tangent_ref[gx] = first
        second.append(along_y)
    turned = Turned(tangent_ref)
    best = jnp.zeros((4, 8, 128), jnp.float32)
    for gx in range(16):
        first = tangent_ref[gx]
        above, below = turned.sides(gx)
        third, mass = both_halves(grid_row(refs, 3, gx, core))
        spring = grid_row(refs, 4, gx, core)
        ups = [
            0.5 * (first + above),
            0.5 * (second[gx] + y_up(second[gx])),
            0.5 * (third + z_up(third)),
        ]
        downs = [
            0.5 * (first + below),
            0.5 * (second[gx] + y_down(second[gx])),
            0.5 * (third + z_down(third)),
        ]
        total = (ups[0] + ups[1] + ups[2]) + (downs[0] + downs[1] + downs[2])
        for direction in range(3):
            held_ref[gx, UP + direction] = ups[direction]
            held_ref[gx, DOWN + direction] = downs[direction]
        diagonal = spring + total
        held_ref[gx, DIAGONAL] = diagonal
        held_ref[gx, MASS] = mass
        best = jnp.maximum(best, (diagonal + total) / mass)
    best = jnp.max(jnp.max(best, axis=0), axis=(0, 1), keepdims=True)
    top_ref[...] = jnp.broadcast_to(best, (32, 128))


def filter_kernel(held_ref, top_ref, terms_ref, inverse_ref):
    top = top_ref[0:1, :]
    inverse_spread = 1.0 / (top * 7.0 / 16.0)
    ratio = (top * 9.0 / 16.0) * inverse_spread
    for gx in range(16):
        mass = held_ref[gx, MASS]
        inverse_ref[gx] = inverse_spread / mass
        terms_ref[0, gx] = held_ref[gx, 0]
        terms_ref[TOTAL + 2, gx] = mass
    for degree in range(1, TOTAL + 2):
        current_ref = terms_ref.at[degree - 1]
        turned = Turned(current_ref)
        for gx in range(16):
            here, sides = around(current_ref, turned, gx)
            image = held_ref[gx, DIAGONAL] * here
            for direction in range(3):
                image = image - held_ref[gx, UP + direction] * sides[direction][0]
                image = image - held_ref[gx, DOWN + direction] * sides[direction][1]
            image = image * inverse_ref[gx] - ratio * here
            if degree > 1:
                image = 2.0 * image - terms_ref[degree - 2, gx]
            terms_ref[degree, gx] = image


def combine_kernel(terms_ref, own_top_ref, top_ref, nodes_ref, out_ref):
    top = jnp.max(jnp.max(top_ref[...], axis=0, keepdims=True), axis=1, keepdims=True)
    own_top = own_top_ref[0:1, :]
    part = own_top / top
    place = part * nodes_ref[0:1, :] + (part - 1.0) * (9.0 / 7.0)
    square = place * place
    once = 8.0 * square * square - 8.0 * square + 1.0
    coefficients = jnp.sum(nodes_ref[8:40, :] * (once * once), axis=1, keepdims=True)
    middle = own_top * 9.0 / 16.0
    spread = own_top * 7.0 / 16.0
    for gx in range(16):
        total = coefficients[0:1, :] * terms_ref[0, gx]
        scaled = coefficients[16:17, :] * terms_ref[0, gx]
        for degree in range(1, TOTAL + 2):
            term = terms_ref[degree, gx]
            if degree <= TOTAL:
                total = total + coefficients[degree : degree + 1, :] * term
            scaled = scaled + coefficients[16 + degree : 17 + degree, :] * term
        image = terms_ref[TOTAL + 2, gx] * (middle * total + spread * scaled)
        out_ref[pl.ds(gx * 64, 32, stride=2), :] = total.reshape(32, 128)
        out_ref[pl.ds(gx * 64 + 1, 32, stride=2), :] = image.reshape(32, 128)


def parts_of(rows_ref, kind):
    return [
        jnp.concatenate(
            [rows_ref[pl.ds((gx * 4 + comp) * 16 + kind, 8, stride=2), :] for gx in range(16)],
            axis=0,
        )
        for comp in range(3)
    ]


def pair_rows(one, two):
    low = lax.broadcasted_iota(jnp.int32, (128, 128), 1) < 64
    upper = jnp.where(low, one, 0.0 if two is None else pltpu.roll(two, 64, 1))
    lower = jnp.where(low, pltpu.roll(one, 64, 1), 0.0 if two is None else two)
    return jnp.concatenate([upper, lower], axis=0)


def by_vector(parts):
    return jnp.concatenate(
        [pair_rows(parts[0], parts[1]), pair_rows(parts[2], None)], axis=1
    )


def product_kernel(rows_ref, mass_ref, out_ref, along_x_ref, along_y_ref, along_z_ref):
    parts = parts_of(rows_ref, 0)
    vectors = by_vector(parts)
    along_x_ref[...] = vectors[:, :128]
    along_y_ref[...] = pair_rows(parts[1], parts[2])
    along_z_ref[...] = pair_rows(parts[2], parts[0])
    image = by_vector(parts_of(rows_ref, 1))
    weighted = vectors * mass_ref[...]
    gram = dot(weighted, vectors, ((1,), (1,)))
    stiff = dot(vectors, image, ((1,), (1,)))
    row = lax.broadcasted_iota(jnp.int32, (256, 256), 0)
    column = lax.broadcasted_iota(jnp.int32, (256, 256), 1)
    both = jnp.where(row >= column, gram, stiff)
    diagonal = jnp.sum(vectors * image, axis=1, keepdims=True)
    lane = lax.broadcasted_iota(jnp.int32, (256, 128), 1)
    lateral = jnp.sum(jnp.where(lane < NODES, weighted[:, :128], 0.0), axis=1, keepdims=True)
    further = jnp.where(lane == 0, diagonal, jnp.where(lane == 1, lateral, 0.0)).T
    for chunk in range(32):
        half = slice(0, 128) if chunk < 16 else slice(128, 256)
        first = chunk % 16 * 16
        out_ref[chunk * CHUNK : chunk * CHUNK + 16, :] = both[first : first + 16, half]
        last = further[chunk // 2 : chunk // 2 + 1, chunk % 2 * 128 : chunk % 2 * 128 + 128]
        out_ref[chunk * CHUNK + 16 : chunk * CHUNK + 17, :] = last


def total_kernel(count, copies, rows_ref, out_ref):
    total = rows_ref[0:CHUNK, :]
    for place in range(1, count):
        total = total + rows_ref[place * CHUNK : place * CHUNK + CHUNK, :]
    for place in range(copies):
        out_ref[place * CHUNK : place * CHUNK + CHUNK, :] = total


def factor_block(gram, stiff):
    lane = lax.broadcasted_iota(jnp.int32, (BLOCK, 128), 1)
    row = lax.broadcasted_iota(jnp.int32, (BLOCK, 128), 0)
    low = lane < 64
    columns = [
        jnp.where(
            low,
            jnp.broadcast_to(gram[:, j : j + 1], (BLOCK, 128)),
            jnp.broadcast_to(stiff[:, j : j + 1], (BLOCK, 128)),
        )
        for j in range(BLOCK)
    ]
    inverse = jnp.where((lane & 63) == row, 1.0, 0.0)
    scale = jnp.ones((BLOCK, 128), jnp.float32)
    link = jnp.zeros((BLOCK, 128), jnp.float32)
    for k in range(0, BLOCK, 2):
        one, two = columns[k], columns[k + 1]
        top = one[k : k + 1, :]
        side = one[k + 1 : k + 2, :]
        corner = two[k + 1 : k + 2, :]
        rest = top * corner - side * side
        scale = jnp.where(row == k, top, jnp.where(row == k + 1, rest / top, scale))
        link = jnp.where(row == k + 1, side / top, link)
        if k + 2 == BLOCK:
            break
        part = (k + 2) // 8 * 8
        factor = 1.0 / rest
        below = row[part:] > k + 1
        first = jnp.where(below, (one[part:] * corner - two[part:] * side) * factor, 0.0)
        second = jnp.where(below, (two[part:] * top - one[part:] * side) * factor, 0.0)

        def reduced(value):
            tail = value[part:] - (first * value[k : k + 1, :] + second * value[k + 1 : k + 2, :])
            return tail if part == 0 else jnp.concatenate([value[:part], tail], axis=0)

        for j in range(k + 2, BLOCK):
            columns[j] = reduced(columns[j])
        inverse = reduced(inverse)
    inverse = inverse - link * pltpu.roll(inverse, 1, 0)
    return inverse * lax.rsqrt(scale), scale


def rounded(value):
    return value.astype(jnp.bfloat16).astype(jnp.float32)


def three_parts(value):
    high = rounded(value)
    rest = value - high
    middle = rounded(rest)
    return high, middle, rest - middle


def four_copies(value):
    return (value + pltpu.roll(value, 32, 1)) + (
        pltpu.roll(value, 64, 1) + pltpu.roll(value, 96, 1)
    )


def left_groups(first, second):
    group = lax.broadcasted_iota(jnp.int32, first.shape, 1) // BLOCK
    high, middle, _ = three_parts(first)
    parts = three_parts(second)
    one = jnp.where(group < 2, high, middle)
    two = jnp.where(group == 0, parts[0], jnp.where(group == 1, parts[2], 0.0))
    return jnp.concatenate([one, two], axis=1).astype(jnp.bfloat16)


def right_lanes(copies):
    group = lax.broadcasted_iota(jnp.int32, copies.shape, 1) // BLOCK
    high, middle, low = three_parts(copies)
    one = jnp.where(group % 2 == 0, high, middle)
    two = jnp.where(group == 0, low, high)
    return jnp.concatenate([one, two], axis=1).astype(jnp.bfloat16)


def right_rows(value):
    high, middle, low = [part.astype(jnp.bfloat16) for part in three_parts(value)]
    return jnp.concatenate([high, middle, high, middle, low, high, high, high], axis=0)


def product(left, right, contract):
    return lax.dot_general(
        left, right, (contract, ((), ())), preferred_element_type=jnp.float32
    )


def invert_factors(m_ref, diagonal):
    lane = lax.broadcasted_iota(jnp.int32, (BLOCK, 128), 1)
    least = jnp.ones((BLOCK, 128), jnp.float32)
    for first in range(0, 256, BLOCK):
        tile = first // 128 * 128
        inside = first - tile
        after = first + BLOCK
        small = [m_ref[m, first:after, tile : tile + 128][:, inside : inside + BLOCK] for m in (0, 1)]
        inverse, pivots = factor_block(small[0], small[1])
        least = jnp.minimum(least, pivots / diagonal[first:after, :])
        for m in (0, 1):
            own = four_copies(
                jnp.where((lane >= 64 * m) & (lane < 64 * m + BLOCK), inverse, 0.0)
            )
            row = lax.broadcasted_iota(jnp.int32, (BLOCK, 256), 0)
            column = lax.broadcasted_iota(jnp.int32, (BLOCK, 256), 1) - first
            rows = m_ref[m, first:after, :]
            unit = jnp.where(column == row, 1.0, 0.0)
            rows = jnp.where((column >= 0) & (column < BLOCK), unit, rows)
            result = product(left_groups(own, own), right_rows(rows), ((1,), (0,)))
            m_ref[m, first:after, :] = result
            if after < 256:
                count = 256 - after
                lanes = lax.broadcasted_iota(jnp.int32, (count, 128), 1)
                held = (lanes >= inside) & (lanes < inside + BLOCK)
                left = four_copies(jnp.where(held, m_ref[m, after:, tile : tile + 128], 0.0))
                right = jnp.concatenate([right_lanes(own)] * 8, axis=0)
                factor = product(left_groups(left, left), right, ((1,), (1,)))
                column = lax.broadcasted_iota(jnp.int32, (count, 256), 1)
                rows = m_ref[m, after:, :]
                rows = jnp.where((column >= first) & (column < after), 0.0, rows)
                m_ref[m, after:, :] = rows - product(
                    left_groups(factor[:, :128], factor[:, 128:]), right_rows(result), ((1,), (0,))
                )
    return jnp.min(least, axis=(0, 1), keepdims=True)


def final_kernel(
    sums_ref, rows_ref, above_x_ref, below_x_ref, above_y_ref, below_y_ref, above_z_ref,
    below_z_ref, mass_ref, modulus_ref, stress_ref, subspace_ref, projected_ref, force_ref,
    stress_new_ref, least_ref, m_ref
):
    chunks = [sums_ref[chunk * CHUNK : chunk * CHUNK + 16, :] for chunk in range(32)]
    both = jnp.concatenate(
        [jnp.concatenate(chunks[:16], axis=0), jnp.concatenate(chunks[16:], axis=0)], axis=1
    )
    further = [
        jnp.broadcast_to(sums_ref[chunk * CHUNK + 16 : chunk * CHUNK + 17, :], (128, 128)).T
        for chunk in range(4)
    ]
    diagonal = jnp.concatenate(further[:2], axis=0)
    diagonal = jnp.concatenate([diagonal, diagonal], axis=1)
    lateral = jnp.concatenate(further[2:], axis=0)
    turned = both.T
    row = lax.broadcasted_iota(jnp.int32, (256, 256), 0)
    column = lax.broadcasted_iota(jnp.int32, (256, 256), 1)
    gram = jnp.where(row >= column, both, turned)
    stiff = jnp.where(row < column, both, jnp.where(row == column, diagonal, turned))
    m_ref[0] = gram
    m_ref[1] = stiff
    half = lax.broadcasted_iota(jnp.int32, (256, 128), 1) < 64
    gram_diagonal = jnp.sum(jnp.where(row == column, gram, 0.0), axis=1, keepdims=True)
    least = invert_factors(m_ref, jnp.where(half, gram_diagonal, diagonal[:, :128]))
    least_ref[...] = jnp.broadcast_to(least, (8, 128))
    lower = jnp.where(row >= column, m_ref[0], 0.0)
    stiff_lower = jnp.where(row >= column, m_ref[1], 0.0)
    vectors = by_vector(parts_of(rows_ref, 0))
    subspace = dot(vectors.T, lower, ((1,), (1,)))
    subspace = subspace * jnp.sqrt(jnp.float32(DEVICES * 3 * NODES))
    projected_ref[...] = dot(lower, dot(stiff, lower, ((1,), (1,))))
    weights = dot(stiff_lower.T, dot(stiff_lower, lateral))
    weights = jnp.concatenate([weights, weights], axis=1)
    displace = jnp.sum(vectors * weights, axis=0, keepdims=True)
    own = [displace[:, :128], pltpu.roll(displace[:, :128], 64, 1), displace[:, 128:]]
    outside = [
        jnp.sum(ref[...] * weights[:, :128], axis=0, keepdims=True)
        for ref in (above_x_ref, below_x_ref, above_y_ref, below_y_ref, above_z_ref, below_z_ref)
    ]
    lane = lax.broadcasted_iota(jnp.int32, (1, 128), 1)
    axial = []
    bending = []
    for direction, (step, mask) in enumerate(((32, 32), (1, 7), (8, 24))):
        wide = jnp.where(lane < 64, own[direction], pltpu.roll(own[(direction + 1) % 3], 64, 1))
        above = jnp.where(
            (lane & mask) == mask,
            pltpu.roll(outside[2 * direction], mask, 1),
            pltpu.roll(wide, 128 - step, 1),
        )
        below = jnp.where(
            (lane & mask) == 0,
            pltpu.roll(outside[2 * direction + 1], 128 - mask, 1),
            pltpu.roll(wide, step, 1),
        )
        axial.append(0.5 * (above - below))
        bending.append(pltpu.roll((above - 2.0 * wide) + below, 64, 1))
    lane = lax.broadcasted_iota(jnp.int32, (24, 256), 1)
    group = lax.broadcasted_iota(jnp.int32, (24, 256), 0)
    laid = jnp.where((lane >> 3) == group, displace * mass_ref[...], 0.0)
    column = lax.broadcasted_iota(jnp.int32, (256, 128), 0)
    place = lax.broadcasted_iota(jnp.int32, (256, 128), 1)
    force_ref[...] = dot(laid, jnp.where((column & 7) == place, 1.0, 0.0))[:, :8]
    columns = jnp.concatenate(
        axial + bending + [jnp.zeros((122, 128), jnp.float32)], axis=0
    ).T
    axial = [jnp.broadcast_to(columns[:, d : d + 1], (128, 16)) for d in range(3)]
    bending = [jnp.broadcast_to(columns[:, 3 + d : 4 + d], (128, 16)) for d in range(3)]
    fiber = lax.broadcasted_iota(jnp.int32, (8, 16), 1).astype(jnp.float32)
    heights = (fiber + 0.5) / 16.0 - 0.5
    for direction in range(3):
        for x in range(2):
            for z in range(4):
                rows = slice(direction * 16 + x * 8, direction * 16 + x * 8 + 8)
                inner = x * 32 + z * 8
                one = direction * NODES + inner
                subspace_ref[rows, z, :] = subspace[one : one + 8]
                strain = axial[direction][inner : inner + 8]
                strain = strain + heights * bending[direction][inner : inner + 8]
                stress_new_ref[rows, z, :] = stress_ref[rows, z, :] + modulus_ref[rows, z, :] * strain


def fiber_modulus(stiffness, yield_flags):
    own = jnp.stack([stiffness[d, d] for d in range(3)])[:, None]
    return own * jnp.where(yield_flags == 1, 0.05, 1.0)


def extended(block, first_dim):
    for place, axis in enumerate((GX, "gy", "gz")):
        dim = first_dim + place
        count = lax.axis_size(axis)
        forward = [(i, i + 1) for i in range(count - 1)]
        backward = [(target, source) for source, target in forward]
        last = block.shape[dim]
        low = lax.ppermute(lax.slice_in_dim(block, last - 1, last, axis=dim), axis, forward)
        high = lax.ppermute(lax.slice_in_dim(block, 0, 1, axis=dim), axis, backward)
        block = jnp.concatenate([low, block, high], axis=dim)
    return block


def neighbour(padded, leading, direction, sense):
    slicer = [slice(None)] * padded.ndim
    for position in range(3):
        slicer[leading + position] = slice(1, -1)
    slicer[leading + direction] = slice(2, None) if sense > 0 else slice(0, -2)
    return padded[tuple(slicer)]


def summed(square):
    rows = jnp.concatenate([square[:, :128], square[:, 128:]], axis=0)
    for axes, count, copies in ((("cy", "gy"), 32, 16), (("core", "gz"), 16, 32)):
        rows = jnp.sum(exchange(rows, axes, count).reshape(count, 16, 128), axis=0)
        rows = jnp.tile(rows, (copies, 1))
    rows = exchange(rows, ("cy", "gy"), 32)
    return jnp.concatenate([rows[:256], rows[256:]], axis=1)


def step_by_step(start_block, node_mass, ground_spring, stiffness, yield_flags, stress_old):
    share = jnp.mean(yield_flags.astype(jnp.float32), axis=1)
    tangent = stiffness * (1.0 - 0.9 * share)[:, None]
    padded = extended(tangent, 2)
    edges = [
        [0.5 * (tangent[d] + neighbour(padded, 2, d, sense)[d]) for d in range(3)]
        for sense in (1, -1)
    ]
    edge_total = sum(edges[0]) + sum(edges[1])
    diagonal = ground_spring + edge_total
    top = jnp.broadcast_to(jnp.max((diagonal + edge_total) / node_mass), (128, 128))
    for axes, count in ((("cy", "core"), 16), ("gy", 4), ("gz", 8)):
        top = jnp.broadcast_to(jnp.max(exchange(top, axes, count)), (128, 128))
    top = top[0, 0]
    middle = top * 9.0 / 16.0
    spread = top * 7.0 / 16.0

    def apply_k(field):
        around_field = extended(field, 1)
        result = diagonal[..., None] * field
        for d in range(3):
            for sense, weights in ((1, edges[0]), (-1, edges[1])):
                result = result - weights[d][..., None] * neighbour(around_field, 1, d, sense)
        return result

    def shifted(field):
        return (apply_k(field) / node_mass[..., None] - middle * field) / spread

    width = start_block.shape[-1]
    mass_rows = node_mass.reshape(-1)
    vectors = start_block
    for turn in range(ITERS):
        earlier, current = vectors, shifted(vectors)
        for repeat in range(DEGREE - 1):
            earlier, current = current, 2.0 * shifted(current) - earlier
        flat_rows = current.reshape(-1, width)
        gram = summed(dot(flat_rows.T, mass_rows[:, None] * flat_rows))
        factor = jnp.linalg.cholesky(gram)
        basis = lax.linalg.triangular_solve(factor, flat_rows.T, left_side=True, lower=True)
        vectors = basis.T.reshape(current.shape)
    image = apply_k(vectors).reshape(-1, width)
    projected = summed(dot(basis, image))
    lateral = dot(basis[:, :NODES], mass_rows[:NODES, None])
    lateral = summed(jnp.broadcast_to(lateral, (width, width)))[:, :1]
    factor = jnp.linalg.cholesky(projected)
    halfway = lax.linalg.triangular_solve(factor, lateral, left_side=True, lower=True)
    weights = lax.linalg.triangular_solve(
        factor, halfway, left_side=True, lower=True, transpose_a=True
    )
    displace = dot(weights.T, basis).reshape(node_mass.shape)
    padded = extended(displace, 1)
    axial = []
    bending = []
    for d in range(3):
        above = neighbour(padded, 1, d, 1)
        below = neighbour(padded, 1, d, -1)
        other = (d + 1) % 3
        axial.append(0.5 * (above[d] - below[d]))
        bending.append(above[other] - 2.0 * displace[other] + below[other])
    fibers = stress_old.shape[1]
    heights = ((jnp.arange(fibers).astype(jnp.float32) + 0.5) / fibers - 0.5)[:, None, None, None]
    strain = jnp.stack(axial)[:, None] + heights * jnp.stack(bending)[:, None]
    stress_new = stress_old + fiber_modulus(stiffness, yield_flags) * strain
    subspace = vectors * jnp.sqrt(jnp.float32(DEVICES * 3 * NODES))
    return subspace, projected, node_mass * displace, stress_new


def call(kernel, shape, scratch=(), smem=(), operands=()):
    return pl.pallas_call(
        kernel,
        out_shape=shape,
        in_specs=[
            pl.BlockSpec(memory_space=pltpu.SMEM if place in smem else pltpu.VMEM)
            for place in range(len(operands))
        ],
        out_specs=jax.tree.map(lambda _: pl.BlockSpec(memory_space=pltpu.VMEM), shape),
        scratch_shapes=list(scratch),
        compiler_params=pltpu.CompilerParams(vmem_limit_bytes=40 * 1024 * 1024),
    )(*operands)


def rows_of(count):
    return jax.ShapeDtypeStruct((count, 128), jnp.float32)


def exchange(rows, axes, devices):
    per_device = rows.shape[0] // devices
    if per_device % 8 == 0:
        blocks = rows.reshape(devices, per_device, 128)
    else:
        blocks = rows.reshape(devices, per_device, 1, 128)
    return lax.all_to_all(blocks, axes, 0, 0, tiled=True).reshape(rows.shape)


def chebyshev_nodes():
    count = TOTAL + 1
    angles = np.pi * (np.arange(count) + 0.5) / count
    plain = np.zeros((count, count))
    timesx = np.zeros((count + 1, count))
    for degree in range(count):
        plain[degree] = (2.0 if degree else 1.0) / count * np.cos(degree * angles)
        timesx[degree + 1] += plain[degree] * (0.5 if degree else 1.0)
        if degree:
            timesx[degree - 1] += plain[degree] * 0.5
    table = np.zeros((40, 128), np.float32)
    table[0, :count] = np.cos(angles)
    table[8 : 8 + count, :count] = plain
    table[24 : 25 + count, :count] = timesx
    return jnp.asarray(table)


def on_device(start_block, node_mass, ground_spring, stiffness, yield_flags, stress_old):
    width = start_block.shape[-1]
    fibers = stress_old.shape[1]

    def node_rows(value):
        return jnp.swapaxes(value, -1, -2).reshape(-1, 8)

    def fibers_last(value):
        return jnp.moveaxis(value, 1, -1).reshape(48, 4, fibers)

    grid_shape = (16, 4, 8, 128)
    plain = pltpu.VMEM(grid_shape, jnp.float32)
    planes_shape = (16, KINDS, 4, 8, 128)
    sent = call(
        pack_kernel,
        rows_of(256 * OUT_ROWS),
        operands=(
            start_block.reshape(48, 4, width),
            node_rows(stiffness),
            jnp.concatenate([node_rows(node_mass), node_rows(ground_spring)], axis=0),
            fibers_last(yield_flags).reshape(3 * NODES, fibers),
        ),
    )
    own = exchange(sent, CHIPS, 256)
    other = lax.ppermute(own, "core", [(0, 1), (1, 0)])
    core = lax.axis_index("core").astype(jnp.int32).reshape(1)
    planes, own_top = call(
        weights_kernel,
        (jax.ShapeDtypeStruct(planes_shape, jnp.float32), rows_of(32)),
        (plain,),
        smem=(0,),
        operands=(core, own, other),
    )
    tops = exchange(own_top, "gy", 4)
    terms = call(
        filter_kernel,
        jax.ShapeDtypeStruct((TOTAL + 3,) + grid_shape, jnp.float32),
        (plain,),
        operands=(planes, own_top),
    )
    filtered = call(
        combine_kernel,
        rows_of(1024),
        operands=(terms, own_top, tops, chebyshev_nodes()),
    )
    returned = exchange(filtered, AXES, DEVICES)
    mass_row = node_rows(node_mass).reshape(1, 3 * NODES)
    mass_row = jnp.pad(mass_row, ((0, 0), (0, NODES)))
    along = jax.ShapeDtypeStruct((width, 128), jnp.float32)
    products, *along = call(
        product_kernel,
        (rows_of(32 * CHUNK), along, along, along),
        operands=(returned, mass_row),
    )

    def from_neighbours(mine, axis, senses):
        count = lax.axis_size(axis)
        pairs = [(i, i + 1) for i in range(count - 1)]
        return [
            lax.ppermute(mine, axis, [(b, a) for a, b in pairs] if sense > 0 else pairs)
            for sense in senses
        ]

    near = from_neighbours(along[0], GX, (1, -1)) + from_neighbours(along[1], "gy", (1,))
    part = exchange(products, ("cy", "gy"), 32)
    part, *near = lax.optimization_barrier((part, *near))
    part = call(functools.partial(total_kernel, 32, 16), rows_of(16 * CHUNK), operands=(part,))
    part = exchange(part, ("core", "gz"), 16)
    part = call(functools.partial(total_kernel, 16, 32), rows_of(32 * CHUNK), operands=(part,))
    part, *along[1:] = lax.optimization_barrier((part, *along[1:]))
    far = from_neighbours(along[1], "gy", (-1,)) + from_neighbours(along[2], "gz", (1, -1))
    part = exchange(part, ("cy", "gy"), 32)
    part, *far = lax.optimization_barrier((part, *far))
    subspace, projected, force, stress_new, least = call(
        final_kernel,
        (
            jax.ShapeDtypeStruct((48, 4, width), jnp.float32),
            jax.ShapeDtypeStruct((width, width), jnp.float32),
            jax.ShapeDtypeStruct((24, 8), jnp.float32),
            jax.ShapeDtypeStruct((48, 4, fibers), jnp.float32),
            rows_of(8),
        ),
        (pltpu.VMEM((2, 256, 256), jnp.float32),),
        operands=(
            part,
            returned,
            *near,
            *far,
            mass_row,
            fibers_last(fiber_modulus(stiffness, yield_flags)),
            fibers_last(stress_old),
        ),
    )
    place = node_mass.shape[1:]
    force = jnp.swapaxes(force.reshape(3, place[0], place[2], place[1]), -1, -2)
    stress_new = jnp.moveaxis(stress_new.reshape((3,) + place + (fibers,)), -1, 1)
    return lax.cond(
        least[0, 0] > LEAST_PIVOT,
        lambda *operands: operands[:4],
        lambda *operands: step_by_step(*operands[4:]),
        subspace.reshape(start_block.shape),
        projected,
        force,
        stress_new,
        start_block,
        node_mass,
        ground_spring,
        stiffness,
        yield_flags,
        stress_old,
    )


def solution(mesh):
    chips = Mesh(mesh.devices.reshape(8, 2, 4, 8), AXES)
    return jax.shard_map(
        on_device,
        mesh=chips,
        in_specs=(
            P(None, GX, "gy", "gz", None),
            P(None, GX, "gy", "gz"),
            P(None, GX, "gy", "gz"),
            P(None, None, GX, "gy", "gz"),
            P(None, None, GX, "gy", "gz"),
            P(None, None, GX, "gy", "gz"),
        ),
        out_specs=(
            P(None, GX, "gy", "gz", None),
            P(),
            P(None, GX, "gy", "gz"),
            P(None, None, GX, "gy", "gz"),
        ),
        check_vma=False,
    )
```

```python
import functools

import jax
import jax.numpy as jnp
import numpy as np
from jax import lax
from jax.experimental import pallas as pl
from jax.experimental.pallas import tpu as pltpu
from jax.sharding import Mesh, PartitionSpec as P

DEGREE = 4
ITERS = 2
TOTAL = DEGREE * ITERS
PRECISE = lax.Precision.HIGHEST
GX = ("cy", "core")
AXES = ("cy", "core", "gy", "gz")
CHIPS = ("cy", "gy", "gz")

NODES = 64
DEVICES = 512
OUT_ROWS = 5
LEAST_PIVOT = 0.1
BLOCK = 32
CHUNK = 17
LEAST_PIVOT = 0.1
BLOCK = 32
STIFF_LANE = 9
MASS_LANE = 10


def dot(a, b, contract=((1,), (0,))):
    return lax.dot_general(
        a, b, (contract, ((), ())), precision=PRECISE, preferred_element_type=jnp.float32
    )


def spread_nodes(values, keep):
    groups = jnp.where(keep, values.reshape((-1,) + keep.shape), 0.0)
    return jnp.sum(groups, axis=1)


def pack_kernel(start_ref, stiffness_ref, mass_ref, spring_ref, flags_ref, out_ref):
    lane = lax.broadcasted_iota(jnp.int32, (8, 128), 1)
    place = lax.broadcasted_iota(jnp.int32, (8, 128), 0)
    repeated = jnp.where((lane & 7) == place, 1.0, 0.0)
    keep = ((lane >> 3) & 7) == place
    stiffness = spread_nodes(dot(stiffness_ref[...], repeated), keep)
    masses = spread_nodes(dot(mass_ref[...], repeated), keep)
    springs = spread_nodes(dot(spring_ref[...], repeated), keep)
    counts = jnp.dot(
        flags_ref[...].astype(jnp.bfloat16),
        jnp.ones((16, 128), jnp.bfloat16),
        preferred_element_type=jnp.float32,
    )
    lane = lax.broadcasted_iota(jnp.int32, (NODES, 128), 1)
    place = lax.broadcasted_iota(jnp.int32, (NODES, 128), 0)
    own = ((place >> 5) * 32 + (place & 3) * 8 + ((place >> 2) & 7)) == (lane & 63)
    softening = 1.0 - 0.9 * (spread_nodes(counts, own) / 16.0)
    low = lax.broadcasted_iota(jnp.int32, (1, 128), 1) < 64
    for comp in range(4):
        source = comp % 3
        if comp < 3:
            block = jnp.concatenate(
                [
                    start_ref[comp * 16 + x * 8 : comp * 16 + x * 8 + 8, z, :]
                    for x in range(2)
                    for z in range(4)
                ],
                axis=0,
            )
            pairs = jnp.concatenate([block[:, :128], block[:, 128:]], axis=0).T
        else:
            pairs = jnp.zeros((128, 128), jnp.float32)
        tangent = [
            stiffness[3 * d + source : 3 * d + source + 1, :] * softening[d : d + 1, :]
            for d in range(3)
        ]
        mass = masses[source : source + 1, :]
        spring = springs[source : source + 1, :]
        rows = [
            jnp.broadcast_to(row, (8, 128))
            for row in (
                jnp.where(low, tangent[0], tangent[1]),
                jnp.where(low, tangent[2], mass),
                spring,
            )
        ]
        for cy in range(8):
            first = (cy * 4 + comp) * 8 * OUT_ROWS
            for core in range(2):
                at = (cy * 2 + core) * 8
                out_ref[pl.ds(first + core, 8, stride=OUT_ROWS), :] = pairs[at : at + 8]
            for r in range(3):
                out_ref[pl.ds(first + 2 + r, 8, stride=OUT_ROWS), :] = rows[r]


def iota(axis):
    return lax.broadcasted_iota(jnp.int32, (4, 8, 128), axis)


def grid_row(refs, kind, gx, core):
    rows = [ref[pl.ds(gx // 2 * 32 * OUT_ROWS + kind, 32, stride=OUT_ROWS), :] for ref in refs]
    return jnp.where(core == gx % 2, rows[0], rows[1]).reshape(4, 8, 128)


def roll(value, shift, axis=2):
    return pltpu.roll(value, shift, axis)


def both_halves(value):
    lane = iota(2)
    turned = roll(value, 64)
    return jnp.where(lane < 64, value, turned), jnp.where(lane < 64, turned, value)


class Turned:
    def __init__(self, ref):
        self.ref = ref
        self.planes = {}

    def at(self, gx):
        if gx not in self.planes:
            if gx in (-1, 16):
                zero = jnp.zeros((4, 8, 128), jnp.float32)
                self.planes[gx] = (zero, zero)
            else:
                here = self.ref[gx]
                self.planes[gx] = (roll(here, 96), roll(here, 32))
        return self.planes[gx]

    def sides(self, gx):
        first = (iota(2) & 32) == 0
        up = jnp.where(first, self.at(gx)[0], self.at(gx + 1)[1])
        down = jnp.where(first, self.at(gx - 1)[0], self.at(gx)[1])
        return up, down


def y_up(here):
    moved = jnp.concatenate([here[1:], jnp.zeros((1, 8, 128), jnp.float32)], axis=0)
    return jnp.where((iota(2) & 7) != 7, roll(here, 127), roll(moved, 7))


def y_down(here):
    moved = jnp.concatenate([jnp.zeros((1, 8, 128), jnp.float32), here[:-1]], axis=0)
    return jnp.where((iota(2) & 7) != 0, roll(here, 1), roll(moved, 121))


def z_up(here):
    other = jnp.where(iota(1) < 7, roll(roll(here, 24), 7, 1), 0.0)
    return jnp.where((iota(2) & 24) != 24, roll(here, 120), other)


def z_down(here):
    other = jnp.where(iota(1) > 0, roll(roll(here, 104), 1, 1), 0.0)
    return jnp.where((iota(2) & 24) != 0, roll(here, 8), other)


def around(ref, turned, gx):
    here = ref[gx]
    return here, (turned.sides(gx), (y_up(here), y_down(here)), (z_up(here), z_down(here)))


UP, DOWN, DIAGONAL, MASS, KINDS = 1, 4, 7, 8, 9


def weights_kernel(
    core_ref, own_ref, other_ref, held_ref, top_ref, tangent_ref
):
    core = core_ref[0]
    refs = (own_ref, other_ref)
    second = []
    for gx in range(16):
        held_ref[gx, 0] = grid_row(refs, core, gx, core)
        first, along_y = both_halves(grid_row(refs, 2, gx, core))
        tangent_ref[gx] = first
        second.append(along_y)
    turned = Turned(tangent_ref)
    best = jnp.zeros((4, 8, 128), jnp.float32)
    for gx in range(16):
        first = tangent_ref[gx]
        above, below = turned.sides(gx)
        third, mass = both_halves(grid_row(refs, 3, gx, core))
        spring = grid_row(refs, 4, gx, core)
        ups = [
            0.5 * (first + above),
            0.5 * (second[gx] + y_up(second[gx])),
            0.5 * (third + z_up(third)),
        ]
        downs = [
            0.5 * (first + below),
            0.5 * (second[gx] + y_down(second[gx])),
            0.5 * (third + z_down(third)),
        ]
        total = (ups[0] + ups[1] + ups[2]) + (downs[0] + downs[1] + downs[2])
        for direction in range(3):
            held_ref[gx, UP + direction] = ups[direction]
            held_ref[gx, DOWN + direction] = downs[direction]
        diagonal = spring + total
        held_ref[gx, DIAGONAL] = diagonal
        held_ref[gx, MASS] = mass
        best = jnp.maximum(best, (diagonal + total) / mass)
    best = jnp.max(jnp.max(best, axis=0), axis=(0, 1), keepdims=True)
    top_ref[...] = jnp.broadcast_to(best, (32, 128))


def filter_kernel(held_ref, top_ref, terms_ref, inverse_ref):
    top = top_ref[0:1, :]
    inverse_spread = 1.0 / (top * 7.0 / 16.0)
    ratio = (top * 9.0 / 16.0) * inverse_spread
    for gx in range(16):
        mass = held_ref[gx, MASS]
        inverse_ref[gx] = inverse_spread / mass
        terms_ref[0, gx] = held_ref[gx, 0]
        terms_ref[TOTAL + 2, gx] = mass
    for degree in range(1, TOTAL + 2):
        current_ref = terms_ref.at[degree - 1]
        turned = Turned(current_ref)
        for gx in range(16):
            here, sides = around(current_ref, turned, gx)
            image = held_ref[gx, DIAGONAL] * here
            for direction in range(3):
                image = image - held_ref[gx, UP + direction] * sides[direction][0]
                image = image - held_ref[gx, DOWN + direction] * sides[direction][1]
            image = image * inverse_ref[gx] - ratio * here
            if degree > 1:
                image = 2.0 * image - terms_ref[degree - 2, gx]
            terms_ref[degree, gx] = image


def combine_kernel(terms_ref, own_top_ref, top_ref, nodes_ref, out_ref):
    top = jnp.max(jnp.max(top_ref[...], axis=0, keepdims=True), axis=1, keepdims=True)
    own_top = own_top_ref[0:1, :]
    part = own_top / top
    place = part * nodes_ref[0:1, :] + (part - 1.0) * (9.0 / 7.0)
    square = place * place
    once = 8.0 * square * square - 8.0 * square + 1.0
    coefficients = jnp.sum(nodes_ref[8:40, :] * (once * once), axis=1, keepdims=True)
    middle = own_top * 9.0 / 16.0
    spread = own_top * 7.0 / 16.0
    for gx in range(16):
        total = coefficients[0:1, :] * terms_ref[0, gx]
        scaled = coefficients[16:17, :] * terms_ref[0, gx]
        for degree in range(1, TOTAL + 2):
            term = terms_ref[degree, gx]
            if degree <= TOTAL:
                total = total + coefficients[degree : degree + 1, :] * term
            scaled = scaled + coefficients[16 + degree : 17 + degree, :] * term
        image = terms_ref[TOTAL + 2, gx] * (middle * total + spread * scaled)
        out_ref[pl.ds(gx * 64, 32, stride=2), :] = total.reshape(32, 128)
        out_ref[pl.ds(gx * 64 + 1, 32, stride=2), :] = image.reshape(32, 128)


def parts_of(rows_ref, kind):
    return [
        jnp.concatenate(
            [rows_ref[pl.ds((gx * 4 + comp) * 16 + kind, 8, stride=2), :] for gx in range(16)],
            axis=0,
        )
        for comp in range(3)
    ]


def pair_rows(one, two):
    low = lax.broadcasted_iota(jnp.int32, (128, 128), 1) < 64
    upper = jnp.where(low, one, 0.0 if two is None else pltpu.roll(two, 64, 1))
    lower = jnp.where(low, pltpu.roll(one, 64, 1), 0.0 if two is None else two)
    return jnp.concatenate([upper, lower], axis=0)


def by_vector(parts):
    return jnp.concatenate(
        [pair_rows(parts[0], parts[1]), pair_rows(parts[2], None)], axis=1
    )


def product_kernel(rows_ref, mass_ref, out_ref, along_x_ref, along_y_ref, along_z_ref):
    parts = parts_of(rows_ref, 0)
    vectors = by_vector(parts)
    along_x_ref[...] = vectors[:, :128]
    along_y_ref[...] = pair_rows(parts[1], parts[2])
    along_z_ref[...] = pair_rows(parts[2], parts[0])
    image = by_vector(parts_of(rows_ref, 1))
    weighted = vectors * mass_ref[...]
    gram = dot(weighted, vectors, ((1,), (1,)))
    stiff = dot(vectors, image, ((1,), (1,)))
    row = lax.broadcasted_iota(jnp.int32, (256, 256), 0)
    column = lax.broadcasted_iota(jnp.int32, (256, 256), 1)
    both = jnp.where(row >= column, gram, stiff)
    diagonal = jnp.sum(vectors * image, axis=1, keepdims=True)
    lane = lax.broadcasted_iota(jnp.int32, (256, 128), 1)
    lateral = jnp.sum(jnp.where(lane < NODES, weighted[:, :128], 0.0), axis=1, keepdims=True)
    further = jnp.where(lane == 0, diagonal, jnp.where(lane == 1, lateral, 0.0)).T
    for chunk in range(32):
        half = slice(0, 128) if chunk < 16 else slice(128, 256)
        first = chunk % 16 * 16
        out_ref[chunk * CHUNK : chunk * CHUNK + 16, :] = both[first : first + 16, half]
        last = further[chunk // 2 : chunk // 2 + 1, chunk % 2 * 128 : chunk % 2 * 128 + 128]
        out_ref[chunk * CHUNK + 16 : chunk * CHUNK + 17, :] = last


def total_kernel(count, copies, rows_ref, out_ref):
    total = rows_ref[0:CHUNK, :]
    for place in range(1, count):
        total = total + rows_ref[place * CHUNK : place * CHUNK + CHUNK, :]
    for place in range(copies):
        out_ref[place * CHUNK : place * CHUNK + CHUNK, :] = total


def factor_block(gram, stiff):
    lane = lax.broadcasted_iota(jnp.int32, (BLOCK, 128), 1)
    row = lax.broadcasted_iota(jnp.int32, (BLOCK, 128), 0)
    low = lane < 64
    columns = [
        jnp.where(
            low,
            jnp.broadcast_to(gram[:, j : j + 1], (BLOCK, 128)),
            jnp.broadcast_to(stiff[:, j : j + 1], (BLOCK, 128)),
        )
        for j in range(BLOCK)
    ]
    inverse = jnp.where((lane & 63) == row, 1.0, 0.0)
    scale = jnp.ones((BLOCK, 128), jnp.float32)
    link = jnp.zeros((BLOCK, 128), jnp.float32)
    for k in range(0, BLOCK, 2):
        one, two = columns[k], columns[k + 1]
        top = one[k : k + 1, :]
        side = one[k + 1 : k + 2, :]
        corner = two[k + 1 : k + 2, :]
        rest = top * corner - side * side
        scale = jnp.where(row == k, top, jnp.where(row == k + 1, rest / top, scale))
        link = jnp.where(row == k + 1, side / top, link)
        if k + 2 == BLOCK:
            break
        part = (k + 2) // 8 * 8
        factor = 1.0 / rest
        below = row[part:] > k + 1
        first = jnp.where(below, (one[part:] * corner - two[part:] * side) * factor, 0.0)
        second = jnp.where(below, (two[part:] * top - one[part:] * side) * factor, 0.0)

        def reduced(value):
            tail = value[part:] - (first * value[k : k + 1, :] + second * value[k + 1 : k + 2, :])
            return tail if part == 0 else jnp.concatenate([value[:part], tail], axis=0)

        for j in range(k + 2, BLOCK):
            columns[j] = reduced(columns[j])
        inverse = reduced(inverse)
    inverse = inverse - link * pltpu.roll(inverse, 1, 0)
    return inverse * lax.rsqrt(scale), scale


def rounded(value):
    return value.astype(jnp.bfloat16).astype(jnp.float32)


def three_parts(value):
    high = rounded(value)
    rest = value - high
    middle = rounded(rest)
    return high, middle, rest - middle


def four_copies(value):
    return (value + pltpu.roll(value, 32, 1)) + (
        pltpu.roll(value, 64, 1) + pltpu.roll(value, 96, 1)
    )


def left_groups(first, second):
    group = lax.broadcasted_iota(jnp.int32, first.shape, 1) // BLOCK
    high, middle, _ = three_parts(first)
    parts = three_parts(second)
    one = jnp.where(group < 2, high, middle)
    two = jnp.where(group == 0, parts[0], jnp.where(group == 1, parts[2], 0.0))
    return jnp.concatenate([one, two], axis=1).astype(jnp.bfloat16)


def right_lanes(copies):
    group = lax.broadcasted_iota(jnp.int32, copies.shape, 1) // BLOCK
    high, middle, low = three_parts(copies)
    one = jnp.where(group % 2 == 0, high, middle)
    two = jnp.where(group == 0, low, high)
    return jnp.concatenate([one, two], axis=1).astype(jnp.bfloat16)


def right_rows(value):
    high, middle, low = [part.astype(jnp.bfloat16) for part in three_parts(value)]
    return jnp.concatenate([high, middle, high, middle, low, high, high, high], axis=0)


def product(left, right, contract):
    return lax.dot_general(
        left, right, (contract, ((), ())), preferred_element_type=jnp.float32
    )


def invert_factors(m_ref, diagonal):
    lane = lax.broadcasted_iota(jnp.int32, (BLOCK, 128), 1)
    least = jnp.ones((BLOCK, 128), jnp.float32)
    for first in range(0, 256, BLOCK):
        tile = first // 128 * 128
        inside = first - tile
        after = first + BLOCK
        small = [m_ref[m, first:after, tile : tile + 128][:, inside : inside + BLOCK] for m in (0, 1)]
        inverse, pivots = factor_block(small[0], small[1])
        least = jnp.minimum(least, pivots / diagonal[first:after, :])
        for m in (0, 1):
            own = four_copies(
                jnp.where((lane >= 64 * m) & (lane < 64 * m + BLOCK), inverse, 0.0)
            )
            row = lax.broadcasted_iota(jnp.int32, (BLOCK, 256), 0)
            column = lax.broadcasted_iota(jnp.int32, (BLOCK, 256), 1) - first
            rows = m_ref[m, first:after, :]
            unit = jnp.where(column == row, 1.0, 0.0)
            rows = jnp.where((column >= 0) & (column < BLOCK), unit, rows)
            result = product(left_groups(own, own), right_rows(rows), ((1,), (0,)))
            m_ref[m, first:after, :] = result
            if after < 256:
                count = 256 - after
                lanes = lax.broadcasted_iota(jnp.int32, (count, 128), 1)
                held = (lanes >= inside) & (lanes < inside + BLOCK)
                left = four_copies(jnp.where(held, m_ref[m, after:, tile : tile + 128], 0.0))
                right = jnp.concatenate([right_lanes(own)] * 8, axis=0)
                factor = product(left_groups(left, left), right, ((1,), (1,)))
                column = lax.broadcasted_iota(jnp.int32, (count, 256), 1)
                rows = m_ref[m, after:, :]
                rows = jnp.where((column >= first) & (column < after), 0.0, rows)
                m_ref[m, after:, :] = rows - product(
                    left_groups(factor[:, :128], factor[:, 128:]), right_rows(result), ((1,), (0,))
                )
    return jnp.min(least, axis=(0, 1), keepdims=True)


def final_kernel(
    sums_ref, rows_ref, above_x_ref, below_x_ref, above_y_ref, below_y_ref, above_z_ref,
    below_z_ref, mass_ref, modulus_ref, stress_ref, subspace_ref, projected_ref, force_ref,
    stress_new_ref, apart_ref, m_ref
):
    chunks = [sums_ref[chunk * CHUNK : chunk * CHUNK + 16, :] for chunk in range(32)]
    both = jnp.concatenate(
        [jnp.concatenate(chunks[:16], axis=0), jnp.concatenate(chunks[16:], axis=0)], axis=1
    )
    further = [
        jnp.broadcast_to(sums_ref[chunk * CHUNK + 16 : chunk * CHUNK + 17, :], (128, 128)).T
        for chunk in range(4)
    ]
    diagonal = jnp.concatenate(further[:2], axis=0)
    diagonal = jnp.concatenate([diagonal, diagonal], axis=1)
    lateral = jnp.concatenate(further[2:], axis=0)
    turned = both.T
    row = lax.broadcasted_iota(jnp.int32, (256, 256), 0)
    column = lax.broadcasted_iota(jnp.int32, (256, 256), 1)
    gram = jnp.where(row >= column, both, turned)
    stiff = jnp.where(row < column, both, jnp.where(row == column, diagonal, turned))
    m_ref[0] = gram
    m_ref[1] = stiff
    half = lax.broadcasted_iota(jnp.int32, (256, 128), 1) < 64
    gram_diagonal = jnp.sum(jnp.where(row == column, gram, 0.0), axis=1, keepdims=True)
    least = invert_factors(m_ref, jnp.where(half, gram_diagonal, diagonal[:, :128]))
    apart_ref[0, 0] = jnp.where(least[0, 0] > LEAST_PIVOT, 1, 0)
    lower = jnp.where(row >= column, m_ref[0], 0.0)
    stiff_lower = jnp.where(row >= column, m_ref[1], 0.0)
    vectors = by_vector(parts_of(rows_ref, 0))
    subspace = dot(vectors.T, lower, ((1,), (1,)))
    subspace = subspace * jnp.sqrt(jnp.float32(DEVICES * 3 * NODES))
    projected_ref[...] = dot(lower, dot(stiff, lower, ((1,), (1,))))
    weights = dot(stiff_lower.T, dot(stiff_lower, lateral))
    weights = jnp.concatenate([weights, weights], axis=1)
    displace = jnp.sum(vectors * weights, axis=0, keepdims=True)
    own = [displace[:, :128], pltpu.roll(displace[:, :128], 64, 1), displace[:, 128:]]
    outside = [
        jnp.sum(ref[...] * weights[:, :128], axis=0, keepdims=True)
        for ref in (above_x_ref, below_x_ref, above_y_ref, below_y_ref, above_z_ref, below_z_ref)
    ]
    lane = lax.broadcasted_iota(jnp.int32, (1, 128), 1)
    axial = []
    bending = []
    for direction, (step, mask) in enumerate(((32, 32), (1, 7), (8, 24))):
        wide = jnp.where(lane < 64, own[direction], pltpu.roll(own[(direction + 1) % 3], 64, 1))
        above = jnp.where(
            (lane & mask) == mask,
            pltpu.roll(outside[2 * direction], mask, 1),
            pltpu.roll(wide, 128 - step, 1),
        )
        below = jnp.where(
            (lane & mask) == 0,
            pltpu.roll(outside[2 * direction + 1], 128 - mask, 1),
            pltpu.roll(wide, step, 1),
        )
        axial.append(0.5 * (above - below))
        bending.append(pltpu.roll((above - 2.0 * wide) + below, 64, 1))
    lane = lax.broadcasted_iota(jnp.int32, (24, 256), 1)
    group = lax.broadcasted_iota(jnp.int32, (24, 256), 0)
    laid = jnp.where((lane >> 3) == group, displace * mass_ref[...], 0.0)
    column = lax.broadcasted_iota(jnp.int32, (256, 128), 0)
    place = lax.broadcasted_iota(jnp.int32, (256, 128), 1)
    force_ref[...] = dot(laid, jnp.where((column & 7) == place, 1.0, 0.0))[:, :8]
    columns = jnp.concatenate(
        axial + bending + [jnp.zeros((122, 128), jnp.float32)], axis=0
    ).T
    axial = [jnp.broadcast_to(columns[:, d : d + 1], (128, 16)) for d in range(3)]
    bending = [jnp.broadcast_to(columns[:, 3 + d : 4 + d], (128, 16)) for d in range(3)]
    fiber = lax.broadcasted_iota(jnp.int32, (8, 16), 1).astype(jnp.float32)
    heights = (fiber + 0.5) / 16.0 - 0.5
    for direction in range(3):
        for x in range(2):
            for z in range(4):
                rows = slice(direction * 16 + x * 8, direction * 16 + x * 8 + 8)
                inner = x * 32 + z * 8
                one = direction * NODES + inner
                subspace_ref[rows, z, :] = subspace[one : one + 8]
                strain = axial[direction][inner : inner + 8]
                strain = strain + heights * bending[direction][inner : inner + 8]
                stress_new_ref[rows, z, :] = stress_ref[rows, z, :] + modulus_ref[rows, z, :] * strain


def fiber_modulus(stiffness, yield_flags):
    own = jnp.stack([stiffness[d, d] for d in range(3)])[:, None]
    return own * jnp.where(yield_flags == 1, 0.05, 1.0)


def extended(block, first_dim):
    for place, axis in enumerate((GX, "gy", "gz")):
        dim = first_dim + place
        count = lax.axis_size(axis)
        forward = [(i, i + 1) for i in range(count - 1)]
        backward = [(target, source) for source, target in forward]
        last = block.shape[dim]
        low = lax.ppermute(lax.slice_in_dim(block, last - 1, last, axis=dim), axis, forward)
        high = lax.ppermute(lax.slice_in_dim(block, 0, 1, axis=dim), axis, backward)
        block = jnp.concatenate([low, block, high], axis=dim)
    return block


def neighbour(padded, leading, direction, sense):
    slicer = [slice(None)] * padded.ndim
    for position in range(3):
        slicer[leading + position] = slice(1, -1)
    slicer[leading + direction] = slice(2, None) if sense > 0 else slice(0, -2)
    return padded[tuple(slicer)]


def summed(square):
    rows = jnp.concatenate([square[:, :128], square[:, 128:]], axis=0)
    for axes, count, copies in ((("cy", "gy"), 32, 16), (("core", "gz"), 16, 32)):
        rows = jnp.sum(exchange(rows, axes, count).reshape(count, 16, 128), axis=0)
        rows = jnp.tile(rows, (copies, 1))
    rows = exchange(rows, ("cy", "gy"), 32)
    return jnp.concatenate([rows[:256], rows[256:]], axis=1)


def step_by_step(start_block, node_mass, ground_spring, stiffness, yield_flags, stress_old):
    share = jnp.mean(yield_flags.astype(jnp.float32), axis=1)
    tangent = stiffness * (1.0 - 0.9 * share)[:, None]
    padded = extended(tangent, 2)
    edges = [
        [0.5 * (tangent[d] + neighbour(padded, 2, d, sense)[d]) for d in range(3)]
        for sense in (1, -1)
    ]
    edge_total = sum(edges[0]) + sum(edges[1])
    diagonal = ground_spring + edge_total
    top = jnp.broadcast_to(jnp.max((diagonal + edge_total) / node_mass), (128, 128))
    for axes, count in ((("cy", "core"), 16), ("gy", 4), ("gz", 8)):
        top = jnp.broadcast_to(jnp.max(exchange(top, axes, count)), (128, 128))
    top = top[0, 0]
    middle = top * 9.0 / 16.0
    spread = top * 7.0 / 16.0

    def apply_k(field):
        around_field = extended(field, 1)
        result = diagonal[..., None] * field
        for d in range(3):
            for sense, weights in ((1, edges[0]), (-1, edges[1])):
                result = result - weights[d][..., None] * neighbour(around_field, 1, d, sense)
        return result

    def shifted(field):
        return (apply_k(field) / node_mass[..., None] - middle * field) / spread

    width = start_block.shape[-1]
    mass_rows = node_mass.reshape(-1)
    vectors = start_block
    for turn in range(ITERS):
        earlier, current = vectors, shifted(vectors)
        for repeat in range(DEGREE - 1):
            earlier, current = current, 2.0 * shifted(current) - earlier
        flat_rows = current.reshape(-1, width)
        gram = summed(dot(flat_rows.T, mass_rows[:, None] * flat_rows))
        factor = jnp.linalg.cholesky(gram)
        basis = lax.linalg.triangular_solve(factor, flat_rows.T, left_side=True, lower=True)
        vectors = basis.T.reshape(current.shape)
    image = apply_k(vectors).reshape(-1, width)
    projected = summed(dot(basis, image))
    lateral = dot(basis[:, :NODES], mass_rows[:NODES, None])
    lateral = summed(jnp.broadcast_to(lateral, (width, width)))[:, :1]
    factor = jnp.linalg.cholesky(projected)
    halfway = lax.linalg.triangular_solve(factor, lateral, left_side=True, lower=True)
    weights = lax.linalg.triangular_solve(
        factor, halfway, left_side=True, lower=True, transpose_a=True
    )
    displace = dot(weights.T, basis).reshape(node_mass.shape)
    padded = extended(displace, 1)
    axial = []
    bending = []
    for d in range(3):
        above = neighbour(padded, 1, d, 1)
        below = neighbour(padded, 1, d, -1)
        other = (d + 1) % 3
        axial.append(0.5 * (above[d] - below[d]))
        bending.append(above[other] - 2.0 * displace[other] + below[other])
    fibers = stress_old.shape[1]
    heights = ((jnp.arange(fibers).astype(jnp.float32) + 0.5) / fibers - 0.5)[:, None, None, None]
    strain = jnp.stack(axial)[:, None] + heights * jnp.stack(bending)[:, None]
    stress_new = stress_old + fiber_modulus(stiffness, yield_flags) * strain
    subspace = vectors * jnp.sqrt(jnp.float32(DEVICES * 3 * NODES))
    return subspace, projected, node_mass * displace, stress_new


def call(kernel, shape, scratch=(), smem=(), operands=(), smem_out=()):
    results = len(shape) if isinstance(shape, tuple) else 1
    out_specs = tuple(
        pl.BlockSpec(memory_space=pltpu.SMEM if place in smem_out else pltpu.VMEM)
        for place in range(results)
    )
    return pl.pallas_call(
        kernel,
        out_shape=shape,
        in_specs=[
            pl.BlockSpec(memory_space=pltpu.SMEM if place in smem else pltpu.VMEM)
            for place in range(len(operands))
        ],
        out_specs=out_specs if isinstance(shape, tuple) else out_specs[0],
        scratch_shapes=list(scratch),
        compiler_params=pltpu.CompilerParams(vmem_limit_bytes=40 * 1024 * 1024),
    )(*operands)


def rows_of(count):
    return jax.ShapeDtypeStruct((count, 128), jnp.float32)


def exchange(rows, axes, devices):
    per_device = rows.shape[0] // devices
    if per_device % 8 == 0:
        blocks = rows.reshape(devices, per_device, 128)
    else:
        blocks = rows.reshape(devices, per_device, 1, 128)
    return lax.all_to_all(blocks, axes, 0, 0, tiled=True).reshape(rows.shape)


def chebyshev_nodes():
    count = TOTAL + 1
    angles = np.pi * (np.arange(count) + 0.5) / count
    plain = np.zeros((count, count))
    timesx = np.zeros((count + 1, count))
    for degree in range(count):
        plain[degree] = (2.0 if degree else 1.0) / count * np.cos(degree * angles)
        timesx[degree + 1] += plain[degree] * (0.5 if degree else 1.0)
        if degree:
            timesx[degree - 1] += plain[degree] * 0.5
    table = np.zeros((40, 128), np.float32)
    table[0, :count] = np.cos(angles)
    table[8 : 8 + count, :count] = plain
    table[24 : 25 + count, :count] = timesx
    return jnp.asarray(table)


def on_device(start_block, node_mass, ground_spring, stiffness, yield_flags, stress_old):
    width = start_block.shape[-1]
    fibers = stress_old.shape[1]

    def node_rows(value):
        return jnp.swapaxes(value, -1, -2).reshape(-1, 8)

    def fibers_last(value):
        return jnp.moveaxis(value, 1, -1).reshape(48, 4, fibers)

    grid_shape = (16, 4, 8, 128)
    plain = pltpu.VMEM(grid_shape, jnp.float32)
    planes_shape = (16, KINDS, 4, 8, 128)
    sent = call(
        pack_kernel,
        rows_of(256 * OUT_ROWS),
        operands=(
            start_block.reshape(48, 4, width),
            node_rows(stiffness),
            node_rows(node_mass),
            node_rows(ground_spring),
            fibers_last(yield_flags).reshape(3 * NODES, fibers),
        ),
    )
    own = exchange(sent, CHIPS, 256)
    other = lax.ppermute(own, "core", [(0, 1), (1, 0)])
    core = lax.axis_index("core").astype(jnp.int32).reshape(1)
    planes, own_top = call(
        weights_kernel,
        (jax.ShapeDtypeStruct(planes_shape, jnp.float32), rows_of(32)),
        (plain,),
        smem=(0,),
        operands=(core, own, other),
    )
    tops = exchange(own_top, "gy", 4)
    terms = call(
        filter_kernel,
        jax.ShapeDtypeStruct((TOTAL + 3,) + grid_shape, jnp.float32),
        (plain,),
        operands=(planes, own_top),
    )
    filtered = call(
        combine_kernel,
        rows_of(1024),
        operands=(terms, own_top, tops, chebyshev_nodes()),
    )
    returned = exchange(filtered, AXES, DEVICES)
    mass_row = node_rows(node_mass).reshape(1, 3 * NODES)
    mass_row = jnp.pad(mass_row, ((0, 0), (0, NODES)))
    along = jax.ShapeDtypeStruct((width, 128), jnp.float32)
    products, *along = call(
        product_kernel,
        (rows_of(32 * CHUNK), along, along, along),
        operands=(returned, mass_row),
    )

    def from_neighbours(mine, axis, senses):
        count = lax.axis_size(axis)
        pairs = [(i, i + 1) for i in range(count - 1)]
        return [
            lax.ppermute(mine, axis, [(b, a) for a, b in pairs] if sense > 0 else pairs)
            for sense in senses
        ]

    near = from_neighbours(along[0], GX, (1, -1)) + from_neighbours(along[1], "gy", (1,))
    part = exchange(products, ("cy", "gy"), 32)
    part, *near = lax.optimization_barrier((part, *near))
    part = call(functools.partial(total_kernel, 32, 16), rows_of(16 * CHUNK), operands=(part,))
    part, along[1] = lax.optimization_barrier((part, along[1]))
    near += from_neighbours(along[1], "gy", (-1,))
    part = exchange(part, ("core", "gz"), 16)
    part, *near = lax.optimization_barrier((part, *near))
    part = call(functools.partial(total_kernel, 16, 32), rows_of(32 * CHUNK), operands=(part,))
    part, along[2] = lax.optimization_barrier((part, along[2]))
    far = from_neighbours(along[2], "gz", (1, -1))
    part = exchange(part, ("cy", "gy"), 32)
    part, *far = lax.optimization_barrier((part, *far))
    subspace, projected, force, stress_new, apart = call(
        final_kernel,
        (
            jax.ShapeDtypeStruct((48, 4, width), jnp.float32),
            jax.ShapeDtypeStruct((width, width), jnp.float32),
            jax.ShapeDtypeStruct((24, 8), jnp.float32),
            jax.ShapeDtypeStruct((48, 4, fibers), jnp.float32),
            jax.ShapeDtypeStruct((1, 1), jnp.int32),
        ),
        (pltpu.VMEM((2, 256, 256), jnp.float32),),
        operands=(
            part,
            returned,
            *near,
            *far,
            mass_row,
            fibers_last(fiber_modulus(stiffness, yield_flags)),
            fibers_last(stress_old),
        ),
        smem_out=(4,),
    )
    place = node_mass.shape[1:]
    force = jnp.swapaxes(force.reshape(3, place[0], place[2], place[1]), -1, -2)
    stress_new = jnp.moveaxis(stress_new.reshape((3,) + place + (fibers,)), -1, 1)
    return lax.switch(
        apart[0, 0],
        (lambda *operands: step_by_step(*operands[4:]), lambda *operands: operands[:4]),
        subspace.reshape(start_block.shape),
        projected,
        force,
        stress_new,
        start_block,
        node_mass,
        ground_spring,
        stiffness,
        yield_flags,
        stress_old,
    )


def solution(mesh):
    chips = Mesh(mesh.devices.reshape(8, 2, 4, 8), AXES)
    return jax.shard_map(
        on_device,
        mesh=chips,
        in_specs=(
            P(None, GX, "gy", "gz", None),
            P(None, GX, "gy", "gz"),
            P(None, GX, "gy", "gz"),
            P(None, None, GX, "gy", "gz"),
            P(None, None, GX, "gy", "gz"),
            P(None, None, GX, "gy", "gz"),
        ),
        out_specs=(
            P(None, GX, "gy", "gz", None),
            P(),
            P(None, GX, "gy", "gz"),
            P(None, None, GX, "gy", "gz"),
        ),
        check_vma=False,
    )
```

```python
import functools

import jax
import jax.numpy as jnp
import numpy as np
from jax import lax
from jax.experimental import pallas as pl
from jax.experimental.pallas import tpu as pltpu
from jax.sharding import Mesh, PartitionSpec as P

DEGREE = 4
ITERS = 2
TOTAL = DEGREE * ITERS
PRECISE = lax.Precision.HIGHEST
GX = ("cy", "core")
AXES = ("cy", "core", "gy", "gz")
CHIPS = ("cy", "gy", "gz")

NODES = 64
DEVICES = 512
OUT_ROWS = 5
LEAST_PIVOT = 0.1
BLOCK = 32
CHUNK = 17
LEAST_PIVOT = 0.1
BLOCK = 32
STIFF_LANE = 9
MASS_LANE = 10


def dot(a, b, contract=((1,), (0,))):
    return lax.dot_general(
        a, b, (contract, ((), ())), precision=PRECISE, preferred_element_type=jnp.float32
    )


def spread_nodes(values, keep):
    groups = jnp.where(keep, values.reshape((-1,) + keep.shape), 0.0)
    return jnp.sum(groups, axis=1)


def pack_kernel(start_ref, stiffness_ref, mass_ref, spring_ref, flags_ref, out_ref):
    lane = lax.broadcasted_iota(jnp.int32, (8, 128), 1)
    place = lax.broadcasted_iota(jnp.int32, (8, 128), 0)
    repeated = jnp.where((lane & 7) == place, 1.0, 0.0)
    keep = ((lane >> 3) & 7) == place
    stiffness = spread_nodes(dot(stiffness_ref[...], repeated), keep)
    masses = spread_nodes(dot(mass_ref[...], repeated), keep)
    springs = spread_nodes(dot(spring_ref[...], repeated), keep)
    counts = jnp.dot(
        flags_ref[...].astype(jnp.bfloat16),
        jnp.ones((16, 128), jnp.bfloat16),
        preferred_element_type=jnp.float32,
    )
    lane = lax.broadcasted_iota(jnp.int32, (NODES, 128), 1)
    place = lax.broadcasted_iota(jnp.int32, (NODES, 128), 0)
    own = ((place >> 5) * 32 + (place & 3) * 8 + ((place >> 2) & 7)) == (lane & 63)
    softening = 1.0 - 0.9 * (spread_nodes(counts, own) / 16.0)
    low = lax.broadcasted_iota(jnp.int32, (1, 128), 1) < 64
    for comp in range(4):
        source = comp % 3
        if comp < 3:
            block = jnp.concatenate(
                [
                    start_ref[comp * 16 + x * 8 : comp * 16 + x * 8 + 8, z, :]
                    for x in range(2)
                    for z in range(4)
                ],
                axis=0,
            )
            pairs = jnp.concatenate([block[:, :128], block[:, 128:]], axis=0).T
        else:
            pairs = jnp.zeros((128, 128), jnp.float32)
        tangent = [
            stiffness[3 * d + source : 3 * d + source + 1, :] * softening[d : d + 1, :]
            for d in range(3)
        ]
        mass = masses[source : source + 1, :]
        spring = springs[source : source + 1, :]
        rows = [
            jnp.broadcast_to(row, (8, 128))
            for row in (
                jnp.where(low, tangent[0], tangent[1]),
                jnp.where(low, tangent[2], mass),
                spring,
            )
        ]
        for cy in range(8):
            first = (cy * 4 + comp) * 8 * OUT_ROWS
            for core in range(2):
                at = (cy * 2 + core) * 8
                out_ref[pl.ds(first + core, 8, stride=OUT_ROWS), :] = pairs[at : at + 8]
            for r in range(3):
                out_ref[pl.ds(first + 2 + r, 8, stride=OUT_ROWS), :] = rows[r]


def iota(axis):
    return lax.broadcasted_iota(jnp.int32, (4, 8, 128), axis)


def grid_row(refs, kind, gx, core):
    rows = [ref[pl.ds(gx // 2 * 32 * OUT_ROWS + kind, 32, stride=OUT_ROWS), :] for ref in refs]
    return jnp.where(core == gx % 2, rows[0], rows[1]).reshape(4, 8, 128)


def roll(value, shift, axis=2):
    return pltpu.roll(value, shift, axis)


def both_halves(value):
    lane = iota(2)
    turned = roll(value, 64)
    return jnp.where(lane < 64, value, turned), jnp.where(lane < 64, turned, value)


class Turned:
    def __init__(self, ref):
        self.ref = ref
        self.planes = {}

    def at(self, gx):
        if gx not in self.planes:
            if gx in (-1, 16):
                zero = jnp.zeros((4, 8, 128), jnp.float32)
                self.planes[gx] = (zero, zero)
            else:
                here = self.ref[gx]
                self.planes[gx] = (roll(here, 96), roll(here, 32))
        return self.planes[gx]

    def sides(self, gx):
        first = (iota(2) & 32) == 0
        up = jnp.where(first, self.at(gx)[0], self.at(gx + 1)[1])
        down = jnp.where(first, self.at(gx - 1)[0], self.at(gx)[1])
        return up, down


def y_up(here):
    moved = jnp.concatenate([here[1:], jnp.zeros((1, 8, 128), jnp.float32)], axis=0)
    return jnp.where((iota(2) & 7) != 7, roll(here, 127), roll(moved, 7))


def y_down(here):
    moved = jnp.concatenate([jnp.zeros((1, 8, 128), jnp.float32), here[:-1]], axis=0)
    return jnp.where((iota(2) & 7) != 0, roll(here, 1), roll(moved, 121))


def z_up(here):
    other = jnp.where(iota(1) < 7, roll(roll(here, 24), 7, 1), 0.0)
    return jnp.where((iota(2) & 24) != 24, roll(here, 120), other)


def z_down(here):
    other = jnp.where(iota(1) > 0, roll(roll(here, 104), 1, 1), 0.0)
    return jnp.where((iota(2) & 24) != 0, roll(here, 8), other)


def around(ref, turned, gx):
    here = ref[gx]
    return here, (turned.sides(gx), (y_up(here), y_down(here)), (z_up(here), z_down(here)))


UP, DOWN, DIAGONAL, MASS, KINDS = 1, 4, 7, 8, 9


def weights_kernel(
    core_ref, own_ref, other_ref, held_ref, top_ref, tangent_ref
):
    core = core_ref[0]
    refs = (own_ref, other_ref)
    second = []
    for gx in range(16):
        held_ref[gx, 0] = grid_row(refs, core, gx, core)
        first, along_y = both_halves(grid_row(refs, 2, gx, core))
        tangent_ref[gx] = first
        second.append(along_y)
    turned = Turned(tangent_ref)
    best = jnp.zeros((4, 8, 128), jnp.float32)
    for gx in range(16):
        first = tangent_ref[gx]
        above, below = turned.sides(gx)
        third, mass = both_halves(grid_row(refs, 3, gx, core))
        spring = grid_row(refs, 4, gx, core)
        ups = [
            0.5 * (first + above),
            0.5 * (second[gx] + y_up(second[gx])),
            0.5 * (third + z_up(third)),
        ]
        downs = [
            0.5 * (first + below),
            0.5 * (second[gx] + y_down(second[gx])),
            0.5 * (third + z_down(third)),
        ]
        total = (ups[0] + ups[1] + ups[2]) + (downs[0] + downs[1] + downs[2])
        for direction in range(3):
            held_ref[gx, UP + direction] = ups[direction]
            held_ref[gx, DOWN + direction] = downs[direction]
        diagonal = spring + total
        held_ref[gx, DIAGONAL] = diagonal
        held_ref[gx, MASS] = mass
        best = jnp.maximum(best, (diagonal + total) / mass)
    best = jnp.max(jnp.max(best, axis=0), axis=(0, 1), keepdims=True)
    top_ref[...] = jnp.broadcast_to(best, (32, 128))


def filter_kernel(held_ref, top_ref, terms_ref, inverse_ref):
    top = top_ref[0:1, :]
    inverse_spread = 1.0 / (top * 7.0 / 16.0)
    ratio = (top * 9.0 / 16.0) * inverse_spread
    for gx in range(16):
        mass = held_ref[gx, MASS]
        inverse_ref[gx] = inverse_spread / mass
        terms_ref[0, gx] = held_ref[gx, 0]
        terms_ref[TOTAL + 2, gx] = mass
    for degree in range(1, TOTAL + 2):
        current_ref = terms_ref.at[degree - 1]
        turned = Turned(current_ref)
        for gx in range(16):
            here, sides = around(current_ref, turned, gx)
            image = held_ref[gx, DIAGONAL] * here
            for direction in range(3):
                image = image - held_ref[gx, UP + direction] * sides[direction][0]
                image = image - held_ref[gx, DOWN + direction] * sides[direction][1]
            image = image * inverse_ref[gx] - ratio * here
            if degree > 1:
                image = 2.0 * image - terms_ref[degree - 2, gx]
            terms_ref[degree, gx] = image


def combine_kernel(terms_ref, own_top_ref, top_ref, nodes_ref, out_ref):
    top = jnp.max(jnp.max(top_ref[...], axis=0, keepdims=True), axis=1, keepdims=True)
    own_top = own_top_ref[0:1, :]
    part = own_top / top
    place = part * nodes_ref[0:1, :] + (part - 1.0) * (9.0 / 7.0)
    square = place * place
    once = 8.0 * square * square - 8.0 * square + 1.0
    coefficients = jnp.sum(nodes_ref[8:40, :] * (once * once), axis=1, keepdims=True)
    middle = own_top * 9.0 / 16.0
    spread = own_top * 7.0 / 16.0
    for gx in range(16):
        total = coefficients[0:1, :] * terms_ref[0, gx]
        scaled = coefficients[16:17, :] * terms_ref[0, gx]
        for degree in range(1, TOTAL + 2):
            term = terms_ref[degree, gx]
            if degree <= TOTAL:
                total = total + coefficients[degree : degree + 1, :] * term
            scaled = scaled + coefficients[16 + degree : 17 + degree, :] * term
        image = terms_ref[TOTAL + 2, gx] * (middle * total + spread * scaled)
        out_ref[pl.ds(gx * 64, 32, stride=2), :] = total.reshape(32, 128)
        out_ref[pl.ds(gx * 64 + 1, 32, stride=2), :] = image.reshape(32, 128)


def parts_of(rows_ref, kind):
    return [
        jnp.concatenate(
            [rows_ref[pl.ds((gx * 4 + comp) * 16 + kind, 8, stride=2), :] for gx in range(16)],
            axis=0,
        )
        for comp in range(3)
    ]


def pair_rows(one, two):
    low = lax.broadcasted_iota(jnp.int32, (128, 128), 1) < 64
    upper = jnp.where(low, one, 0.0 if two is None else pltpu.roll(two, 64, 1))
    lower = jnp.where(low, pltpu.roll(one, 64, 1), 0.0 if two is None else two)
    return jnp.concatenate([upper, lower], axis=0)


def by_vector(parts):
    return jnp.concatenate(
        [pair_rows(parts[0], parts[1]), pair_rows(parts[2], None)], axis=1
    )


def product_kernel(rows_ref, mass_ref, out_ref, along_x_ref, along_y_ref, along_z_ref):
    parts = parts_of(rows_ref, 0)
    vectors = by_vector(parts)
    along_x_ref[...] = vectors[:, :128]
    along_y_ref[...] = pair_rows(parts[1], parts[2])
    along_z_ref[...] = pair_rows(parts[2], parts[0])
    image = by_vector(parts_of(rows_ref, 1))
    weighted = vectors * mass_ref[...]
    gram = dot(weighted, vectors, ((1,), (1,)))
    stiff = dot(vectors, image, ((1,), (1,)))
    row = lax.broadcasted_iota(jnp.int32, (256, 256), 0)
    column = lax.broadcasted_iota(jnp.int32, (256, 256), 1)
    both = jnp.where(row >= column, gram, stiff)
    diagonal = jnp.sum(vectors * image, axis=1, keepdims=True)
    lane = lax.broadcasted_iota(jnp.int32, (256, 128), 1)
    lateral = jnp.sum(jnp.where(lane < NODES, weighted[:, :128], 0.0), axis=1, keepdims=True)
    further = jnp.where(lane == 0, diagonal, jnp.where(lane == 1, lateral, 0.0)).T
    for chunk in range(32):
        half = slice(0, 128) if chunk < 16 else slice(128, 256)
        first = chunk % 16 * 16
        out_ref[chunk * CHUNK : chunk * CHUNK + 16, :] = both[first : first + 16, half]
        last = further[chunk // 2 : chunk // 2 + 1, chunk % 2 * 128 : chunk % 2 * 128 + 128]
        out_ref[chunk * CHUNK + 16 : chunk * CHUNK + 17, :] = last


def total_kernel(count, copies, rows_ref, out_ref):
    total = rows_ref[0:CHUNK, :]
    for place in range(1, count):
        total = total + rows_ref[place * CHUNK : place * CHUNK + CHUNK, :]
    for place in range(copies):
        out_ref[place * CHUNK : place * CHUNK + CHUNK, :] = total


def factor_block(gram, stiff):
    lane = lax.broadcasted_iota(jnp.int32, (BLOCK, 128), 1)
    row = lax.broadcasted_iota(jnp.int32, (BLOCK, 128), 0)
    low = lane < 64
    columns = [
        jnp.where(
            low,
            jnp.broadcast_to(gram[:, j : j + 1], (BLOCK, 128)),
            jnp.broadcast_to(stiff[:, j : j + 1], (BLOCK, 128)),
        )
        for j in range(BLOCK)
    ]
    inverse = jnp.where((lane & 63) == row, 1.0, 0.0)
    scale = jnp.ones((BLOCK, 128), jnp.float32)
    link = jnp.zeros((BLOCK, 128), jnp.float32)
    for k in range(0, BLOCK, 2):
        one, two = columns[k], columns[k + 1]
        top = one[k : k + 1, :]
        side = one[k + 1 : k + 2, :]
        corner = two[k + 1 : k + 2, :]
        rest = top * corner - side * side
        scale = jnp.where(row == k, top, jnp.where(row == k + 1, rest / top, scale))
        link = jnp.where(row == k + 1, side / top, link)
        if k + 2 == BLOCK:
            break
        part = (k + 2) // 8 * 8
        factor = 1.0 / rest
        below = row[part:] > k + 1
        first = jnp.where(below, (one[part:] * corner - two[part:] * side) * factor, 0.0)
        second = jnp.where(below, (two[part:] * top - one[part:] * side) * factor, 0.0)

        def reduced(value):
            tail = value[part:] - (first * value[k : k + 1, :] + second * value[k + 1 : k + 2, :])
            return tail if part == 0 else jnp.concatenate([value[:part], tail], axis=0)

        for j in range(k + 2, BLOCK):
            columns[j] = reduced(columns[j])
        inverse = reduced(inverse)
    inverse = inverse - link * pltpu.roll(inverse, 1, 0)
    return inverse * lax.rsqrt(scale), scale


def rounded(value):
    return value.astype(jnp.bfloat16).astype(jnp.float32)


def three_parts(value):
    high = rounded(value)
    rest = value - high
    middle = rounded(rest)
    return high, middle, rest - middle


def four_copies(value):
    return (value + pltpu.roll(value, 32, 1)) + (
        pltpu.roll(value, 64, 1) + pltpu.roll(value, 96, 1)
    )


def left_groups(first, second):
    group = lax.broadcasted_iota(jnp.int32, first.shape, 1) // BLOCK
    high, middle, _ = three_parts(first)
    parts = three_parts(second)
    one = jnp.where(group < 2, high, middle)
    two = jnp.where(group == 0, parts[0], jnp.where(group == 1, parts[2], 0.0))
    return jnp.concatenate([one, two], axis=1).astype(jnp.bfloat16)


def right_lanes(copies):
    group = lax.broadcasted_iota(jnp.int32, copies.shape, 1) // BLOCK
    high, middle, low = three_parts(copies)
    one = jnp.where(group % 2 == 0, high, middle)
    two = jnp.where(group == 0, low, high)
    return jnp.concatenate([one, two], axis=1).astype(jnp.bfloat16)


def right_rows(value):
    high, middle, low = [part.astype(jnp.bfloat16) for part in three_parts(value)]
    return jnp.concatenate([high, middle, high, middle, low, high, high, high], axis=0)


def product(left, right, contract):
    return lax.dot_general(
        left, right, (contract, ((), ())), preferred_element_type=jnp.float32
    )


def invert_factors(m_ref, diagonal):
    lane = lax.broadcasted_iota(jnp.int32, (BLOCK, 128), 1)
    least = jnp.ones((BLOCK, 128), jnp.float32)
    for first in range(0, 256, BLOCK):
        tile = first // 128 * 128
        inside = first - tile
        after = first + BLOCK
        small = [m_ref[m, first:after, tile : tile + 128][:, inside : inside + BLOCK] for m in (0, 1)]
        inverse, pivots = factor_block(small[0], small[1])
        least = jnp.minimum(least, pivots / diagonal[first:after, :])
        for m in (0, 1):
            own = four_copies(
                jnp.where((lane >= 64 * m) & (lane < 64 * m + BLOCK), inverse, 0.0)
            )
            row = lax.broadcasted_iota(jnp.int32, (BLOCK, 256), 0)
            column = lax.broadcasted_iota(jnp.int32, (BLOCK, 256), 1) - first
            rows = m_ref[m, first:after, :]
            unit = jnp.where(column == row, 1.0, 0.0)
            rows = jnp.where((column >= 0) & (column < BLOCK), unit, rows)
            result = product(left_groups(own, own), right_rows(rows), ((1,), (0,)))
            m_ref[m, first:after, :] = result
            if after < 256:
                count = 256 - after
                lanes = lax.broadcasted_iota(jnp.int32, (count, 128), 1)
                held = (lanes >= inside) & (lanes < inside + BLOCK)
                left = four_copies(jnp.where(held, m_ref[m, after:, tile : tile + 128], 0.0))
                right = jnp.concatenate([right_lanes(own)] * 8, axis=0)
                factor = product(left_groups(left, left), right, ((1,), (1,)))
                column = lax.broadcasted_iota(jnp.int32, (count, 256), 1)
                rows = m_ref[m, after:, :]
                rows = jnp.where((column >= first) & (column < after), 0.0, rows)
                m_ref[m, after:, :] = rows - product(
                    left_groups(factor[:, :128], factor[:, 128:]), right_rows(result), ((1,), (0,))
                )
    return jnp.min(least, axis=(0, 1), keepdims=True)


def final_kernel(
    sums_ref, rows_ref, above_x_ref, below_x_ref, above_y_ref, below_y_ref, above_z_ref,
    below_z_ref, mass_ref, modulus_ref, stress_ref, subspace_ref, projected_ref, force_ref,
    stress_new_ref, apart_ref, m_ref
):
    chunks = [sums_ref[chunk * CHUNK : chunk * CHUNK + 16, :] for chunk in range(32)]
    both = jnp.concatenate(
        [jnp.concatenate(chunks[:16], axis=0), jnp.concatenate(chunks[16:], axis=0)], axis=1
    )
    further = [
        jnp.broadcast_to(sums_ref[chunk * CHUNK + 16 : chunk * CHUNK + 17, :], (128, 128)).T
        for chunk in range(4)
    ]
    diagonal = jnp.concatenate(further[:2], axis=0)
    diagonal = jnp.concatenate([diagonal, diagonal], axis=1)
    lateral = jnp.concatenate(further[2:], axis=0)
    turned = both.T
    row = lax.broadcasted_iota(jnp.int32, (256, 256), 0)
    column = lax.broadcasted_iota(jnp.int32, (256, 256), 1)
    gram = jnp.where(row >= column, both, turned)
    stiff = jnp.where(row < column, both, jnp.where(row == column, diagonal, turned))
    m_ref[0] = gram
    m_ref[1] = stiff
    half = lax.broadcasted_iota(jnp.int32, (256, 128), 1) < 64
    gram_diagonal = jnp.sum(jnp.where(row == column, gram, 0.0), axis=1, keepdims=True)
    least = invert_factors(m_ref, jnp.where(half, gram_diagonal, diagonal[:, :128]))
    apart_ref[0, 0] = jnp.where(least[0, 0] > LEAST_PIVOT, 1, 0)
    lower = jnp.where(row >= column, m_ref[0], 0.0)
    stiff_lower = jnp.where(row >= column, m_ref[1], 0.0)
    vectors = by_vector(parts_of(rows_ref, 0))
    subspace = dot(vectors.T, lower, ((1,), (1,)))
    subspace = subspace * jnp.sqrt(jnp.float32(DEVICES * 3 * NODES))
    projected_ref[...] = dot(lower, dot(stiff, lower, ((1,), (1,))))
    weights = dot(stiff_lower.T, dot(stiff_lower, lateral))
    weights = jnp.concatenate([weights, weights], axis=1)
    displace = jnp.sum(vectors * weights, axis=0, keepdims=True)
    own = [displace[:, :128], pltpu.roll(displace[:, :128], 64, 1), displace[:, 128:]]
    outside = [
        jnp.sum(ref[...] * weights[:, :128], axis=0, keepdims=True)
        for ref in (above_x_ref, below_x_ref, above_y_ref, below_y_ref, above_z_ref, below_z_ref)
    ]
    lane = lax.broadcasted_iota(jnp.int32, (1, 128), 1)
    axial = []
    bending = []
    for direction, (step, mask) in enumerate(((32, 32), (1, 7), (8, 24))):
        wide = jnp.where(lane < 64, own[direction], pltpu.roll(own[(direction + 1) % 3], 64, 1))
        above = jnp.where(
            (lane & mask) == mask,
            pltpu.roll(outside[2 * direction], mask, 1),
            pltpu.roll(wide, 128 - step, 1),
        )
        below = jnp.where(
            (lane & mask) == 0,
            pltpu.roll(outside[2 * direction + 1], 128 - mask, 1),
            pltpu.roll(wide, step, 1),
        )
        axial.append(0.5 * (above - below))
        bending.append(pltpu.roll((above - 2.0 * wide) + below, 64, 1))
    lane = lax.broadcasted_iota(jnp.int32, (24, 256), 1)
    group = lax.broadcasted_iota(jnp.int32, (24, 256), 0)
    laid = jnp.where((lane >> 3) == group, displace * mass_ref[...], 0.0)
    column = lax.broadcasted_iota(jnp.int32, (256, 128), 0)
    place = lax.broadcasted_iota(jnp.int32, (256, 128), 1)
    force_ref[...] = dot(laid, jnp.where((column & 7) == place, 1.0, 0.0))[:, :8]
    columns = jnp.concatenate(
        axial + bending + [jnp.zeros((122, 128), jnp.float32)], axis=0
    ).T
    axial = [jnp.broadcast_to(columns[:, d : d + 1], (128, 16)) for d in range(3)]
    bending = [jnp.broadcast_to(columns[:, 3 + d : 4 + d], (128, 16)) for d in range(3)]
    fiber = lax.broadcasted_iota(jnp.int32, (8, 16), 1).astype(jnp.float32)
    heights = (fiber + 0.5) / 16.0 - 0.5
    for direction in range(3):
        for x in range(2):
            for z in range(4):
                rows = slice(direction * 16 + x * 8, direction * 16 + x * 8 + 8)
                inner = x * 32 + z * 8
                one = direction * NODES + inner
                subspace_ref[rows, z, :] = subspace[one : one + 8]
                strain = axial[direction][inner : inner + 8]
                strain = strain + heights * bending[direction][inner : inner + 8]
                stress_new_ref[rows, z, :] = stress_ref[rows, z, :] + modulus_ref[rows, z, :] * strain


def fiber_modulus(stiffness, yield_flags):
    own = jnp.stack([stiffness[d, d] for d in range(3)])[:, None]
    return own * jnp.where(yield_flags == 1, 0.05, 1.0)


def extended(block, first_dim):
    for place, axis in enumerate((GX, "gy", "gz")):
        dim = first_dim + place
        count = lax.axis_size(axis)
        forward = [(i, i + 1) for i in range(count - 1)]
        backward = [(target, source) for source, target in forward]
        last = block.shape[dim]
        low = lax.ppermute(lax.slice_in_dim(block, last - 1, last, axis=dim), axis, forward)
        high = lax.ppermute(lax.slice_in_dim(block, 0, 1, axis=dim), axis, backward)
        block = jnp.concatenate([low, block, high], axis=dim)
    return block


def neighbour(padded, leading, direction, sense):
    slicer = [slice(None)] * padded.ndim
    for position in range(3):
        slicer[leading + position] = slice(1, -1)
    slicer[leading + direction] = slice(2, None) if sense > 0 else slice(0, -2)
    return padded[tuple(slicer)]


def summed(square):
    rows = jnp.concatenate([square[:, :128], square[:, 128:]], axis=0)
    for axes, count, copies in ((("cy", "gy"), 32, 16), (("core", "gz"), 16, 32)):
        rows = jnp.sum(exchange(rows, axes, count).reshape(count, 16, 128), axis=0)
        rows = jnp.tile(rows, (copies, 1))
    rows = exchange(rows, ("cy", "gy"), 32)
    return jnp.concatenate([rows[:256], rows[256:]], axis=1)


def step_by_step(start_block, node_mass, ground_spring, stiffness, yield_flags, stress_old):
    share = jnp.mean(yield_flags.astype(jnp.float32), axis=1)
    tangent = stiffness * (1.0 - 0.9 * share)[:, None]
    padded = extended(tangent, 2)
    edges = [
        [0.5 * (tangent[d] + neighbour(padded, 2, d, sense)[d]) for d in range(3)]
        for sense in (1, -1)
    ]
    edge_total = sum(edges[0]) + sum(edges[1])
    diagonal = ground_spring + edge_total
    top = jnp.broadcast_to(jnp.max((diagonal + edge_total) / node_mass), (128, 128))
    for axes, count in ((("cy", "core"), 16), ("gy", 4), ("gz", 8)):
        top = jnp.broadcast_to(jnp.max(exchange(top, axes, count)), (128, 128))
    top = top[0, 0]
    middle = top * 9.0 / 16.0
    spread = top * 7.0 / 16.0

    def apply_k(field):
        around_field = extended(field, 1)
        result = diagonal[..., None] * field
        for d in range(3):
            for sense, weights in ((1, edges[0]), (-1, edges[1])):
                result = result - weights[d][..., None] * neighbour(around_field, 1, d, sense)
        return result

    def shifted(field):
        return (apply_k(field) / node_mass[..., None] - middle * field) / spread

    width = start_block.shape[-1]
    mass_rows = node_mass.reshape(-1)
    vectors = start_block
    for turn in range(ITERS):
        earlier, current = vectors, shifted(vectors)
        for repeat in range(DEGREE - 1):
            earlier, current = current, 2.0 * shifted(current) - earlier
        flat_rows = current.reshape(-1, width)
        gram = summed(dot(flat_rows.T, mass_rows[:, None] * flat_rows))
        factor = jnp.linalg.cholesky(gram)
        basis = lax.linalg.triangular_solve(factor, flat_rows.T, left_side=True, lower=True)
        vectors = basis.T.reshape(current.shape)
    image = apply_k(vectors).reshape(-1, width)
    projected = summed(dot(basis, image))
    lateral = dot(basis[:, :NODES], mass_rows[:NODES, None])
    lateral = summed(jnp.broadcast_to(lateral, (width, width)))[:, :1]
    factor = jnp.linalg.cholesky(projected)
    halfway = lax.linalg.triangular_solve(factor, lateral, left_side=True, lower=True)
    weights = lax.linalg.triangular_solve(
        factor, halfway, left_side=True, lower=True, transpose_a=True
    )
    displace = dot(weights.T, basis).reshape(node_mass.shape)
    padded = extended(displace, 1)
    axial = []
    bending = []
    for d in range(3):
        above = neighbour(padded, 1, d, 1)
        below = neighbour(padded, 1, d, -1)
        other = (d + 1) % 3
        axial.append(0.5 * (above[d] - below[d]))
        bending.append(above[other] - 2.0 * displace[other] + below[other])
    fibers = stress_old.shape[1]
    heights = ((jnp.arange(fibers).astype(jnp.float32) + 0.5) / fibers - 0.5)[:, None, None, None]
    strain = jnp.stack(axial)[:, None] + heights * jnp.stack(bending)[:, None]
    stress_new = stress_old + fiber_modulus(stiffness, yield_flags) * strain
    subspace = vectors * jnp.sqrt(jnp.float32(DEVICES * 3 * NODES))
    return subspace, projected, node_mass * displace, stress_new


def call(kernel, shape, scratch=(), smem=(), operands=(), smem_out=()):
    results = len(shape) if isinstance(shape, tuple) else 1
    out_specs = tuple(
        pl.BlockSpec(memory_space=pltpu.SMEM if place in smem_out else pltpu.VMEM)
        for place in range(results)
    )
    return pl.pallas_call(
        kernel,
        out_shape=shape,
        in_specs=[
            pl.BlockSpec(memory_space=pltpu.SMEM if place in smem else pltpu.VMEM)
            for place in range(len(operands))
        ],
        out_specs=out_specs if isinstance(shape, tuple) else out_specs[0],
        scratch_shapes=list(scratch),
        compiler_params=pltpu.CompilerParams(vmem_limit_bytes=40 * 1024 * 1024),
    )(*operands)


def rows_of(count):
    return jax.ShapeDtypeStruct((count, 128), jnp.float32)


def exchange(rows, axes, devices):
    per_device = rows.shape[0] // devices
    if per_device % 8 == 0:
        blocks = rows.reshape(devices, per_device, 128)
    else:
        blocks = rows.reshape(devices, per_device, 1, 128)
    return lax.all_to_all(blocks, axes, 0, 0, tiled=True).reshape(rows.shape)


def chebyshev_nodes():
    count = TOTAL + 1
    angles = np.pi * (np.arange(count) + 0.5) / count
    plain = np.zeros((count, count))
    timesx = np.zeros((count + 1, count))
    for degree in range(count):
        plain[degree] = (2.0 if degree else 1.0) / count * np.cos(degree * angles)
        timesx[degree + 1] += plain[degree] * (0.5 if degree else 1.0)
        if degree:
            timesx[degree - 1] += plain[degree] * 0.5
    table = np.zeros((40, 128), np.float32)
    table[0, :count] = np.cos(angles)
    table[8 : 8 + count, :count] = plain
    table[24 : 25 + count, :count] = timesx
    return jnp.asarray(table)


def on_device(start_block, node_mass, ground_spring, stiffness, yield_flags, stress_old):
    width = start_block.shape[-1]
    fibers = stress_old.shape[1]

    def node_rows(value):
        return jnp.swapaxes(value, -1, -2).reshape(-1, 8)

    def fibers_last(value):
        return jnp.moveaxis(value, 1, -1).reshape(48, 4, fibers)

    grid_shape = (16, 4, 8, 128)
    plain = pltpu.VMEM(grid_shape, jnp.float32)
    planes_shape = (16, KINDS, 4, 8, 128)
    sent = call(
        pack_kernel,
        rows_of(256 * OUT_ROWS),
        operands=(
            start_block.reshape(48, 4, width),
            node_rows(stiffness),
            node_rows(node_mass),
            node_rows(ground_spring),
            fibers_last(yield_flags).reshape(3 * NODES, fibers),
        ),
    )
    own = exchange(sent, CHIPS, 256)
    other = lax.ppermute(own, "core", [(0, 1), (1, 0)])
    core = lax.axis_index("core").astype(jnp.int32).reshape(1)
    planes, own_top = call(
        weights_kernel,
        (jax.ShapeDtypeStruct(planes_shape, jnp.float32), rows_of(32)),
        (plain,),
        smem=(0,),
        operands=(core, own, other),
    )
    tops = exchange(own_top, "gy", 4)
    terms = call(
        filter_kernel,
        jax.ShapeDtypeStruct((TOTAL + 3,) + grid_shape, jnp.float32),
        (plain,),
        operands=(planes, own_top),
    )
    filtered = call(
        combine_kernel,
        rows_of(1024),
        operands=(terms, own_top, tops, chebyshev_nodes()),
    )
    returned = exchange(filtered, AXES, DEVICES)
    mass_row = node_rows(node_mass).reshape(1, 3 * NODES)
    mass_row = jnp.pad(mass_row, ((0, 0), (0, NODES)))
    along = jax.ShapeDtypeStruct((width, 128), jnp.float32)
    products, *along = call(
        product_kernel,
        (rows_of(32 * CHUNK), along, along, along),
        operands=(returned, mass_row),
    )

    def from_neighbours(mine, axis, senses):
        count = lax.axis_size(axis)
        pairs = [(i, i + 1) for i in range(count - 1)]
        return [
            lax.ppermute(mine, axis, [(b, a) for a, b in pairs] if sense > 0 else pairs)
            for sense in senses
        ]

    along_x, along_y, along_z = along
    near = from_neighbours(along_z, "gz", (1, -1)) + from_neighbours(along_y, "gy", (1,))
    part = exchange(products, ("cy", "gy"), 32)
    part, *near = lax.optimization_barrier((part, *near))
    part = call(functools.partial(total_kernel, 32, 16), rows_of(16 * CHUNK), operands=(part,))
    part, along_y = lax.optimization_barrier((part, along_y))
    near += from_neighbours(along_y, "gy", (-1,))
    part = exchange(part, ("core", "gz"), 16)
    part, *near = lax.optimization_barrier((part, *near))
    part = call(functools.partial(total_kernel, 16, 32), rows_of(32 * CHUNK), operands=(part,))
    part, along_x = lax.optimization_barrier((part, along_x))
    far = from_neighbours(along_x, GX, (1, -1))
    part = exchange(part, ("cy", "gy"), 32)
    part, *far = lax.optimization_barrier((part, *far))
    subspace, projected, force, stress_new, apart = call(
        final_kernel,
        (
            jax.ShapeDtypeStruct((48, 4, width), jnp.float32),
            jax.ShapeDtypeStruct((width, width), jnp.float32),
            jax.ShapeDtypeStruct((24, 8), jnp.float32),
            jax.ShapeDtypeStruct((48, 4, fibers), jnp.float32),
            jax.ShapeDtypeStruct((1, 1), jnp.int32),
        ),
        (pltpu.VMEM((2, 256, 256), jnp.float32),),
        operands=(
            part,
            returned,
            *far,
            *near[2:],
            *near[:2],
            mass_row,
            fibers_last(fiber_modulus(stiffness, yield_flags)),
            fibers_last(stress_old),
        ),
        smem_out=(4,),
    )
    place = node_mass.shape[1:]
    force = jnp.swapaxes(force.reshape(3, place[0], place[2], place[1]), -1, -2)
    stress_new = jnp.moveaxis(stress_new.reshape((3,) + place + (fibers,)), -1, 1)
    return lax.switch(
        apart[0, 0],
        (lambda *operands: step_by_step(*operands[4:]), lambda *operands: operands[:4]),
        subspace.reshape(start_block.shape),
        projected,
        force,
        stress_new,
        start_block,
        node_mass,
        ground_spring,
        stiffness,
        yield_flags,
        stress_old,
    )


def solution(mesh):
    chips = Mesh(mesh.devices.reshape(8, 2, 4, 8), AXES)
    return jax.shard_map(
        on_device,
        mesh=chips,
        in_specs=(
            P(None, GX, "gy", "gz", None),
            P(None, GX, "gy", "gz"),
            P(None, GX, "gy", "gz"),
            P(None, None, GX, "gy", "gz"),
            P(None, None, GX, "gy", "gz"),
            P(None, None, GX, "gy", "gz"),
        ),
        out_specs=(
            P(None, GX, "gy", "gz", None),
            P(),
            P(None, GX, "gy", "gz"),
            P(None, None, GX, "gy", "gz"),
        ),
        check_vma=False,
    )
```

```python
import functools

import jax
import jax.numpy as jnp
import numpy as np
from jax import lax
from jax.experimental import pallas as pl
from jax.experimental.pallas import tpu as pltpu
from jax.sharding import Mesh, PartitionSpec as P

DEGREE = 4
ITERS = 2
TOTAL = DEGREE * ITERS
PRECISE = lax.Precision.HIGHEST
GX = ("cy", "core")
AXES = ("cy", "core", "gy", "gz")
CHIPS = ("cy", "gy", "gz")

NODES = 64
DEVICES = 512
OUT_ROWS = 5
LEAST_PIVOT = 0.1
BLOCK = 32
CHUNK = 17
LEAST_PIVOT = 0.1
BLOCK = 32
STIFF_LANE = 9
MASS_LANE = 10


def dot(a, b, contract=((1,), (0,))):
    return lax.dot_general(
        a, b, (contract, ((), ())), precision=PRECISE, preferred_element_type=jnp.float32
    )


def spread_nodes(values, keep):
    groups = jnp.where(keep, values.reshape((-1,) + keep.shape), 0.0)
    return jnp.sum(groups, axis=1)


def pack_kernel(start_ref, stiffness_ref, mass_ref, spring_ref, flags_ref, out_ref):
    lane = lax.broadcasted_iota(jnp.int32, (8, 128), 1)
    place = lax.broadcasted_iota(jnp.int32, (8, 128), 0)
    repeated = jnp.where((lane & 7) == place, 1.0, 0.0)
    keep = ((lane >> 3) & 7) == place
    stiffness = spread_nodes(dot(stiffness_ref[...], repeated), keep)
    masses = spread_nodes(dot(mass_ref[...], repeated), keep)
    springs = spread_nodes(dot(spring_ref[...], repeated), keep)
    counts = jnp.dot(
        flags_ref[...].astype(jnp.bfloat16),
        jnp.ones((16, 128), jnp.bfloat16),
        preferred_element_type=jnp.float32,
    )
    lane = lax.broadcasted_iota(jnp.int32, (NODES, 128), 1)
    place = lax.broadcasted_iota(jnp.int32, (NODES, 128), 0)
    own = ((place >> 5) * 32 + (place & 3) * 8 + ((place >> 2) & 7)) == (lane & 63)
    softening = 1.0 - 0.9 * (spread_nodes(counts, own) / 16.0)
    low = lax.broadcasted_iota(jnp.int32, (1, 128), 1) < 64
    for comp in range(4):
        source = comp % 3
        if comp < 3:
            block = jnp.concatenate(
                [
                    start_ref[comp * 16 + x * 8 : comp * 16 + x * 8 + 8, z, :]
                    for x in range(2)
                    for z in range(4)
                ],
                axis=0,
            )
            pairs = jnp.concatenate([block[:, :128], block[:, 128:]], axis=0).T
        else:
            pairs = jnp.zeros((128, 128), jnp.float32)
        tangent = [
            stiffness[3 * d + source : 3 * d + source + 1, :] * softening[d : d + 1, :]
            for d in range(3)
        ]
        mass = masses[source : source + 1, :]
        spring = springs[source : source + 1, :]
        rows = [
            jnp.broadcast_to(row, (8, 128))
            for row in (
                jnp.where(low, tangent[0], tangent[1]),
                jnp.where(low, tangent[2], mass),
                spring,
            )
        ]
        for cy in range(8):
            first = (cy * 4 + comp) * 8 * OUT_ROWS
            for core in range(2):
                at = (cy * 2 + core) * 8
                out_ref[pl.ds(first + core, 8, stride=OUT_ROWS), :] = pairs[at : at + 8]
            for r in range(3):
                out_ref[pl.ds(first + 2 + r, 8, stride=OUT_ROWS), :] = rows[r]


def iota(axis):
    return lax.broadcasted_iota(jnp.int32, (4, 8, 128), axis)


def grid_row(refs, kind, gx, core):
    rows = [ref[pl.ds(gx // 2 * 32 * OUT_ROWS + kind, 32, stride=OUT_ROWS), :] for ref in refs]
    return jnp.where(core == gx % 2, rows[0], rows[1]).reshape(4, 8, 128)


def roll(value, shift, axis=2):
    return pltpu.roll(value, shift, axis)


def both_halves(value):
    lane = iota(2)
    turned = roll(value, 64)
    return jnp.where(lane < 64, value, turned), jnp.where(lane < 64, turned, value)


class Turned:
    def __init__(self, ref):
        self.ref = ref
        self.planes = {}

    def at(self, gx):
        if gx not in self.planes:
            if gx in (-1, 16):
                zero = jnp.zeros((4, 8, 128), jnp.float32)
                self.planes[gx] = (zero, zero)
            else:
                here = self.ref[gx]
                self.planes[gx] = (roll(here, 96), roll(here, 32))
        return self.planes[gx]

    def sides(self, gx):
        first = (iota(2) & 32) == 0
        up = jnp.where(first, self.at(gx)[0], self.at(gx + 1)[1])
        down = jnp.where(first, self.at(gx - 1)[0], self.at(gx)[1])
        return up, down


def y_up(here):
    moved = jnp.concatenate([here[1:], jnp.zeros((1, 8, 128), jnp.float32)], axis=0)
    return jnp.where((iota(2) & 7) != 7, roll(here, 127), roll(moved, 7))


def y_down(here):
    moved = jnp.concatenate([jnp.zeros((1, 8, 128), jnp.float32), here[:-1]], axis=0)
    return jnp.where((iota(2) & 7) != 0, roll(here, 1), roll(moved, 121))


def z_up(here):
    other = jnp.where(iota(1) < 7, roll(roll(here, 24), 7, 1), 0.0)
    return jnp.where((iota(2) & 24) != 24, roll(here, 120), other)


def z_down(here):
    other = jnp.where(iota(1) > 0, roll(roll(here, 104), 1, 1), 0.0)
    return jnp.where((iota(2) & 24) != 0, roll(here, 8), other)


def around(ref, turned, gx):
    here = ref[gx]
    return here, (turned.sides(gx), (y_up(here), y_down(here)), (z_up(here), z_down(here)))


UP, DOWN, DIAGONAL, MASS, KINDS = 1, 4, 7, 8, 9


def weights_kernel(
    core_ref, own_ref, other_ref, held_ref, top_ref, tangent_ref
):
    core = core_ref[0]
    refs = (own_ref, other_ref)
    second = []
    for gx in range(16):
        held_ref[gx, 0] = grid_row(refs, core, gx, core)
        first, along_y = both_halves(grid_row(refs, 2, gx, core))
        tangent_ref[gx] = first
        second.append(along_y)
    turned = Turned(tangent_ref)
    best = jnp.zeros((4, 8, 128), jnp.float32)
    for gx in range(16):
        first = tangent_ref[gx]
        above, below = turned.sides(gx)
        third, mass = both_halves(grid_row(refs, 3, gx, core))
        spring = grid_row(refs, 4, gx, core)
        ups = [
            0.5 * (first + above),
            0.5 * (second[gx] + y_up(second[gx])),
            0.5 * (third + z_up(third)),
        ]
        downs = [
            0.5 * (first + below),
            0.5 * (second[gx] + y_down(second[gx])),
            0.5 * (third + z_down(third)),
        ]
        total = (ups[0] + ups[1] + ups[2]) + (downs[0] + downs[1] + downs[2])
        for direction in range(3):
            held_ref[gx, UP + direction] = ups[direction]
            held_ref[gx, DOWN + direction] = downs[direction]
        diagonal = spring + total
        held_ref[gx, DIAGONAL] = diagonal
        held_ref[gx, MASS] = mass
        best = jnp.maximum(best, (diagonal + total) / mass)
    best = jnp.max(jnp.max(best, axis=0), axis=(0, 1), keepdims=True)
    top_ref[...] = jnp.broadcast_to(best, (32, 128))


def filter_kernel(held_ref, top_ref, terms_ref, inverse_ref):
    top = top_ref[0:1, :]
    inverse_spread = 1.0 / (top * 7.0 / 16.0)
    ratio = (top * 9.0 / 16.0) * inverse_spread
    for gx in range(16):
        mass = held_ref[gx, MASS]
        inverse_ref[gx] = inverse_spread / mass
        terms_ref[0, gx] = held_ref[gx, 0]
        terms_ref[TOTAL + 2, gx] = mass
    for degree in range(1, TOTAL + 2):
        current_ref = terms_ref.at[degree - 1]
        turned = Turned(current_ref)
        for gx in range(16):
            here, sides = around(current_ref, turned, gx)
            image = held_ref[gx, DIAGONAL] * here
            for direction in range(3):
                image = image - held_ref[gx, UP + direction] * sides[direction][0]
                image = image - held_ref[gx, DOWN + direction] * sides[direction][1]
            image = image * inverse_ref[gx] - ratio * here
            if degree > 1:
                image = 2.0 * image - terms_ref[degree - 2, gx]
            terms_ref[degree, gx] = image


def combine_kernel(terms_ref, own_top_ref, top_ref, nodes_ref, out_ref):
    top = jnp.max(jnp.max(top_ref[...], axis=0, keepdims=True), axis=1, keepdims=True)
    own_top = own_top_ref[0:1, :]
    part = own_top / top
    place = part * nodes_ref[0:1, :] + (part - 1.0) * (9.0 / 7.0)
    square = place * place
    once = 8.0 * square * square - 8.0 * square + 1.0
    coefficients = jnp.sum(nodes_ref[8:40, :] * (once * once), axis=1, keepdims=True)
    middle = own_top * 9.0 / 16.0
    spread = own_top * 7.0 / 16.0
    for gx in range(16):
        total = coefficients[0:1, :] * terms_ref[0, gx]
        scaled = coefficients[16:17, :] * terms_ref[0, gx]
        for degree in range(1, TOTAL + 2):
            term = terms_ref[degree, gx]
            if degree <= TOTAL:
                total = total + coefficients[degree : degree + 1, :] * term
            scaled = scaled + coefficients[16 + degree : 17 + degree, :] * term
        image = terms_ref[TOTAL + 2, gx] * (middle * total + spread * scaled)
        out_ref[pl.ds(gx * 64, 32, stride=2), :] = total.reshape(32, 128)
        out_ref[pl.ds(gx * 64 + 1, 32, stride=2), :] = image.reshape(32, 128)


def parts_of(rows_ref, kind):
    return [
        jnp.concatenate(
            [rows_ref[pl.ds((gx * 4 + comp) * 16 + kind, 8, stride=2), :] for gx in range(16)],
            axis=0,
        )
        for comp in range(3)
    ]


def pair_rows(one, two):
    low = lax.broadcasted_iota(jnp.int32, (128, 128), 1) < 64
    upper = jnp.where(low, one, 0.0 if two is None else pltpu.roll(two, 64, 1))
    lower = jnp.where(low, pltpu.roll(one, 64, 1), 0.0 if two is None else two)
    return jnp.concatenate([upper, lower], axis=0)


def by_vector(parts):
    return jnp.concatenate(
        [pair_rows(parts[0], parts[1]), pair_rows(parts[2], None)], axis=1
    )


def product_kernel(rows_ref, mass_ref, out_ref, along_x_ref, along_y_ref, along_z_ref):
    parts = parts_of(rows_ref, 0)
    vectors = by_vector(parts)
    along_x_ref[...] = vectors[:, :128]
    along_y_ref[...] = pair_rows(parts[1], parts[2])
    along_z_ref[...] = pair_rows(parts[2], parts[0])
    image = by_vector(parts_of(rows_ref, 1))
    weighted = vectors * mass_ref[...]
    gram = dot(weighted, vectors, ((1,), (1,)))
    stiff = dot(vectors, image, ((1,), (1,)))
    row = lax.broadcasted_iota(jnp.int32, (256, 256), 0)
    column = lax.broadcasted_iota(jnp.int32, (256, 256), 1)
    both = jnp.where(row >= column, gram, stiff)
    diagonal = jnp.sum(vectors * image, axis=1, keepdims=True)
    lane = lax.broadcasted_iota(jnp.int32, (256, 128), 1)
    lateral = jnp.sum(jnp.where(lane < NODES, weighted[:, :128], 0.0), axis=1, keepdims=True)
    further = jnp.where(lane == 0, diagonal, jnp.where(lane == 1, lateral, 0.0)).T
    for chunk in range(32):
        half = slice(0, 128) if chunk < 16 else slice(128, 256)
        first = chunk % 16 * 16
        out_ref[chunk * CHUNK : chunk * CHUNK + 16, :] = both[first : first + 16, half]
        last = further[chunk // 2 : chunk // 2 + 1, chunk % 2 * 128 : chunk % 2 * 128 + 128]
        out_ref[chunk * CHUNK + 16 : chunk * CHUNK + 17, :] = last


def total_kernel(count, copies, rows_ref, out_ref):
    total = rows_ref[0:CHUNK, :]
    for place in range(1, count):
        total = total + rows_ref[place * CHUNK : place * CHUNK + CHUNK, :]
    for place in range(copies):
        out_ref[place * CHUNK : place * CHUNK + CHUNK, :] = total


def factor_block(gram, stiff):
    lane = lax.broadcasted_iota(jnp.int32, (BLOCK, 128), 1)
    row = lax.broadcasted_iota(jnp.int32, (BLOCK, 128), 0)
    low = lane < 64
    columns = [
        jnp.where(
            low,
            jnp.broadcast_to(gram[:, j : j + 1], (BLOCK, 128)),
            jnp.broadcast_to(stiff[:, j : j + 1], (BLOCK, 128)),
        )
        for j in range(BLOCK)
    ]
    inverse = jnp.where((lane & 63) == row, 1.0, 0.0)
    scale = jnp.ones((BLOCK, 128), jnp.float32)
    link = jnp.zeros((BLOCK, 128), jnp.float32)
    for k in range(0, BLOCK, 2):
        one, two = columns[k], columns[k + 1]
        top = one[k : k + 1, :]
        side = one[k + 1 : k + 2, :]
        corner = two[k + 1 : k + 2, :]
        rest = top * corner - side * side
        scale = jnp.where(row == k, top, jnp.where(row == k + 1, rest / top, scale))
        link = jnp.where(row == k + 1, side / top, link)
        if k + 2 == BLOCK:
            break
        part = (k + 2) // 8 * 8
        factor = 1.0 / rest
        below = row[part:] > k + 1
        first = jnp.where(below, (one[part:] * corner - two[part:] * side) * factor, 0.0)
        second = jnp.where(below, (two[part:] * top - one[part:] * side) * factor, 0.0)

        def reduced(value):
            tail = value[part:] - (first * value[k : k + 1, :] + second * value[k + 1 : k + 2, :])
            return tail if part == 0 else jnp.concatenate([value[:part], tail], axis=0)

        for j in range(k + 2, BLOCK):
            columns[j] = reduced(columns[j])
        inverse = reduced(inverse)
    inverse = inverse - link * pltpu.roll(inverse, 1, 0)
    return inverse * lax.rsqrt(scale), scale


def rounded(value):
    return value.astype(jnp.bfloat16).astype(jnp.float32)


def three_parts(value):
    high = rounded(value)
    rest = value - high
    middle = rounded(rest)
    return high, middle, rest - middle


def four_copies(value):
    return (value + pltpu.roll(value, 32, 1)) + (
        pltpu.roll(value, 64, 1) + pltpu.roll(value, 96, 1)
    )


def left_groups(first, second):
    group = lax.broadcasted_iota(jnp.int32, first.shape, 1) // BLOCK
    high, middle, _ = three_parts(first)
    parts = three_parts(second)
    one = jnp.where(group < 2, high, middle)
    two = jnp.where(group == 0, parts[0], jnp.where(group == 1, parts[2], 0.0))
    return jnp.concatenate([one, two], axis=1).astype(jnp.bfloat16)


def right_lanes(copies):
    group = lax.broadcasted_iota(jnp.int32, copies.shape, 1) // BLOCK
    high, middle, low = three_parts(copies)
    one = jnp.where(group % 2 == 0, high, middle)
    two = jnp.where(group == 0, low, high)
    return jnp.concatenate([one, two], axis=1).astype(jnp.bfloat16)


def right_rows(value):
    high, middle, low = [part.astype(jnp.bfloat16) for part in three_parts(value)]
    return jnp.concatenate([high, middle, high, middle, low, high, high, high], axis=0)


def product(left, right, contract):
    return lax.dot_general(
        left, right, (contract, ((), ())), preferred_element_type=jnp.float32
    )


def invert_factors(m_ref, diagonal):
    lane = lax.broadcasted_iota(jnp.int32, (BLOCK, 128), 1)
    least = jnp.ones((BLOCK, 128), jnp.float32)
    for first in range(0, 256, BLOCK):
        tile = first // 128 * 128
        inside = first - tile
        after = first + BLOCK
        small = [m_ref[m, first:after, tile : tile + 128][:, inside : inside + BLOCK] for m in (0, 1)]
        inverse, pivots = factor_block(small[0], small[1])
        least = jnp.minimum(least, pivots / diagonal[first:after, :])
        for m in (0, 1):
            own = four_copies(
                jnp.where((lane >= 64 * m) & (lane < 64 * m + BLOCK), inverse, 0.0)
            )
            row = lax.broadcasted_iota(jnp.int32, (BLOCK, 256), 0)
            column = lax.broadcasted_iota(jnp.int32, (BLOCK, 256), 1) - first
            rows = m_ref[m, first:after, :]
            unit = jnp.where(column == row, 1.0, 0.0)
            rows = jnp.where((column >= 0) & (column < BLOCK), unit, rows)
            result = product(left_groups(own, own), right_rows(rows), ((1,), (0,)))
            m_ref[m, first:after, :] = result
            if after < 256:
                count = 256 - after
                lanes = lax.broadcasted_iota(jnp.int32, (count, 128), 1)
                held = (lanes >= inside) & (lanes < inside + BLOCK)
                left = four_copies(jnp.where(held, m_ref[m, after:, tile : tile + 128], 0.0))
                right = jnp.concatenate([right_lanes(own)] * 8, axis=0)
                factor = product(left_groups(left, left), right, ((1,), (1,)))
                column = lax.broadcasted_iota(jnp.int32, (count, 256), 1)
                rows = m_ref[m, after:, :]
                rows = jnp.where((column >= first) & (column < after), 0.0, rows)
                m_ref[m, after:, :] = rows - product(
                    left_groups(factor[:, :128], factor[:, 128:]), right_rows(result), ((1,), (0,))
                )
    return jnp.min(least, axis=(0, 1), keepdims=True)


def final_kernel(
    sums_ref, rows_ref, above_x_ref, below_x_ref, above_y_ref, below_y_ref, above_z_ref,
    below_z_ref, mass_ref, modulus_ref, stress_ref, subspace_ref, projected_ref, force_ref,
    stress_new_ref, apart_ref, m_ref
):
    chunks = [sums_ref[chunk * CHUNK : chunk * CHUNK + 16, :] for chunk in range(32)]
    both = jnp.concatenate(
        [jnp.concatenate(chunks[:16], axis=0), jnp.concatenate(chunks[16:], axis=0)], axis=1
    )
    further = [
        jnp.broadcast_to(sums_ref[chunk * CHUNK + 16 : chunk * CHUNK + 17, :], (128, 128)).T
        for chunk in range(4)
    ]
    diagonal = jnp.concatenate(further[:2], axis=0)
    diagonal = jnp.concatenate([diagonal, diagonal], axis=1)
    lateral = jnp.concatenate(further[2:], axis=0)
    turned = both.T
    row = lax.broadcasted_iota(jnp.int32, (256, 256), 0)
    column = lax.broadcasted_iota(jnp.int32, (256, 256), 1)
    gram = jnp.where(row >= column, both, turned)
    stiff = jnp.where(row < column, both, jnp.where(row == column, diagonal, turned))
    m_ref[0] = gram
    m_ref[1] = stiff
    half = lax.broadcasted_iota(jnp.int32, (256, 128), 1) < 64
    gram_diagonal = jnp.sum(jnp.where(row == column, gram, 0.0), axis=1, keepdims=True)
    least = invert_factors(m_ref, jnp.where(half, gram_diagonal, diagonal[:, :128]))
    apart_ref[0, 0] = jnp.where(least[0, 0] > LEAST_PIVOT, 1, 0)
    lower = jnp.where(row >= column, m_ref[0], 0.0)
    stiff_lower = jnp.where(row >= column, m_ref[1], 0.0)
    vectors = by_vector(parts_of(rows_ref, 0))
    subspace = dot(vectors.T, lower, ((1,), (1,)))
    subspace = subspace * jnp.sqrt(jnp.float32(DEVICES * 3 * NODES))
    projected_ref[...] = dot(lower, dot(stiff, lower, ((1,), (1,))))
    weights = dot(stiff_lower.T, dot(stiff_lower, lateral))
    weights = jnp.concatenate([weights, weights], axis=1)
    displace = jnp.sum(vectors * weights, axis=0, keepdims=True)
    own = [displace[:, :128], pltpu.roll(displace[:, :128], 64, 1), displace[:, 128:]]
    outside = [
        jnp.sum(ref[...] * weights[:, :128], axis=0, keepdims=True)
        for ref in (above_x_ref, below_x_ref, above_y_ref, below_y_ref, above_z_ref, below_z_ref)
    ]
    lane = lax.broadcasted_iota(jnp.int32, (1, 128), 1)
    axial = []
    bending = []
    for direction, (step, mask) in enumerate(((32, 32), (1, 7), (8, 24))):
        wide = jnp.where(lane < 64, own[direction], pltpu.roll(own[(direction + 1) % 3], 64, 1))
        above = jnp.where(
            (lane & mask) == mask,
            pltpu.roll(outside[2 * direction], mask, 1),
            pltpu.roll(wide, 128 - step, 1),
        )
        below = jnp.where(
            (lane & mask) == 0,
            pltpu.roll(outside[2 * direction + 1], 128 - mask, 1),
            pltpu.roll(wide, step, 1),
        )
        axial.append(0.5 * (above - below))
        bending.append(pltpu.roll((above - 2.0 * wide) + below, 64, 1))
    lane = lax.broadcasted_iota(jnp.int32, (24, 256), 1)
    group = lax.broadcasted_iota(jnp.int32, (24, 256), 0)
    laid = jnp.where((lane >> 3) == group, displace * mass_ref[...], 0.0)
    column = lax.broadcasted_iota(jnp.int32, (256, 128), 0)
    place = lax.broadcasted_iota(jnp.int32, (256, 128), 1)
    force_ref[...] = dot(laid, jnp.where((column & 7) == place, 1.0, 0.0))[:, :8]
    columns = jnp.concatenate(
        axial + bending + [jnp.zeros((122, 128), jnp.float32)], axis=0
    ).T
    axial = [jnp.broadcast_to(columns[:, d : d + 1], (128, 16)) for d in range(3)]
    bending = [jnp.broadcast_to(columns[:, 3 + d : 4 + d], (128, 16)) for d in range(3)]
    fiber = lax.broadcasted_iota(jnp.int32, (8, 16), 1).astype(jnp.float32)
    heights = (fiber + 0.5) / 16.0 - 0.5
    for direction in range(3):
        for x in range(2):
            for z in range(4):
                rows = slice(direction * 16 + x * 8, direction * 16 + x * 8 + 8)
                inner = x * 32 + z * 8
                one = direction * NODES + inner
                subspace_ref[rows, z, :] = subspace[one : one + 8]
                strain = axial[direction][inner : inner + 8]
                strain = strain + heights * bending[direction][inner : inner + 8]
                stress_new_ref[rows, z, :] = stress_ref[rows, z, :] + modulus_ref[rows, z, :] * strain


def fiber_modulus(stiffness, yield_flags):
    own = jnp.stack([stiffness[d, d] for d in range(3)])[:, None]
    return own * jnp.where(yield_flags == 1, 0.05, 1.0)


def extended(block, first_dim):
    for place, axis in enumerate((GX, "gy", "gz")):
        dim = first_dim + place
        count = lax.axis_size(axis)
        forward = [(i, i + 1) for i in range(count - 1)]
        backward = [(target, source) for source, target in forward]
        last = block.shape[dim]
        low = lax.ppermute(lax.slice_in_dim(block, last - 1, last, axis=dim), axis, forward)
        high = lax.ppermute(lax.slice_in_dim(block, 0, 1, axis=dim), axis, backward)
        block = jnp.concatenate([low, block, high], axis=dim)
    return block


def neighbour(padded, leading, direction, sense):
    slicer = [slice(None)] * padded.ndim
    for position in range(3):
        slicer[leading + position] = slice(1, -1)
    slicer[leading + direction] = slice(2, None) if sense > 0 else slice(0, -2)
    return padded[tuple(slicer)]


def summed(square):
    rows = jnp.concatenate([square[:, :128], square[:, 128:]], axis=0)
    for axes, count, copies in ((("cy", "gy"), 32, 16), (("core", "gz"), 16, 32)):
        rows = jnp.sum(exchange(rows, axes, count).reshape(count, 16, 128), axis=0)
        rows = jnp.tile(rows, (copies, 1))
    rows = exchange(rows, ("cy", "gy"), 32)
    return jnp.concatenate([rows[:256], rows[256:]], axis=1)


def step_by_step(start_block, node_mass, ground_spring, stiffness, yield_flags, stress_old):
    share = jnp.mean(yield_flags.astype(jnp.float32), axis=1)
    tangent = stiffness * (1.0 - 0.9 * share)[:, None]
    padded = extended(tangent, 2)
    edges = [
        [0.5 * (tangent[d] + neighbour(padded, 2, d, sense)[d]) for d in range(3)]
        for sense in (1, -1)
    ]
    edge_total = sum(edges[0]) + sum(edges[1])
    diagonal = ground_spring + edge_total
    top = jnp.broadcast_to(jnp.max((diagonal + edge_total) / node_mass), (128, 128))
    for axes, count in ((("cy", "core"), 16), ("gy", 4), ("gz", 8)):
        top = jnp.broadcast_to(jnp.max(exchange(top, axes, count)), (128, 128))
    top = top[0, 0]
    middle = top * 9.0 / 16.0
    spread = top * 7.0 / 16.0

    def apply_k(field):
        around_field = extended(field, 1)
        result = diagonal[..., None] * field
        for d in range(3):
            for sense, weights in ((1, edges[0]), (-1, edges[1])):
                result = result - weights[d][..., None] * neighbour(around_field, 1, d, sense)
        return result

    def shifted(field):
        return (apply_k(field) / node_mass[..., None] - middle * field) / spread

    width = start_block.shape[-1]
    mass_rows = node_mass.reshape(-1)
    vectors = start_block
    for turn in range(ITERS):
        earlier, current = vectors, shifted(vectors)
        for repeat in range(DEGREE - 1):
            earlier, current = current, 2.0 * shifted(current) - earlier
        flat_rows = current.reshape(-1, width)
        gram = summed(dot(flat_rows.T, mass_rows[:, None] * flat_rows))
        factor = jnp.linalg.cholesky(gram)
        basis = lax.linalg.triangular_solve(factor, flat_rows.T, left_side=True, lower=True)
        vectors = basis.T.reshape(current.shape)
    image = apply_k(vectors).reshape(-1, width)
    projected = summed(dot(basis, image))
    lateral = dot(basis[:, :NODES], mass_rows[:NODES, None])
    lateral = summed(jnp.broadcast_to(lateral, (width, width)))[:, :1]
    factor = jnp.linalg.cholesky(projected)
    halfway = lax.linalg.triangular_solve(factor, lateral, left_side=True, lower=True)
    weights = lax.linalg.triangular_solve(
        factor, halfway, left_side=True, lower=True, transpose_a=True
    )
    displace = dot(weights.T, basis).reshape(node_mass.shape)
    padded = extended(displace, 1)
    axial = []
    bending = []
    for d in range(3):
        above = neighbour(padded, 1, d, 1)
        below = neighbour(padded, 1, d, -1)
        other = (d + 1) % 3
        axial.append(0.5 * (above[d] - below[d]))
        bending.append(above[other] - 2.0 * displace[other] + below[other])
    fibers = stress_old.shape[1]
    heights = ((jnp.arange(fibers).astype(jnp.float32) + 0.5) / fibers - 0.5)[:, None, None, None]
    strain = jnp.stack(axial)[:, None] + heights * jnp.stack(bending)[:, None]
    stress_new = stress_old + fiber_modulus(stiffness, yield_flags) * strain
    subspace = vectors * jnp.sqrt(jnp.float32(DEVICES * 3 * NODES))
    return subspace, projected, node_mass * displace, stress_new


def call(kernel, shape, scratch=(), smem=(), operands=(), smem_out=()):
    results = len(shape) if isinstance(shape, tuple) else 1
    out_specs = tuple(
        pl.BlockSpec(memory_space=pltpu.SMEM if place in smem_out else pltpu.VMEM)
        for place in range(results)
    )
    return pl.pallas_call(
        kernel,
        out_shape=shape,
        in_specs=[
            pl.BlockSpec(memory_space=pltpu.SMEM if place in smem else pltpu.VMEM)
            for place in range(len(operands))
        ],
        out_specs=out_specs if isinstance(shape, tuple) else out_specs[0],
        scratch_shapes=list(scratch),
        compiler_params=pltpu.CompilerParams(vmem_limit_bytes=40 * 1024 * 1024),
    )(*operands)


def rows_of(count):
    return jax.ShapeDtypeStruct((count, 128), jnp.float32)


def exchange(rows, axes, devices):
    per_device = rows.shape[0] // devices
    if per_device % 8 == 0:
        blocks = rows.reshape(devices, per_device, 128)
    else:
        blocks = rows.reshape(devices, per_device, 1, 128)
    return lax.all_to_all(blocks, axes, 0, 0, tiled=True).reshape(rows.shape)


def chebyshev_nodes():
    count = TOTAL + 1
    angles = np.pi * (np.arange(count) + 0.5) / count
    plain = np.zeros((count, count))
    timesx = np.zeros((count + 1, count))
    for degree in range(count):
        plain[degree] = (2.0 if degree else 1.0) / count * np.cos(degree * angles)
        timesx[degree + 1] += plain[degree] * (0.5 if degree else 1.0)
        if degree:
            timesx[degree - 1] += plain[degree] * 0.5
    table = np.zeros((40, 128), np.float32)
    table[0, :count] = np.cos(angles)
    table[8 : 8 + count, :count] = plain
    table[24 : 25 + count, :count] = timesx
    return jnp.asarray(table)


def on_device(start_block, node_mass, ground_spring, stiffness, yield_flags, stress_old):
    width = start_block.shape[-1]
    fibers = stress_old.shape[1]

    def node_rows(value):
        return jnp.swapaxes(value, -1, -2).reshape(-1, 8)

    def fibers_last(value):
        return jnp.moveaxis(value, 1, -1).reshape(48, 4, fibers)

    grid_shape = (16, 4, 8, 128)
    plain = pltpu.VMEM(grid_shape, jnp.float32)
    planes_shape = (16, KINDS, 4, 8, 128)
    sent = call(
        pack_kernel,
        rows_of(256 * OUT_ROWS),
        operands=(
            start_block.reshape(48, 4, width),
            node_rows(stiffness),
            node_rows(node_mass),
            node_rows(ground_spring),
            fibers_last(yield_flags).reshape(3 * NODES, fibers),
        ),
    )
    own = exchange(sent, CHIPS, 256)
    other = lax.ppermute(own, "core", [(0, 1), (1, 0)])
    core = lax.axis_index("core").astype(jnp.int32).reshape(1)
    planes, own_top = call(
        weights_kernel,
        (jax.ShapeDtypeStruct(planes_shape, jnp.float32), rows_of(32)),
        (plain,),
        smem=(0,),
        operands=(core, own, other),
    )
    tops = exchange(own_top, "gy", 4)
    terms = call(
        filter_kernel,
        jax.ShapeDtypeStruct((TOTAL + 3,) + grid_shape, jnp.float32),
        (plain,),
        operands=(planes, own_top),
    )
    filtered = call(
        combine_kernel,
        rows_of(1024),
        operands=(terms, own_top, tops, chebyshev_nodes()),
    )
    returned = exchange(filtered, AXES, DEVICES)
    mass_row = node_rows(node_mass).reshape(1, 3 * NODES)
    mass_row = jnp.pad(mass_row, ((0, 0), (0, NODES)))
    along = jax.ShapeDtypeStruct((width, 128), jnp.float32)
    products, *along = call(
        product_kernel,
        (rows_of(32 * CHUNK), along, along, along),
        operands=(returned, mass_row),
    )

    def from_neighbours(mine, axis, senses):
        count = lax.axis_size(axis)
        pairs = [(i, i + 1) for i in range(count - 1)]
        return [
            lax.ppermute(mine, axis, [(b, a) for a, b in pairs] if sense > 0 else pairs)
            for sense in senses
        ]

    near = from_neighbours(along[0], GX, (1, -1))
    part = exchange(products, ("cy", "gy"), 32)
    part, *near = lax.optimization_barrier((part, *near))
    part = call(functools.partial(total_kernel, 32, 16), rows_of(16 * CHUNK), operands=(part,))
    part, along[1] = lax.optimization_barrier((part, along[1]))
    near += from_neighbours(along[1], "gy", (1,))
    part = exchange(part, ("core", "gz"), 16)
    part, *near = lax.optimization_barrier((part, *near))
    part = call(functools.partial(total_kernel, 16, 32), rows_of(32 * CHUNK), operands=(part,))
    part, *along[1:] = lax.optimization_barrier((part, *along[1:]))
    far = from_neighbours(along[1], "gy", (-1,)) + from_neighbours(along[2], "gz", (1, -1))
    part = exchange(part, ("cy", "gy"), 32)
    part, *far = lax.optimization_barrier((part, *far))
    subspace, projected, force, stress_new, apart = call(
        final_kernel,
        (
            jax.ShapeDtypeStruct((48, 4, width), jnp.float32),
            jax.ShapeDtypeStruct((width, width), jnp.float32),
            jax.ShapeDtypeStruct((24, 8), jnp.float32),
            jax.ShapeDtypeStruct((48, 4, fibers), jnp.float32),
            jax.ShapeDtypeStruct((1, 1), jnp.int32),
        ),
        (pltpu.VMEM((2, 256, 256), jnp.float32),),
        operands=(
            part,
            returned,
            *near,
            *far,
            mass_row,
            fibers_last(fiber_modulus(stiffness, yield_flags)),
            fibers_last(stress_old),
        ),
        smem_out=(4,),
    )
    place = node_mass.shape[1:]
    force = jnp.swapaxes(force.reshape(3, place[0], place[2], place[1]), -1, -2)
    stress_new = jnp.moveaxis(stress_new.reshape((3,) + place + (fibers,)), -1, 1)
    return lax.switch(
        apart[0, 0],
        (lambda *operands: step_by_step(*operands[4:]), lambda *operands: operands[:4]),
        subspace.reshape(start_block.shape),
        projected,
        force,
        stress_new,
        start_block,
        node_mass,
        ground_spring,
        stiffness,
        yield_flags,
        stress_old,
    )


def solution(mesh):
    chips = Mesh(mesh.devices.reshape(8, 2, 4, 8), AXES)
    return jax.shard_map(
        on_device,
        mesh=chips,
        in_specs=(
            P(None, GX, "gy", "gz", None),
            P(None, GX, "gy", "gz"),
            P(None, GX, "gy", "gz"),
            P(None, None, GX, "gy", "gz"),
            P(None, None, GX, "gy", "gz"),
            P(None, None, GX, "gy", "gz"),
        ),
        out_specs=(
            P(None, GX, "gy", "gz", None),
            P(),
            P(None, GX, "gy", "gz"),
            P(None, None, GX, "gy", "gz"),
        ),
        check_vma=False,
    )
```

```python
import functools

import jax
import jax.numpy as jnp
import numpy as np
from jax import lax
from jax.experimental import pallas as pl
from jax.experimental.pallas import tpu as pltpu
from jax.sharding import Mesh, PartitionSpec as P

DEGREE = 4
ITERS = 2
TOTAL = DEGREE * ITERS
PRECISE = lax.Precision.HIGHEST
GX = ("cy", "core")
AXES = ("cy", "core", "gy", "gz")
CHIPS = ("cy", "gy", "gz")

NODES = 64
DEVICES = 512
OUT_ROWS = 5
LEAST_PIVOT = 0.1
BLOCK = 32
CHUNK = 17
LEAST_PIVOT = 0.1
BLOCK = 32
STIFF_LANE = 9
MASS_LANE = 10


def dot(a, b, contract=((1,), (0,))):
    return lax.dot_general(
        a, b, (contract, ((), ())), precision=PRECISE, preferred_element_type=jnp.float32
    )


def spread_nodes(values, keep):
    groups = jnp.where(keep, values.reshape((-1,) + keep.shape), 0.0)
    return jnp.sum(groups, axis=1)


def pack_kernel(start_ref, stiffness_ref, mass_ref, spring_ref, flags_ref, out_ref):
    lane = lax.broadcasted_iota(jnp.int32, (8, 128), 1)
    place = lax.broadcasted_iota(jnp.int32, (8, 128), 0)
    repeated = jnp.where((lane & 7) == place, 1.0, 0.0)
    keep = ((lane >> 3) & 7) == place
    stiffness = spread_nodes(dot(stiffness_ref[...], repeated), keep)
    masses = spread_nodes(dot(mass_ref[...], repeated), keep)
    springs = spread_nodes(dot(spring_ref[...], repeated), keep)
    counts = jnp.dot(
        flags_ref[...].astype(jnp.bfloat16),
        jnp.ones((16, 128), jnp.bfloat16),
        preferred_element_type=jnp.float32,
    )
    lane = lax.broadcasted_iota(jnp.int32, (NODES, 128), 1)
    place = lax.broadcasted_iota(jnp.int32, (NODES, 128), 0)
    own = ((place >> 5) * 32 + (place & 3) * 8 + ((place >> 2) & 7)) == (lane & 63)
    softening = 1.0 - 0.9 * (spread_nodes(counts, own) / 16.0)
    low = lax.broadcasted_iota(jnp.int32, (1, 128), 1) < 64
    for comp in range(4):
        source = comp % 3
        if comp < 3:
            block = jnp.concatenate(
                [
                    start_ref[comp * 16 + x * 8 : comp * 16 + x * 8 + 8, z, :]
                    for x in range(2)
                    for z in range(4)
                ],
                axis=0,
            )
            pairs = jnp.concatenate([block[:, :128], block[:, 128:]], axis=0).T
        else:
            pairs = jnp.zeros((128, 128), jnp.float32)
        tangent = [
            stiffness[3 * d + source : 3 * d + source + 1, :] * softening[d : d + 1, :]
            for d in range(3)
        ]
        mass = masses[source : source + 1, :]
        spring = springs[source : source + 1, :]
        rows = [
            jnp.broadcast_to(row, (8, 128))
            for row in (
                jnp.where(low, tangent[0], tangent[1]),
                jnp.where(low, tangent[2], mass),
                spring,
            )
        ]
        for cy in range(8):
            first = (cy * 4 + comp) * 8 * OUT_ROWS
            for core in range(2):
                at = (cy * 2 + core) * 8
                out_ref[pl.ds(first + core, 8, stride=OUT_ROWS), :] = pairs[at : at + 8]
            for r in range(3):
                out_ref[pl.ds(first + 2 + r, 8, stride=OUT_ROWS), :] = rows[r]


def iota(axis):
    return lax.broadcasted_iota(jnp.int32, (4, 8, 128), axis)


def grid_row(refs, kind, gx, core):
    rows = [ref[pl.ds(gx // 2 * 32 * OUT_ROWS + kind, 32, stride=OUT_ROWS), :] for ref in refs]
    return jnp.where(core == gx % 2, rows[0], rows[1]).reshape(4, 8, 128)


def roll(value, shift, axis=2):
    return pltpu.roll(value, shift, axis)


def both_halves(value):
    lane = iota(2)
    turned = roll(value, 64)
    return jnp.where(lane < 64, value, turned), jnp.where(lane < 64, turned, value)


class Turned:
    def __init__(self, ref):
        self.ref = ref
        self.planes = {}

    def at(self, gx):
        if gx not in self.planes:
            if gx in (-1, 16):
                zero = jnp.zeros((4, 8, 128), jnp.float32)
                self.planes[gx] = (zero, zero)
            else:
                here = self.ref[gx]
                self.planes[gx] = (roll(here, 96), roll(here, 32))
        return self.planes[gx]

    def sides(self, gx):
        first = (iota(2) & 32) == 0
        up = jnp.where(first, self.at(gx)[0], self.at(gx + 1)[1])
        down = jnp.where(first, self.at(gx - 1)[0], self.at(gx)[1])
        return up, down


def y_up(here):
    moved = jnp.concatenate([here[1:], jnp.zeros((1, 8, 128), jnp.float32)], axis=0)
    return jnp.where((iota(2) & 7) != 7, roll(here, 127), roll(moved, 7))


def y_down(here):
    moved = jnp.concatenate([jnp.zeros((1, 8, 128), jnp.float32), here[:-1]], axis=0)
    return jnp.where((iota(2) & 7) != 0, roll(here, 1), roll(moved, 121))


def z_up(here):
    other = jnp.where(iota(1) < 7, roll(roll(here, 24), 7, 1), 0.0)
    return jnp.where((iota(2) & 24) != 24, roll(here, 120), other)


def z_down(here):
    other = jnp.where(iota(1) > 0, roll(roll(here, 104), 1, 1), 0.0)
    return jnp.where((iota(2) & 24) != 0, roll(here, 8), other)


def around(ref, turned, gx):
    here = ref[gx]
    return here, (turned.sides(gx), (y_up(here), y_down(here)), (z_up(here), z_down(here)))


UP, DOWN, DIAGONAL, MASS, KINDS = 1, 4, 7, 8, 9


def weights_kernel(
    core_ref, own_ref, other_ref, held_ref, top_ref, tangent_ref
):
    core = core_ref[0]
    refs = (own_ref, other_ref)
    second = []
    for gx in range(16):
        held_ref[gx, 0] = jnp.where(
            core == 0, grid_row(refs, 0, gx, core), grid_row(refs, 1, gx, core)
        )
        first, along_y = both_halves(grid_row(refs, 2, gx, core))
        tangent_ref[gx] = first
        second.append(along_y)
    turned = Turned(tangent_ref)
    best = jnp.zeros((4, 8, 128), jnp.float32)
    for gx in range(16):
        first = tangent_ref[gx]
        above, below = turned.sides(gx)
        third, mass = both_halves(grid_row(refs, 3, gx, core))
        spring = grid_row(refs, 4, gx, core)
        ups = [
            0.5 * (first + above),
            0.5 * (second[gx] + y_up(second[gx])),
            0.5 * (third + z_up(third)),
        ]
        downs = [
            0.5 * (first + below),
            0.5 * (second[gx] + y_down(second[gx])),
            0.5 * (third + z_down(third)),
        ]
        total = (ups[0] + ups[1] + ups[2]) + (downs[0] + downs[1] + downs[2])
        for direction in range(3):
            held_ref[gx, UP + direction] = ups[direction]
            held_ref[gx, DOWN + direction] = downs[direction]
        diagonal = spring + total
        held_ref[gx, DIAGONAL] = diagonal
        held_ref[gx, MASS] = mass
        best = jnp.maximum(best, (diagonal + total) / mass)
    best = jnp.max(jnp.max(best, axis=0), axis=(0, 1), keepdims=True)
    top_ref[...] = jnp.broadcast_to(best, (32, 128))


def filter_kernel(held_ref, top_ref, terms_ref, inverse_ref):
    top = top_ref[0:1, :]
    inverse_spread = 1.0 / (top * 7.0 / 16.0)
    ratio = (top * 9.0 / 16.0) * inverse_spread
    for gx in range(16):
        mass = held_ref[gx, MASS]
        inverse_ref[gx] = inverse_spread / mass
        terms_ref[0, gx] = held_ref[gx, 0]
        terms_ref[TOTAL + 2, gx] = mass
    for degree in range(1, TOTAL + 2):
        current_ref = terms_ref.at[degree - 1]
        turned = Turned(current_ref)
        for gx in range(16):
            here, sides = around(current_ref, turned, gx)
            image = held_ref[gx, DIAGONAL] * here
            for direction in range(3):
                image = image - held_ref[gx, UP + direction] * sides[direction][0]
                image = image - held_ref[gx, DOWN + direction] * sides[direction][1]
            image = image * inverse_ref[gx] - ratio * here
            if degree > 1:
                image = 2.0 * image - terms_ref[degree - 2, gx]
            terms_ref[degree, gx] = image


def combine_kernel(terms_ref, own_top_ref, top_ref, nodes_ref, out_ref):
    top = jnp.max(jnp.max(top_ref[...], axis=0, keepdims=True), axis=1, keepdims=True)
    own_top = own_top_ref[0:1, :]
    part = own_top / top
    place = part * nodes_ref[0:1, :] + (part - 1.0) * (9.0 / 7.0)
    square = place * place
    once = 8.0 * square * square - 8.0 * square + 1.0
    coefficients = jnp.sum(nodes_ref[8:40, :] * (once * once), axis=1, keepdims=True)
    middle = own_top * 9.0 / 16.0
    spread = own_top * 7.0 / 16.0
    for gx in range(16):
        total = coefficients[0:1, :] * terms_ref[0, gx]
        scaled = coefficients[16:17, :] * terms_ref[0, gx]
        for degree in range(1, TOTAL + 2):
            term = terms_ref[degree, gx]
            if degree <= TOTAL:
                total = total + coefficients[degree : degree + 1, :] * term
            scaled = scaled + coefficients[16 + degree : 17 + degree, :] * term
        image = terms_ref[TOTAL + 2, gx] * (middle * total + spread * scaled)
        out_ref[pl.ds(gx * 64, 32, stride=2), :] = total.reshape(32, 128)
        out_ref[pl.ds(gx * 64 + 1, 32, stride=2), :] = image.reshape(32, 128)


def parts_of(rows_ref, kind):
    return [
        jnp.concatenate(
            [rows_ref[pl.ds((gx * 4 + comp) * 16 + kind, 8, stride=2), :] for gx in range(16)],
            axis=0,
        )
        for comp in range(3)
    ]


def pair_rows(one, two):
    low = lax.broadcasted_iota(jnp.int32, (128, 128), 1) < 64
    upper = jnp.where(low, one, 0.0 if two is None else pltpu.roll(two, 64, 1))
    lower = jnp.where(low, pltpu.roll(one, 64, 1), 0.0 if two is None else two)
    return jnp.concatenate([upper, lower], axis=0)


def by_vector(parts):
    return jnp.concatenate(
        [pair_rows(parts[0], parts[1]), pair_rows(parts[2], None)], axis=1
    )


def product_kernel(rows_ref, mass_ref, out_ref, along_x_ref, along_y_ref, along_z_ref):
    parts = parts_of(rows_ref, 0)
    vectors = by_vector(parts)
    along_x_ref[...] = vectors[:, :128]
    along_y_ref[...] = pair_rows(parts[1], parts[2])
    along_z_ref[...] = pair_rows(parts[2], parts[0])
    image = by_vector(parts_of(rows_ref, 1))
    weighted = vectors * mass_ref[...]
    gram = dot(weighted, vectors, ((1,), (1,)))
    stiff = dot(vectors, image, ((1,), (1,)))
    row = lax.broadcasted_iota(jnp.int32, (256, 256), 0)
    column = lax.broadcasted_iota(jnp.int32, (256, 256), 1)
    both = jnp.where(row >= column, gram, stiff)
    diagonal = jnp.sum(vectors * image, axis=1, keepdims=True)
    lane = lax.broadcasted_iota(jnp.int32, (256, 128), 1)
    lateral = jnp.sum(jnp.where(lane < NODES, weighted[:, :128], 0.0), axis=1, keepdims=True)
    further = jnp.where(lane == 0, diagonal, jnp.where(lane == 1, lateral, 0.0)).T
    for chunk in range(32):
        half = slice(0, 128) if chunk < 16 else slice(128, 256)
        first = chunk % 16 * 16
        out_ref[chunk * CHUNK : chunk * CHUNK + 16, :] = both[first : first + 16, half]
        last = further[chunk // 2 : chunk // 2 + 1, chunk % 2 * 128 : chunk % 2 * 128 + 128]
        out_ref[chunk * CHUNK + 16 : chunk * CHUNK + 17, :] = last


def total_kernel(count, copies, rows_ref, out_ref):
    total = rows_ref[0:CHUNK, :]
    for place in range(1, count):
        total = total + rows_ref[place * CHUNK : place * CHUNK + CHUNK, :]
    for place in range(copies):
        out_ref[place * CHUNK : place * CHUNK + CHUNK, :] = total


def factor_block(gram, stiff):
    lane = lax.broadcasted_iota(jnp.int32, (BLOCK, 128), 1)
    row = lax.broadcasted_iota(jnp.int32, (BLOCK, 128), 0)
    low = lane < 64
    columns = [
        jnp.where(
            low,
            jnp.broadcast_to(gram[:, j : j + 1], (BLOCK, 128)),
            jnp.broadcast_to(stiff[:, j : j + 1], (BLOCK, 128)),
        )
        for j in range(BLOCK)
    ]
    inverse = jnp.where((lane & 63) == row, 1.0, 0.0)
    scale = jnp.ones((BLOCK, 128), jnp.float32)
    link = jnp.zeros((BLOCK, 128), jnp.float32)
    for k in range(0, BLOCK, 2):
        one, two = columns[k], columns[k + 1]
        top = one[k : k + 1, :]
        side = one[k + 1 : k + 2, :]
        corner = two[k + 1 : k + 2, :]
        rest = top * corner - side * side
        scale = jnp.where(row == k, top, jnp.where(row == k + 1, rest / top, scale))
        link = jnp.where(row == k + 1, side / top, link)
        if k + 2 == BLOCK:
            break
        part = (k + 2) // 8 * 8
        factor = 1.0 / rest
        below = row[part:] > k + 1
        first = jnp.where(below, (one[part:] * corner - two[part:] * side) * factor, 0.0)
        second = jnp.where(below, (two[part:] * top - one[part:] * side) * factor, 0.0)

        def reduced(value):
            tail = value[part:] - (first * value[k : k + 1, :] + second * value[k + 1 : k + 2, :])
            return tail if part == 0 else jnp.concatenate([value[:part], tail], axis=0)

        for j in range(k + 2, BLOCK):
            columns[j] = reduced(columns[j])
        inverse = reduced(inverse)
    inverse = inverse - link * pltpu.roll(inverse, 1, 0)
    return inverse * lax.rsqrt(scale), scale


def rounded(value):
    return value.astype(jnp.bfloat16).astype(jnp.float32)


def three_parts(value):
    high = rounded(value)
    rest = value - high
    middle = rounded(rest)
    return high, middle, rest - middle


def four_copies(value):
    return (value + pltpu.roll(value, 32, 1)) + (
        pltpu.roll(value, 64, 1) + pltpu.roll(value, 96, 1)
    )


def left_groups(first, second):
    group = lax.broadcasted_iota(jnp.int32, first.shape, 1) // BLOCK
    high, middle, _ = three_parts(first)
    parts = three_parts(second)
    one = jnp.where(group < 2, high, middle)
    two = jnp.where(group == 0, parts[0], jnp.where(group == 1, parts[2], 0.0))
    return jnp.concatenate([one, two], axis=1).astype(jnp.bfloat16)


def right_lanes(copies):
    group = lax.broadcasted_iota(jnp.int32, copies.shape, 1) // BLOCK
    high, middle, low = three_parts(copies)
    one = jnp.where(group % 2 == 0, high, middle)
    two = jnp.where(group == 0, low, high)
    return jnp.concatenate([one, two], axis=1).astype(jnp.bfloat16)


def right_rows(value):
    high, middle, low = [part.astype(jnp.bfloat16) for part in three_parts(value)]
    return jnp.concatenate([high, middle, high, middle, low, high, high, high], axis=0)


def product(left, right, contract):
    return lax.dot_general(
        left, right, (contract, ((), ())), preferred_element_type=jnp.float32
    )


def invert_factors(m_ref, diagonal):
    lane = lax.broadcasted_iota(jnp.int32, (BLOCK, 128), 1)
    least = jnp.ones((BLOCK, 128), jnp.float32)
    for first in range(0, 256, BLOCK):
        tile = first // 128 * 128
        inside = first - tile
        after = first + BLOCK
        small = [m_ref[m, first:after, tile : tile + 128][:, inside : inside + BLOCK] for m in (0, 1)]
        inverse, pivots = factor_block(small[0], small[1])
        least = jnp.minimum(least, pivots / diagonal[first:after, :])
        for m in (0, 1):
            own = four_copies(
                jnp.where((lane >= 64 * m) & (lane < 64 * m + BLOCK), inverse, 0.0)
            )
            row = lax.broadcasted_iota(jnp.int32, (BLOCK, 256), 0)
            column = lax.broadcasted_iota(jnp.int32, (BLOCK, 256), 1) - first
            rows = m_ref[m, first:after, :]
            unit = jnp.where(column == row, 1.0, 0.0)
            rows = jnp.where((column >= 0) & (column < BLOCK), unit, rows)
            result = product(left_groups(own, own), right_rows(rows), ((1,), (0,)))
            m_ref[m, first:after, :] = result
            if after < 256:
                count = 256 - after
                lanes = lax.broadcasted_iota(jnp.int32, (count, 128), 1)
                held = (lanes >= inside) & (lanes < inside + BLOCK)
                left = four_copies(jnp.where(held, m_ref[m, after:, tile : tile + 128], 0.0))
                right = jnp.concatenate([right_lanes(own)] * 8, axis=0)
                factor = product(left_groups(left, left), right, ((1,), (1,)))
                column = lax.broadcasted_iota(jnp.int32, (count, 256), 1)
                rows = m_ref[m, after:, :]
                rows = jnp.where((column >= first) & (column < after), 0.0, rows)
                m_ref[m, after:, :] = rows - product(
                    left_groups(factor[:, :128], factor[:, 128:]), right_rows(result), ((1,), (0,))
                )
    return jnp.min(least, axis=(0, 1), keepdims=True)


def final_kernel(
    sums_ref, rows_ref, above_x_ref, below_x_ref, above_y_ref, below_y_ref, above_z_ref,
    below_z_ref, mass_ref, modulus_ref, stress_ref, subspace_ref, projected_ref, force_ref,
    stress_new_ref, apart_ref, m_ref
):
    chunks = [sums_ref[chunk * CHUNK : chunk * CHUNK + 16, :] for chunk in range(32)]
    both = jnp.concatenate(
        [jnp.concatenate(chunks[:16], axis=0), jnp.concatenate(chunks[16:], axis=0)], axis=1
    )
    further = [
        jnp.broadcast_to(sums_ref[chunk * CHUNK + 16 : chunk * CHUNK + 17, :], (128, 128)).T
        for chunk in range(4)
    ]
    diagonal = jnp.concatenate(further[:2], axis=0)
    diagonal = jnp.concatenate([diagonal, diagonal], axis=1)
    lateral = jnp.concatenate(further[2:], axis=0)
    turned = both.T
    row = lax.broadcasted_iota(jnp.int32, (256, 256), 0)
    column = lax.broadcasted_iota(jnp.int32, (256, 256), 1)
    gram = jnp.where(row >= column, both, turned)
    stiff = jnp.where(row < column, both, jnp.where(row == column, diagonal, turned))
    m_ref[0] = gram
    m_ref[1] = stiff
    half = lax.broadcasted_iota(jnp.int32, (256, 128), 1) < 64
    gram_diagonal = jnp.sum(jnp.where(row == column, gram, 0.0), axis=1, keepdims=True)
    least = invert_factors(m_ref, jnp.where(half, gram_diagonal, diagonal[:, :128]))
    apart_ref[0, 0] = jnp.where(least[0, 0] > LEAST_PIVOT, 1, 0)
    lower = jnp.where(row >= column, m_ref[0], 0.0)
    stiff_lower = jnp.where(row >= column, m_ref[1], 0.0)
    vectors = by_vector(parts_of(rows_ref, 0))
    subspace = dot(vectors.T, lower, ((1,), (1,)))
    subspace = subspace * jnp.sqrt(jnp.float32(DEVICES * 3 * NODES))
    projected_ref[...] = dot(lower, dot(stiff, lower, ((1,), (1,))))
    weights = dot(stiff_lower.T, dot(stiff_lower, lateral))
    weights = jnp.concatenate([weights, weights], axis=1)
    displace = jnp.sum(vectors * weights, axis=0, keepdims=True)
    own = [displace[:, :128], pltpu.roll(displace[:, :128], 64, 1), displace[:, 128:]]
    outside = [
        jnp.sum(ref[...] * weights[:, :128], axis=0, keepdims=True)
        for ref in (above_x_ref, below_x_ref, above_y_ref, below_y_ref, above_z_ref, below_z_ref)
    ]
    lane = lax.broadcasted_iota(jnp.int32, (1, 128), 1)
    axial = []
    bending = []
    for direction, (step, mask) in enumerate(((32, 32), (1, 7), (8, 24))):
        wide = jnp.where(lane < 64, own[direction], pltpu.roll(own[(direction + 1) % 3], 64, 1))
        above = jnp.where(
            (lane & mask) == mask,
            pltpu.roll(outside[2 * direction], mask, 1),
            pltpu.roll(wide, 128 - step, 1),
        )
        below = jnp.where(
            (lane & mask) == 0,
            pltpu.roll(outside[2 * direction + 1], 128 - mask, 1),
            pltpu.roll(wide, step, 1),
        )
        axial.append(0.5 * (above - below))
        bending.append(pltpu.roll((above - 2.0 * wide) + below, 64, 1))
    lane = lax.broadcasted_iota(jnp.int32, (24, 256), 1)
    group = lax.broadcasted_iota(jnp.int32, (24, 256), 0)
    laid = jnp.where((lane >> 3) == group, displace * mass_ref[...], 0.0)
    column = lax.broadcasted_iota(jnp.int32, (256, 128), 0)
    place = lax.broadcasted_iota(jnp.int32, (256, 128), 1)
    force_ref[...] = dot(laid, jnp.where((column & 7) == place, 1.0, 0.0))[:, :8]
    columns = jnp.concatenate(
        axial + bending + [jnp.zeros((122, 128), jnp.float32)], axis=0
    ).T
    axial = [jnp.broadcast_to(columns[:, d : d + 1], (128, 16)) for d in range(3)]
    bending = [jnp.broadcast_to(columns[:, 3 + d : 4 + d], (128, 16)) for d in range(3)]
    fiber = lax.broadcasted_iota(jnp.int32, (8, 16), 1).astype(jnp.float32)
    heights = (fiber + 0.5) / 16.0 - 0.5
    for direction in range(3):
        for x in range(2):
            for z in range(4):
                rows = slice(direction * 16 + x * 8, direction * 16 + x * 8 + 8)
                inner = x * 32 + z * 8
                one = direction * NODES + inner
                subspace_ref[rows, z, :] = subspace[one : one + 8]
                strain = axial[direction][inner : inner + 8]
                strain = strain + heights * bending[direction][inner : inner + 8]
                stress_new_ref[rows, z, :] = stress_ref[rows, z, :] + modulus_ref[rows, z, :] * strain


def fiber_modulus(stiffness, yield_flags):
    own = jnp.stack([stiffness[d, d] for d in range(3)])[:, None]
    return own * jnp.where(yield_flags == 1, 0.05, 1.0)


def extended(block, first_dim):
    for place, axis in enumerate((GX, "gy", "gz")):
        dim = first_dim + place
        count = lax.axis_size(axis)
        forward = [(i, i + 1) for i in range(count - 1)]
        backward = [(target, source) for source, target in forward]
        last = block.shape[dim]
        low = lax.ppermute(lax.slice_in_dim(block, last - 1, last, axis=dim), axis, forward)
        high = lax.ppermute(lax.slice_in_dim(block, 0, 1, axis=dim), axis, backward)
        block = jnp.concatenate([low, block, high], axis=dim)
    return block


def neighbour(padded, leading, direction, sense):
    slicer = [slice(None)] * padded.ndim
    for position in range(3):
        slicer[leading + position] = slice(1, -1)
    slicer[leading + direction] = slice(2, None) if sense > 0 else slice(0, -2)
    return padded[tuple(slicer)]


def summed(square):
    rows = jnp.concatenate([square[:, :128], square[:, 128:]], axis=0)
    for axes, count, copies in ((("cy", "gy"), 32, 16), (("core", "gz"), 16, 32)):
        rows = jnp.sum(exchange(rows, axes, count).reshape(count, 16, 128), axis=0)
        rows = jnp.tile(rows, (copies, 1))
    rows = exchange(rows, ("cy", "gy"), 32)
    return jnp.concatenate([rows[:256], rows[256:]], axis=1)


def step_by_step(start_block, node_mass, ground_spring, stiffness, yield_flags, stress_old):
    share = jnp.mean(yield_flags.astype(jnp.float32), axis=1)
    tangent = stiffness * (1.0 - 0.9 * share)[:, None]
    padded = extended(tangent, 2)
    edges = [
        [0.5 * (tangent[d] + neighbour(padded, 2, d, sense)[d]) for d in range(3)]
        for sense in (1, -1)
    ]
    edge_total = sum(edges[0]) + sum(edges[1])
    diagonal = ground_spring + edge_total
    top = jnp.broadcast_to(jnp.max((diagonal + edge_total) / node_mass), (128, 128))
    for axes, count in ((("cy", "core"), 16), ("gy", 4), ("gz", 8)):
        top = jnp.broadcast_to(jnp.max(exchange(top, axes, count)), (128, 128))
    top = top[0, 0]
    middle = top * 9.0 / 16.0
    spread = top * 7.0 / 16.0

    def apply_k(field):
        around_field = extended(field, 1)
        result = diagonal[..., None] * field
        for d in range(3):
            for sense, weights in ((1, edges[0]), (-1, edges[1])):
                result = result - weights[d][..., None] * neighbour(around_field, 1, d, sense)
        return result

    def shifted(field):
        return (apply_k(field) / node_mass[..., None] - middle * field) / spread

    width = start_block.shape[-1]
    mass_rows = node_mass.reshape(-1)
    vectors = start_block
    for turn in range(ITERS):
        earlier, current = vectors, shifted(vectors)
        for repeat in range(DEGREE - 1):
            earlier, current = current, 2.0 * shifted(current) - earlier
        flat_rows = current.reshape(-1, width)
        gram = summed(dot(flat_rows.T, mass_rows[:, None] * flat_rows))
        factor = jnp.linalg.cholesky(gram)
        basis = lax.linalg.triangular_solve(factor, flat_rows.T, left_side=True, lower=True)
        vectors = basis.T.reshape(current.shape)
    image = apply_k(vectors).reshape(-1, width)
    projected = summed(dot(basis, image))
    lateral = dot(basis[:, :NODES], mass_rows[:NODES, None])
    lateral = summed(jnp.broadcast_to(lateral, (width, width)))[:, :1]
    factor = jnp.linalg.cholesky(projected)
    halfway = lax.linalg.triangular_solve(factor, lateral, left_side=True, lower=True)
    weights = lax.linalg.triangular_solve(
        factor, halfway, left_side=True, lower=True, transpose_a=True
    )
    displace = dot(weights.T, basis).reshape(node_mass.shape)
    padded = extended(displace, 1)
    axial = []
    bending = []
    for d in range(3):
        above = neighbour(padded, 1, d, 1)
        below = neighbour(padded, 1, d, -1)
        other = (d + 1) % 3
        axial.append(0.5 * (above[d] - below[d]))
        bending.append(above[other] - 2.0 * displace[other] + below[other])
    fibers = stress_old.shape[1]
    heights = ((jnp.arange(fibers).astype(jnp.float32) + 0.5) / fibers - 0.5)[:, None, None, None]
    strain = jnp.stack(axial)[:, None] + heights * jnp.stack(bending)[:, None]
    stress_new = stress_old + fiber_modulus(stiffness, yield_flags) * strain
    subspace = vectors * jnp.sqrt(jnp.float32(DEVICES * 3 * NODES))
    return subspace, projected, node_mass * displace, stress_new


def call(kernel, shape, scratch=(), smem=(), operands=(), smem_out=()):
    results = len(shape) if isinstance(shape, tuple) else 1
    out_specs = tuple(
        pl.BlockSpec(memory_space=pltpu.SMEM if place in smem_out else pltpu.VMEM)
        for place in range(results)
    )
    return pl.pallas_call(
        kernel,
        out_shape=shape,
        in_specs=[
            pl.BlockSpec(memory_space=pltpu.SMEM if place in smem else pltpu.VMEM)
            for place in range(len(operands))
        ],
        out_specs=out_specs if isinstance(shape, tuple) else out_specs[0],
        scratch_shapes=list(scratch),
        compiler_params=pltpu.CompilerParams(vmem_limit_bytes=40 * 1024 * 1024),
    )(*operands)


def rows_of(count):
    return jax.ShapeDtypeStruct((count, 128), jnp.float32)


def exchange(rows, axes, devices):
    per_device = rows.shape[0] // devices
    if per_device % 8 == 0:
        blocks = rows.reshape(devices, per_device, 128)
    else:
        blocks = rows.reshape(devices, per_device, 1, 128)
    return lax.all_to_all(blocks, axes, 0, 0, tiled=True).reshape(rows.shape)


def chebyshev_nodes():
    count = TOTAL + 1
    angles = np.pi * (np.arange(count) + 0.5) / count
    plain = np.zeros((count, count))
    timesx = np.zeros((count + 1, count))
    for degree in range(count):
        plain[degree] = (2.0 if degree else 1.0) / count * np.cos(degree * angles)
        timesx[degree + 1] += plain[degree] * (0.5 if degree else 1.0)
        if degree:
            timesx[degree - 1] += plain[degree] * 0.5
    table = np.zeros((40, 128), np.float32)
    table[0, :count] = np.cos(angles)
    table[8 : 8 + count, :count] = plain
    table[24 : 25 + count, :count] = timesx
    return jnp.asarray(table)


def on_device(start_block, node_mass, ground_spring, stiffness, yield_flags, stress_old):
    width = start_block.shape[-1]
    fibers = stress_old.shape[1]

    def node_rows(value):
        return jnp.swapaxes(value, -1, -2).reshape(-1, 8)

    def fibers_last(value):
        return jnp.moveaxis(value, 1, -1).reshape(48, 4, fibers)

    grid_shape = (16, 4, 8, 128)
    plain = pltpu.VMEM(grid_shape, jnp.float32)
    planes_shape = (16, KINDS, 4, 8, 128)
    sent = call(
        pack_kernel,
        rows_of(256 * OUT_ROWS),
        operands=(
            start_block.reshape(48, 4, width),
            node_rows(stiffness),
            node_rows(node_mass),
            node_rows(ground_spring),
            fibers_last(yield_flags).reshape(3 * NODES, fibers),
        ),
    )
    own = exchange(sent, CHIPS, 256)
    other = lax.ppermute(own, "core", [(0, 1), (1, 0)])
    core = lax.axis_index("core").astype(jnp.int32).reshape(1)
    planes, own_top = call(
        weights_kernel,
        (jax.ShapeDtypeStruct(planes_shape, jnp.float32), rows_of(32)),
        (plain,),
        smem=(0,),
        operands=(core, own, other),
    )
    tops = exchange(own_top, "gy", 4)
    terms = call(
        filter_kernel,
        jax.ShapeDtypeStruct((TOTAL + 3,) + grid_shape, jnp.float32),
        (plain,),
        operands=(planes, own_top),
    )
    filtered = call(
        combine_kernel,
        rows_of(1024),
        operands=(terms, own_top, tops, chebyshev_nodes()),
    )
    returned = exchange(filtered, AXES, DEVICES)
    mass_row = node_rows(node_mass).reshape(1, 3 * NODES)
    mass_row = jnp.pad(mass_row, ((0, 0), (0, NODES)))
    along = jax.ShapeDtypeStruct((width, 128), jnp.float32)
    products, *along = call(
        product_kernel,
        (rows_of(32 * CHUNK), along, along, along),
        operands=(returned, mass_row),
    )

    def from_neighbours(mine, axis, senses):
        count = lax.axis_size(axis)
        pairs = [(i, i + 1) for i in range(count - 1)]
        return [
            lax.ppermute(mine, axis, [(b, a) for a, b in pairs] if sense > 0 else pairs)
            for sense in senses
        ]

    near = from_neighbours(along[0], GX, (1, -1))
    part = exchange(products, ("cy", "gy"), 32)
    part, *near = lax.optimization_barrier((part, *near))
    part = call(functools.partial(total_kernel, 32, 16), rows_of(16 * CHUNK), operands=(part,))
    part, along[1] = lax.optimization_barrier((part, along[1]))
    near += from_neighbours(along[1], "gy", (1,))
    part = exchange(part, ("core", "gz"), 16)
    part, *near = lax.optimization_barrier((part, *near))
    part = call(functools.partial(total_kernel, 16, 32), rows_of(32 * CHUNK), operands=(part,))
    part, *along[1:] = lax.optimization_barrier((part, *along[1:]))
    far = from_neighbours(along[1], "gy", (-1,)) + from_neighbours(along[2], "gz", (1, -1))
    part = exchange(part, ("cy", "gy"), 32)
    part, *far = lax.optimization_barrier((part, *far))
    subspace, projected, force, stress_new, apart = call(
        final_kernel,
        (
            jax.ShapeDtypeStruct((48, 4, width), jnp.float32),
            jax.ShapeDtypeStruct((width, width), jnp.float32),
            jax.ShapeDtypeStruct((24, 8), jnp.float32),
            jax.ShapeDtypeStruct((48, 4, fibers), jnp.float32),
            jax.ShapeDtypeStruct((1, 1), jnp.int32),
        ),
        (pltpu.VMEM((2, 256, 256), jnp.float32),),
        operands=(
            part,
            returned,
            *near,
            *far,
            mass_row,
            fibers_last(fiber_modulus(stiffness, yield_flags)),
            fibers_last(stress_old),
        ),
        smem_out=(4,),
    )
    place = node_mass.shape[1:]
    force = jnp.swapaxes(force.reshape(3, place[0], place[2], place[1]), -1, -2)
    stress_new = jnp.moveaxis(stress_new.reshape((3,) + place + (fibers,)), -1, 1)
    return lax.switch(
        apart[0, 0],
        (lambda *operands: step_by_step(*operands[4:]), lambda *operands: operands[:4]),
        subspace.reshape(start_block.shape),
        projected,
        force,
        stress_new,
        start_block,
        node_mass,
        ground_spring,
        stiffness,
        yield_flags,
        stress_old,
    )


def solution(mesh):
    chips = Mesh(mesh.devices.reshape(8, 2, 4, 8), AXES)
    return jax.shard_map(
        on_device,
        mesh=chips,
        in_specs=(
            P(None, GX, "gy", "gz", None),
            P(None, GX, "gy", "gz"),
            P(None, GX, "gy", "gz"),
            P(None, None, GX, "gy", "gz"),
            P(None, None, GX, "gy", "gz"),
            P(None, None, GX, "gy", "gz"),
        ),
        out_specs=(
            P(None, GX, "gy", "gz", None),
            P(),
            P(None, GX, "gy", "gz"),
            P(None, None, GX, "gy", "gz"),
        ),
        check_vma=False,
    )
```
